512 devices in a mesh: seq: 128 (over x, z, core), head: 4 (over y).
Axes of the slice: x: 4, y: 4, z: 16, core: 2. Of those that a mesh axis runs over, the one named last changes fastest.
Arguments:
- query_states: bfloat16 [65536, 2048], P('seq', 'head'), may hold values from -17 to 17
- key_states: bfloat16 [65536, 2048], P('seq', 'head'), may hold values from -10 to 10
- value_states: bfloat16 [65536, 2048], P('seq', 'head'), may hold values from -10 to 10
- output_weight: bfloat16 [2048, 2048], P('head', 'seq'), may hold values from -0.125 to 0.125
Outputs:
- mixed: bfloat16 [65536, 2048], P('seq', 'head')
The draws below stay inside these ranges and needn't reach their ends.
All inputs are finite; a program needn't handle non-finite values.
Results may differ from the reference program's by a relative error of at most 0.015.
Values may be sent and summed in bfloat16 or wider, within the bound.
No kernel may reach another device: no remote copies, remote signals or barrier semaphores. Data moves between devices by JAX's collectives and lax.ppermute only.
A program may use at most 64 MiB of HBM per device.

```python
import math
import jax
import jax.numpy as jnp
from jax import lax

HEADS = 16
HEAD_DIM = 128
D = 2048
BLOCK = 128
LEVELS = 3
SEQ = 65536
N_HEAD = 4


def spread_tables(tables):
    feature_width = HEADS * HEAD_DIM
    summed = jnp.zeros((SEQ, feature_width), jnp.float32)
    for table in tables:
        table_rows = table.shape[0]
        copies = SEQ // table_rows
        widened = jnp.broadcast_to(table[:, None, :], (table_rows, copies, feature_width)).reshape(SEQ, feature_width)
        summed = summed + widened
    return summed


def region_lengths():
    return [math.gcd(BLOCK, SEQ), math.gcd(8 * BLOCK, SEQ), math.gcd(32 * BLOCK, SEQ)]


def draw_query_states(key, part):
    stream_key = jax.random.fold_in(key, 11)
    streams = jax.random.split(stream_key, 4)
    feature_width = HEADS * HEAD_DIM
    noise_part = 0.6 * jax.random.truncated_normal(streams[0], -4.0, 4.0, (SEQ, feature_width), jnp.float32)
    tables = [0.8 * jax.random.truncated_normal(streams[1 + member], -3.0, 3.0, (SEQ // length, feature_width), jnp.float32) for member, length in enumerate(region_lengths())]
    field = noise_part + spread_tables(tables)
    return field.astype(jnp.bfloat16)


def draw_key_states(key, part):
    stream_key = jax.random.fold_in(key, 12)
    streams = jax.random.split(stream_key, 4)
    feature_width = HEADS * HEAD_DIM
    noise_part = 0.6 * jax.random.truncated_normal(streams[0], -4.0, 4.0, (SEQ, feature_width), jnp.float32)
    tables = [0.8 * jax.random.truncated_normal(streams[1 + member], -3.0, 3.0, (SEQ // length, feature_width), jnp.float32) for member, length in enumerate(region_lengths())]
    field = noise_part + spread_tables(tables)
    return field.astype(jnp.bfloat16)


def draw_value_states(key, part):
    stream_key = jax.random.fold_in(key, 13)
    streams = jax.random.split(stream_key, 4)
    feature_width = HEADS * HEAD_DIM
    noise_part = 0.6 * jax.random.truncated_normal(streams[0], -4.0, 4.0, (SEQ, feature_width), jnp.float32)
    tables = [0.8 * jax.random.truncated_normal(streams[1 + member], -3.0, 3.0, (SEQ // length, feature_width), jnp.float32) for member, length in enumerate(region_lengths())]
    field = noise_part + spread_tables(tables)
    return field.astype(jnp.bfloat16)


def levels(rng, shape, pieces, smallest, largest):
    def one(axis_at, shards_of):
        heights = jax.random.uniform(jax.random.fold_in(jax.random.fold_in(rng, 6), axis_at), (shards_of,), jnp.float32, smallest / len(pieces), largest / len(pieces))
        return jnp.repeat(jnp.exp(heights), shape[axis_at] // shards_of).reshape((-1,) + (1,) * (len(shape) - axis_at - 1))

    factor_of = one(*pieces[0])
    for cut in pieces[1:]:
        factor_of = factor_of * one(*cut)
    return factor_of


def scatter_about(own_key, extent, spread, reach, shards=(), held_as=jnp.bfloat16):
    loudness = levels(own_key, extent, shards, -0.22, 0.18) if shards else 1.0
    entries = jax.random.normal(own_key, extent, jnp.float32) * spread * loudness
    return jnp.minimum(jnp.maximum(entries, -reach), reach).astype(held_as)


def setup_inputs(seed: int = 0) -> dict:
    seeds = jax.random.split(jax.random.key(seed), 5)
    query_states = draw_query_states(jax.random.fold_in(seeds[4], 71), 0)
    key_states = draw_key_states(jax.random.fold_in(seeds[4], 71), 0)
    value_states = draw_value_states(jax.random.fold_in(seeds[4], 71), 0)
    output_weight = scatter_about(seeds[3], (HEADS * HEAD_DIM, D), (HEADS * HEAD_DIM) ** -0.5, 0.125, ((0, 4), (1, 128)))
    return dict(query_states=query_states, key_states=key_states, value_states=value_states, output_weight=output_weight)


def coarsen(field):
    shape = field.shape
    pairs = field.astype(jnp.float32).reshape(shape[:-2] + (shape[-2] // 2, 2, shape[-1]))
    return ((pairs[..., 0, :] + pairs[..., 1, :]) * 0.5).astype(jnp.bfloat16)


def double_rows(field):
    shape = field.shape
    widened = jnp.broadcast_to(field[:, None], (shape[0], 2) + shape[1:])
    return widened.reshape((shape[0] * 2,) + shape[1:])


def edge_mask(left_ok, right_ok):
    block_count = left_ok.shape[0]
    middle = jnp.ones((block_count, BLOCK), dtype=bool)
    return jnp.concatenate([jnp.broadcast_to(left_ok[:, None], (block_count, BLOCK)), middle, jnp.broadcast_to(right_ok[:, None], (block_count, BLOCK))], axis=1)


def block_stats(queries, keys_level, values_level):
    row_total = queries.shape[0]
    block_count = row_total // BLOCK
    zero_block = jnp.zeros((BLOCK, HEAD_DIM), keys_level.dtype)
    padded_keys = jnp.concatenate([zero_block, keys_level, zero_block], axis=0).reshape(block_count + 2, BLOCK, HEAD_DIM)
    padded_values = jnp.concatenate([zero_block, values_level, zero_block], axis=0).reshape(block_count + 2, BLOCK, HEAD_DIM)
    key_blocks = jnp.concatenate([padded_keys[:-2], padded_keys[1:-1], padded_keys[2:]], axis=1)
    value_blocks = jnp.concatenate([padded_values[:-2], padded_values[1:-1], padded_values[2:]], axis=1)
    query_blocks = queries.reshape(block_count, BLOCK, HEAD_DIM)
    scores = jnp.einsum("nqd,nkd->nqk", query_blocks.astype(jnp.float32), key_blocks.astype(jnp.float32), precision=lax.Precision.HIGHEST) * (HEAD_DIM ** -0.5)
    block_ids = jnp.arange(block_count, dtype=jnp.int32)
    usable = edge_mask(block_ids > 0, block_ids < block_count - 1)
    scores = jnp.where(usable[:, None, :], scores, -jnp.inf)
    row_max = jnp.max(scores, axis=-1)
    weights = jnp.exp(scores - row_max[..., None])
    row_sum = jnp.sum(weights, axis=-1)
    numerator = jnp.einsum("nqk,nkd->nqd", weights.astype(jnp.bfloat16).astype(jnp.float32), value_blocks.astype(jnp.float32), precision=lax.Precision.HIGHEST)
    return row_max.reshape(row_total), row_sum.reshape(row_total), numerator.reshape(row_total, HEAD_DIM)


def head_attention(queries, keys_level, values_level):
    statistics = []
    for level_num in range(LEVELS + 1):
        if level_num > 0:
            queries = coarsen(queries)
            keys_level = coarsen(keys_level)
            values_level = coarsen(values_level)
        statistics.append(block_stats(queries, keys_level, values_level))
    row_max, row_sum, numerator = statistics[LEVELS]
    for level_num in range(LEVELS - 1, -1, -1):
        row_max = double_rows(row_max)
        row_sum = double_rows(row_sum)
        numerator = double_rows(numerator)
        finer_max, finer_sum, finer_numerator = statistics[level_num]
        merged_max = jnp.maximum(row_max, finer_max)
        coarse_factor = jnp.exp(row_max - merged_max)
        finer_factor = jnp.exp(finer_max - merged_max)
        row_sum = row_sum * coarse_factor + finer_sum * finer_factor
        numerator = numerator * coarse_factor[:, None] + finer_numerator * finer_factor[:, None]
        row_max = merged_max
    return (numerator / row_sum[:, None]).astype(jnp.bfloat16)


def reference(query_states, key_states, value_states, output_weight):
    def one_head(head_number):
        first_column = head_number * HEAD_DIM
        return head_attention(
            lax.dynamic_slice_in_dim(query_states, first_column, HEAD_DIM, axis=1),
            lax.dynamic_slice_in_dim(key_states, first_column, HEAD_DIM, axis=1),
            lax.dynamic_slice_in_dim(value_states, first_column, HEAD_DIM, axis=1))

    attended = lax.map(one_head, jnp.arange(HEADS, dtype=jnp.int32))
    weight_heads = output_weight.reshape(HEADS, HEAD_DIM, D)
    group_heads = HEADS // N_HEAD
    rows_block = BLOCK * 2 ** LEVELS

    def project_rows(first_row):
        row_slab = lax.dynamic_slice_in_dim(attended, first_row, rows_block, axis=1).astype(jnp.float32)
        summed = jnp.zeros((rows_block, D), jnp.float32)
        for group_num in range(N_HEAD):
            lower = group_num * group_heads
            upper = lower + group_heads
            partial_group = jnp.einsum("hsd,hde->se", row_slab[lower:upper], weight_heads[lower:upper].astype(jnp.float32), precision=lax.Precision.HIGHEST).astype(jnp.bfloat16)
            partial_group = lax.optimization_barrier(partial_group)
            summed = summed + partial_group.astype(jnp.float32)
        return summed.astype(jnp.bfloat16)

    starts = jnp.arange(SEQ // rows_block, dtype=jnp.int32) * rows_block
    mixed = lax.map(project_rows, starts)
    return mixed.reshape(SEQ, D)
```

```python
import functools

import jax
import jax.numpy as jnp
from jax import lax
from jax.experimental import pallas as pl
from jax.experimental.pallas import tpu as pltpu
from jax.sharding import Mesh, PartitionSpec as P

HEAD_DIM = 128
BLOCK = 128
GROUP = 16
ROWS = 512
WIDTH = 512
HEADS_HERE = WIDTH // HEAD_DIM
SCALE2 = HEAD_DIM ** (-0.5) * 1.4426950408889634
MASKED = -1e30
F32 = jnp.float32
BF16 = jnp.bfloat16
VMEM_LIMIT = 48 * 1024 * 1024

NT = (((1,), (1,)), ((), ()))
NN = (((1,), (0,)), ((), ()))


def dot(a, b, dims=NN):
    return lax.dot_general(a, b, dims, preferred_element_type=F32)


def iota2(shape, dim):
    return lax.broadcasted_iota(jnp.int32, shape, dim)


def pair_average():
    row, col = iota2((64, 128), 0), iota2((64, 128), 1)
    return jnp.where((col >> 1) == 4 * (row & 15) + (row >> 4), 0.5, 0.0).astype(BF16)


def row_order():
    row, col = iota2((128, 128), 0), iota2((128, 128), 1)
    return jnp.where(col == 8 * (row & 15) + (row >> 4), 1.0, 0.0).astype(BF16)


def row_order_back():
    row, col = iota2((128, 128), 0), iota2((128, 128), 1)
    return jnp.where(row == 8 * (col & 15) + (col >> 4), 1.0, 0.0).astype(BF16)


def halve(x):
    wide = x.astype(F32)
    parts = [
        (wide[32 * i : 32 * i + 16] + wide[32 * i + 16 : 32 * i + 32]) * 0.5
        for i in range(x.shape[0] // 32)
    ]
    out = parts[0] if len(parts) == 1 else jnp.concatenate(parts, axis=0)
    return out.astype(BF16)


def double(x):
    parts = []
    for i in range(x.shape[0] // GROUP):
        piece = x[GROUP * i : GROUP * (i + 1)]
        parts += [piece, piece]
    return jnp.concatenate(parts, axis=0)


def prepare_kernel(k_ref, v_ref, ka_ref, va_ref, near_ref, chip_ref, own1_ref, own2_ref, side_ref):
    core = lax.axis_index("core")
    average = pair_average()
    for which, own, other in ((0, k_ref, ka_ref), (1, v_ref, va_ref)):
        own1 = [dot(average, own[128 * n : 128 * n + 128, :]).astype(BF16) for n in range(4)]
        own2 = [halve(x) for x in own1]
        own3 = [halve(x) for x in own2]
        for n in range(4):
            own1_ref[which, 64 * n : 64 * n + 64, :] = own1[n]
            own2_ref[which, 32 * n : 32 * n + 32, :] = own2[n]
            chip_ref[which, 16 * n : 16 * n + 16, :] = own3[n]
        other1 = [dot(average, other[128 * n : 128 * n + 128, :]).astype(BF16) for n in range(4)]
        other2 = [halve(x) for x in other1]
        other3 = [halve(x) for x in other2]
        for n in range(4):
            side_ref[which, 256 + 32 * n : 288 + 32 * n, :] = other2[n]
            chip_ref[which, 64 + 16 * n : 80 + 16 * n, :] = other3[n]
            near_ref[which, 256 + 16 * n : 272 + 16 * n, :] = other3[n]

        def edges(to_left):
            first, second, third, fourth = (0, 1, 2, 3) if to_left else (3, 2, 1, 0)
            near_ref[which, 0:128, :] = own[128 * first : 128 * first + 128, :]
            near_ref[which, 128:192, :] = own1[second]
            near_ref[which, 192:224, :] = own2[third]
            near_ref[which, 224:256, :] = own2[fourth]
            side_ref[which, 0:128, :] = other[128 * first : 128 * first + 128, :]
            side_ref[which, 128:192, :] = other1[first]
            side_ref[which, 192:256, :] = other1[second]

        pl.when(core == 0)(functools.partial(edges, True))
        pl.when(core != 0)(functools.partial(edges, False))


def weigh(query, keys, values, bias_left, bias_right):
    scores = dot(query, jnp.concatenate(keys, axis=0), NT)
    if bias_left is not None:
        scores = jnp.concatenate([scores[:, :128] + bias_left, scores[:, 128:]], axis=1)
    if bias_right is not None:
        scores = jnp.concatenate([scores[:, :256], scores[:, 256:] + bias_right], axis=1)
    top = jnp.max(scores, axis=1, keepdims=True)
    probs = jnp.exp2((scores - top) * SCALE2).astype(BF16)
    wide = jnp.concatenate(values, axis=0)
    wide = jnp.concatenate([wide, jnp.ones_like(wide)], axis=1)
    return top, dot(probs, wide)


def merge(fine, coarse):
    fine_top, fine_sums = fine
    top, sums = double(coarse[0]), double(coarse[1])
    fall = jnp.exp2(-jnp.abs(fine_top - top) * SCALE2)
    higher = fine_top >= top
    fine_factor = jnp.where(higher, 1.0, fall)
    factor = jnp.where(higher, fall, 1.0)
    return jnp.maximum(fine_top, top), fine_sums * fine_factor + sums * factor


def attention_kernel(
    q_ref, k_ref, v_ref, own1_ref, own2_ref, chip_ref, side_ref, near_ref, far_ref,
    out_ref, halo_ref, chips_ref,
):
    core = lax.axis_index("core")
    chip = lax.axis_index("x") * lax.axis_size("z") + lax.axis_index("z")
    last = lax.axis_size("x") * lax.axis_size("z") - 1
    left_chip = jnp.where(chip > 0, 0.0, MASKED).astype(F32)
    right_chip = jnp.where(chip < last, 0.0, MASKED).astype(F32)
    left_bias = jnp.where(core == 0, left_chip, 0.0)
    right_bias = jnp.where(core == 0, 0.0, right_chip)
    average = pair_average()
    order = row_order()
    back = row_order_back()
    side_slot, near_slot = 1 - core, core
    for which in range(2):
        halo_ref[which, side_slot] = side_ref[which]
        edge = near_ref[which, 0:128, :]
        edge1 = dot(average, edge).astype(BF16)
        next1 = near_ref[which, 128:192, :]
        rest2 = near_ref[which, 192:256, :]
        edge2, next2 = halve(edge1), halve(next1)
        halo_ref[which, near_slot, 0:128, :] = edge
        halo_ref[which, near_slot, 128:192, :] = edge1
        halo_ref[which, near_slot, 192:256, :] = next1
        halo_ref[which, near_slot, 256:288, :] = edge2
        halo_ref[which, near_slot, 288:320, :] = next2
        halo_ref[which, near_slot, 320:384, :] = rest2
        chips_ref[which, near_slot, 0:16, :] = halve(edge2)
        chips_ref[which, near_slot, 16:32, :] = halve(next2)
        chips_ref[which, near_slot, 32:64, :] = halve(rest2)
        chips_ref[which, near_slot, 64:128, :] = near_ref[which, 256:320, :]
        chips_ref[which, side_slot] = far_ref[which]

    def one_head(head, carry):
        lanes = pl.ds(pl.multiple_of(head * HEAD_DIM, HEAD_DIM), HEAD_DIM)
        q0 = [dot(order, q_ref[128 * n : 128 * n + 128, lanes]).astype(BF16) for n in range(4)]
        q1 = [halve(x) for x in q0]
        q2 = [halve(x) for x in q1]
        q3 = [halve(x) for x in q2]

        def piece(own, which, level, index, count):
            if index < 0:
                return halo_ref[which, 0, 128 * level : 128 * level + 128, lanes]
            if index >= count:
                return halo_ref[which, 1, 128 * level : 128 * level + 128, lanes]
            return own(which, index)

        def own_0(which, index):
            return (k_ref, v_ref)[which][128 * index : 128 * index + 128, lanes]

        def own_1(which, index):
            return own1_ref[which, 128 * index : 128 * index + 128, lanes]

        def own_2(which, index):
            return own2_ref[which, :, lanes]

        def tile(query, own, level, index, count):
            near = [index - 1, index, index + 1]
            return weigh(
                query,
                [piece(own, 0, level, i, count) for i in near],
                [piece(own, 1, level, i, count) for i in near],
                left_bias if index == 0 else None,
                right_bias if index == count - 1 else None,
            )

        at_3 = weigh(
            jnp.concatenate(q3, axis=0),
            [chips_ref[0, 0, :, lanes], chip_ref[0, :, lanes], chips_ref[0, 1, :, lanes]],
            [chips_ref[1, 0, :, lanes], chip_ref[1, :, lanes], chips_ref[1, 1, :, lanes]],
            left_chip,
            right_chip,
        )
        at_2 = merge(tile(jnp.concatenate(q2, axis=0), own_2, 2, 0, 1), at_3)
        for j in range(2):
            half_2 = tuple(x[64 * j : 64 * j + 64] for x in at_2)
            query_1 = jnp.concatenate(q1[2 * j : 2 * j + 2], axis=0)
            at_1 = merge(tile(query_1, own_1, 1, j, 2), half_2)
            for n in (2 * j, 2 * j + 1):
                start = 64 * (n - 2 * j)
                half_1 = tuple(x[start : start + 64] for x in at_1)
                _, sums = merge(tile(q0[n], own_0, 0, n, 4), half_1)
                attended = (sums[:, :128] / sums[:, 128:]).astype(BF16)
                out_ref[128 * n : 128 * n + 128, lanes] = dot(back, attended).astype(BF16)
        return carry

    lax.fori_loop(0, HEADS_HERE, one_head, 0)


def project_kernel(own_ref, left_ref, right_ref, upper_ref, lower_ref, w_ref, out_ref):
    group = lax.axis_index("head")
    count = lax.axis_size("head")

    def weight(which):
        return jnp.concatenate(
            [w_ref[c, which, 16 * z : 16 * z + 16, :] for z in range(16) for c in range(2)], axis=0
        )

    w_own = weight(group)
    w_left = weight(lax.rem(group + count - 1, count))
    w_right = weight(lax.rem(group + 1, count))
    w_across = weight(lax.rem(group + 2, count))
    for rows, across in ((slice(0, 256), upper_ref), (slice(256, 512), lower_ref)):
        total = dot(own_ref[rows, :], w_own, NT)
        total += dot(left_ref[rows, :], w_left, NT)
        total += dot(right_ref[rows, :], w_right, NT)
        total += dot(across[...], w_across, NT)
        out_ref[rows, :] = total.astype(BF16)


def call(kernel, outs, args, flops, scratch=()):
    size = sum(a.size for a in args) * 2 + sum(2 * functools.reduce(lambda a, b: a * b, s, 1) for s in outs)
    shapes = [jax.ShapeDtypeStruct(s, BF16) for s in outs]
    return pl.pallas_call(
        kernel,
        out_shape=shapes if len(shapes) > 1 else shapes[0],
        scratch_shapes=list(scratch),
        cost_estimate=pl.CostEstimate(flops=flops, bytes_accessed=size, transcendentals=0),
        compiler_params=pltpu.CompilerParams(vmem_limit_bytes=VMEM_LIMIT),
    )(*args)


def on_device(q, k, v, w):
    x_size, z_size = lax.axis_size("x"), lax.axis_size("z")
    count = lax.axis_size("head")
    chips = x_size * z_size
    devices = 2 * chips
    seq = ("x", "z", "core")

    swap = [(i, i ^ 1) for i in range(devices)]
    k_other = lax.ppermute(k, seq, swap)
    v_other = lax.ppermute(v, seq, swap)

    turn = [(a * count + b, b * count + a) for a in range(x_size) for b in range(count)]
    w_turned = lax.ppermute(w.T, ("x", "head"), turn)
    w_all = lax.all_gather(w_turned, "z", axis=0, tiled=True)
    w_all = lax.all_gather(w_all, "x", axis=0)
    w_all = lax.all_gather(w_all, "core", axis=0)

    near, chip3, own1, own2, side = call(
        prepare_kernel,
        [(2, 320, WIDTH), (2, 128, WIDTH), (2, 256, WIDTH), (2, 128, WIDTH), (2, 384, WIDTH)],
        (k, v, k_other, v_other),
        16 * 2 * 64 * 128 * 512,
    )
    to_near = [(i, (i + 1 if i % 2 else i - 1) % devices) for i in range(devices)]
    to_far = [(i, (i - 3 if i % 2 else i + 3) % devices) for i in range(devices)]
    near_in = lax.ppermute(near, seq, to_near)
    far_in = lax.ppermute(chip3, seq, to_far)

    attended = call(
        attention_kernel,
        [(ROWS, WIDTH)],
        (q, k, v, own1, own2, chip3, side, near_in, far_in),
        4 * 960 * 384 * 128 * 4,
        [pltpu.VMEM((2, 2, 384, WIDTH), BF16), pltpu.VMEM((2, 2, 128, WIDTH), BF16)],
    )

    up = [(i, (i + 1) % count) for i in range(count)]
    down = [(i, (i - 1) % count) for i in range(count)]
    from_left = lax.ppermute(attended, "head", up)
    from_right = lax.ppermute(attended, "head", down)
    half = ROWS // 2
    across_upper = lax.ppermute(from_left[:half], "head", up)
    across_lower = lax.ppermute(from_right[half:], "head", down)
    return call(
        project_kernel,
        [(ROWS, WIDTH)],
        (attended, from_left, from_right, across_upper, across_lower, w_all),
        2 * 512 * 512 * 2048,
    )


def solution(mesh):
    count = mesh.shape["head"]
    grid = Mesh(mesh.devices.reshape(4, mesh.shape["seq"] // 8, 2, count), ("x", "z", "core", "head"))
    rows = ("x", "z", "core")
    return jax.shard_map(
        on_device,
        mesh=grid,
        in_specs=(P(rows, "head"), P(rows, "head"), P(rows, "head"), P("head", rows)),
        out_specs=P(rows, "head"),
        check_vma=False,
    )
```

```python
import functools

import jax
import jax.numpy as jnp
from jax import lax
from jax.experimental import pallas as pl
from jax.experimental.pallas import tpu as pltpu
from jax.sharding import Mesh, PartitionSpec as P

HEAD_DIM = 128
BLOCK = 128
GROUP = 16
ROWS = 512
WIDTH = 512
HEADS_HERE = WIDTH // HEAD_DIM
SCALE2 = HEAD_DIM ** (-0.5) * 1.4426950408889634
MASKED = -1e30
F32 = jnp.float32
BF16 = jnp.bfloat16
VMEM_LIMIT = 48 * 1024 * 1024

NT = (((1,), (1,)), ((), ()))
NN = (((1,), (0,)), ((), ()))


def dot(a, b, dims=NN):
    return lax.dot_general(a, b, dims, preferred_element_type=F32)


def iota2(shape, dim):
    return lax.broadcasted_iota(jnp.int32, shape, dim)


def pair_average():
    row, col = iota2((64, 128), 0), iota2((64, 128), 1)
    return jnp.where((col >> 1) == 4 * (row & 15) + (row >> 4), 0.5, 0.0).astype(BF16)


def row_order():
    row, col = iota2((128, 128), 0), iota2((128, 128), 1)
    return jnp.where(col == 8 * (row & 15) + (row >> 4), 1.0, 0.0).astype(BF16)


def row_order_back():
    row, col = iota2((128, 128), 0), iota2((128, 128), 1)
    return jnp.where(row == 8 * (col & 15) + (col >> 4), 1.0, 0.0).astype(BF16)


def halve(x):
    wide = x.astype(F32)
    parts = [
        (wide[32 * i : 32 * i + 16] + wide[32 * i + 16 : 32 * i + 32]) * 0.5
        for i in range(x.shape[0] // 32)
    ]
    out = parts[0] if len(parts) == 1 else jnp.concatenate(parts, axis=0)
    return out.astype(BF16)


def double(x):
    parts = []
    for i in range(x.shape[0] // GROUP):
        piece = x[GROUP * i : GROUP * (i + 1)]
        parts += [piece, piece]
    return jnp.concatenate(parts, axis=0)


def coarsen_kernel(k_hbm, v_hbm, kv_ref, near_ref, side_ref, own1_ref, own2_ref, own3_ref, sems):
    core = lax.axis_index("core")
    copies = [
        pltpu.make_async_copy(source, kv_ref.at[which], sems.at[which])
        for which, source in enumerate((k_hbm, v_hbm))
    ]
    for copy in copies:
        copy.start()
    average = pair_average()
    for which, copy in enumerate(copies):
        copy.wait()
        own1 = [dot(average, kv_ref[which, 128 * n : 128 * n + 128, :]).astype(BF16) for n in range(4)]
        own2 = [halve(x) for x in own1]
        own3 = [halve(x) for x in own2]
        for n in range(4):
            own1_ref[which, 64 * n : 64 * n + 64, :] = own1[n]
            own2_ref[which, 32 * n : 32 * n + 32, :] = own2[n]
            own3_ref[which, 16 * n : 16 * n + 16, :] = own3[n]

        def edges(pack_ref, to_left):
            first, second, third, fourth = (0, 1, 2, 3) if to_left else (3, 2, 1, 0)
            pack_ref[which, 0:128, :] = kv_ref[which, 128 * first : 128 * first + 128, :]
            pack_ref[which, 128:192, :] = own1[second]
            pack_ref[which, 192:224, :] = own2[third]
            pack_ref[which, 224:256, :] = own2[fourth]

        def both_edges(near_is_left):
            edges(near_ref, near_is_left)
            edges(side_ref, not near_is_left)

        pl.when(core == 0)(functools.partial(both_edges, True))
        pl.when(core != 0)(functools.partial(both_edges, False))


def unpack(pack_ref, which, average, halo_ref, slot, chips_ref, chips_slot, start):
    edge = pack_ref[which, 0:128, :]
    edge1 = dot(average, edge).astype(BF16)
    next1 = pack_ref[which, 128:192, :]
    rest2 = pack_ref[which, 192:256, :]
    edge2, next2 = halve(edge1), halve(next1)
    pieces = ((0, edge), (128, edge1), (192, next1), (256, edge2), (288, next2), (320, rest2))
    for row, x in pieces:
        halo_ref[which, slot, row : row + x.shape[0], :] = x
    for row, x in ((0, halve(edge2)), (16, halve(next2)), (32, halve(rest2))):
        chips_ref[which, chips_slot, start + row : start + row + x.shape[0], :] = x


def prepare_kernel(pack_ref, near_own_ref, own3_ref, near_ref, chip_ref, side_ref):
    average = pair_average()
    for which in range(2):
        unpack(pack_ref, which, average, side_ref, 0, chip_ref, 0, 64)
        chip_ref[which, 0, 0:64, :] = own3_ref[which]
        near_ref[which, 0:256, :] = near_own_ref[which]
        near_ref[which, 256:320, :] = chip_ref[which, 0, 64:128, :]


def weigh(query, keys, values, bias_left, bias_right):
    scores = dot(query, jnp.concatenate(keys, axis=0), NT)
    if bias_left is not None:
        scores = jnp.concatenate([scores[:, :128] + bias_left, scores[:, 128:]], axis=1)
    if bias_right is not None:
        scores = jnp.concatenate([scores[:, :256], scores[:, 256:] + bias_right], axis=1)
    top = jnp.max(scores, axis=1, keepdims=True)
    probs = jnp.exp2((scores - top) * SCALE2).astype(BF16)
    wide = jnp.concatenate(values, axis=0)
    wide = jnp.concatenate([wide, jnp.ones_like(wide)], axis=1)
    return top, dot(probs, wide)


def merge(fine, coarse):
    fine_top, fine_sums = fine
    top, sums = double(coarse[0]), double(coarse[1])
    fall = jnp.exp2(-jnp.abs(fine_top - top) * SCALE2)
    higher = fine_top >= top
    fine_factor = jnp.where(higher, 1.0, fall)
    factor = jnp.where(higher, fall, 1.0)
    return jnp.maximum(fine_top, top), fine_sums * fine_factor + sums * factor


def attention_kernel(
    q_ref, kv_ref, own1_ref, own2_ref, chip_ref, side_ref, near_ref, far_ref,
    out_ref, halo_ref, chips_ref,
):
    core = lax.axis_index("core")
    chip = lax.axis_index("x") * lax.axis_size("z") + lax.axis_index("z")
    last = lax.axis_size("x") * lax.axis_size("z") - 1
    left_chip = jnp.where(chip > 0, 0.0, MASKED).astype(F32)
    right_chip = jnp.where(chip < last, 0.0, MASKED).astype(F32)
    left_bias = jnp.where(core == 0, left_chip, 0.0)
    right_bias = jnp.where(core == 0, 0.0, right_chip)
    average = pair_average()
    order = row_order()
    back = row_order_back()
    side_slot, near_slot = 1 - core, core
    for which in range(2):
        halo_ref[which, side_slot] = side_ref[which, 0]
        unpack(near_ref, which, average, halo_ref, near_slot, chips_ref, near_slot, 0)
        chips_ref[which, near_slot, 64:128, :] = near_ref[which, 256:320, :]
        chips_ref[which, side_slot] = far_ref[which, 0]

    def one_head(head, carry):
        lanes = pl.ds(pl.multiple_of(head * HEAD_DIM, HEAD_DIM), HEAD_DIM)
        q0 = [dot(order, q_ref[128 * n : 128 * n + 128, lanes]).astype(BF16) for n in range(4)]
        q1 = [halve(x) for x in q0]
        q2 = [halve(x) for x in q1]
        q3 = [halve(x) for x in q2]

        def piece(own, which, level, index, count):
            if index < 0:
                return halo_ref[which, 0, 128 * level : 128 * level + 128, lanes]
            if index >= count:
                return halo_ref[which, 1, 128 * level : 128 * level + 128, lanes]
            return own(which, index)

        def own_0(which, index):
            return kv_ref[which, 128 * index : 128 * index + 128, lanes]

        def own_1(which, index):
            return own1_ref[which, 128 * index : 128 * index + 128, lanes]

        def own_2(which, index):
            return own2_ref[which, :, lanes]

        def tile(query, own, level, index, count):
            near = [index - 1, index, index + 1]
            return weigh(
                query,
                [piece(own, 0, level, i, count) for i in near],
                [piece(own, 1, level, i, count) for i in near],
                left_bias if index == 0 else None,
                right_bias if index == count - 1 else None,
            )

        at_3 = weigh(
            jnp.concatenate(q3, axis=0),
            [chips_ref[0, 0, :, lanes], chip_ref[0, 0, :, lanes], chips_ref[0, 1, :, lanes]],
            [chips_ref[1, 0, :, lanes], chip_ref[1, 0, :, lanes], chips_ref[1, 1, :, lanes]],
            left_chip,
            right_chip,
        )
        at_2 = merge(tile(jnp.concatenate(q2, axis=0), own_2, 2, 0, 1), at_3)
        for j in range(2):
            half_2 = tuple(x[64 * j : 64 * j + 64] for x in at_2)
            query_1 = jnp.concatenate(q1[2 * j : 2 * j + 2], axis=0)
            at_1 = merge(tile(query_1, own_1, 1, j, 2), half_2)
            for n in (2 * j, 2 * j + 1):
                start = 64 * (n - 2 * j)
                half_1 = tuple(x[start : start + 64] for x in at_1)
                _, sums = merge(tile(q0[n], own_0, 0, n, 4), half_1)
                attended = (sums[:, :128] / sums[:, 128:]).astype(BF16)
                attended = dot(back, attended).astype(BF16)
                for copy in range(out_ref.shape[0]):
                    out_ref[copy, 128 * n : 128 * n + 128, lanes] = attended
        return carry

    lax.fori_loop(0, HEADS_HERE, one_head, 0)


def project_kernel(attended_ref, mine_ref, other_ref, out_ref, w_ref):
    core = lax.axis_index("core")
    groups = attended_ref.shape[0]
    for ref, slot in ((mine_ref, core), (other_ref, 1 - core)):
        for g in range(groups):
            for z in range(16):
                row = pl.multiple_of(32 * z + 16 * slot, 16)
                w_ref[g, pl.ds(row, 16), :] = ref[g, 16 * z : 16 * z + 16, :]
    for start in range(0, ROWS, 256):
        rows = slice(start, start + 256)
        total = dot(attended_ref[0, rows, :], w_ref[0], NT)
        for g in range(1, groups):
            total += dot(attended_ref[g, rows, :], w_ref[g], NT)
        out_ref[rows, :] = total.astype(BF16)


def call(kernel, outs, args, flops, scratch=(), in_specs=None):
    size = sum(a.size for a in args) * 2 + sum(2 * functools.reduce(lambda a, b: a * b, s, 1) for s in outs)
    shapes = [jax.ShapeDtypeStruct(s, BF16) for s in outs]
    return pl.pallas_call(
        kernel,
        out_shape=shapes if len(shapes) > 1 else shapes[0],
        in_specs=in_specs or [pl.BlockSpec(memory_space=pltpu.VMEM)] * len(args),
        scratch_shapes=list(scratch),
        cost_estimate=pl.CostEstimate(flops=flops, bytes_accessed=size, transcendentals=0),
        compiler_params=pltpu.CompilerParams(vmem_limit_bytes=VMEM_LIMIT),
    )(*args)


def on_device(q, k, v, w):
    x_size, z_size = lax.axis_size("x"), lax.axis_size("z")
    count = lax.axis_size("head")
    devices = 2 * x_size * z_size
    seq = ("x", "z", "core")
    swap = [(i, i ^ 1) for i in range(devices)]

    turn = [(a * count + b, b * count + a) for a in range(x_size) for b in range(count)]
    w_turned = lax.ppermute(w.T, ("x", "head"), turn)
    w_z = lax.all_to_all(
        jnp.broadcast_to(w_turned[None], (z_size,) + w_turned.shape), "z", 0, 0, tiled=True
    )
    w_z = w_z.reshape(1, -1, WIDTH)
    w_mine = lax.all_to_all(jnp.broadcast_to(w_z, (x_size,) + w_z.shape[1:]), "x", 0, 0, tiled=True)
    w_other = lax.ppermute(w_mine, seq, swap)

    kv, near_own, side_own, own1, own2, own3 = call(
        coarsen_kernel,
        [(2, ROWS, WIDTH), (2, 256, WIDTH), (2, 256, WIDTH), (2, 256, WIDTH), (2, 128, WIDTH), (2, 64, WIDTH)],
        (k, v),
        8 * 2 * 64 * 128 * 512,
        [pltpu.SemaphoreType.DMA((2,))],
        [pl.BlockSpec(memory_space=pltpu.HBM)] * 2,
    )
    pack_in = lax.ppermute(side_own, seq, swap)
    near, chip3, side = call(
        prepare_kernel,
        [(2, 320, WIDTH), (2, 1, 128, WIDTH), (2, 1, 384, WIDTH)],
        (pack_in, near_own, own3),
        2 * 2 * 64 * 128 * 512,
    )
    to_near = [(i, (i + 1 if i % 2 else i - 1) % devices) for i in range(devices)]
    to_far = [(i, (i - 3 if i % 2 else i + 3) % devices) for i in range(devices)]
    near_in = lax.ppermute(near, seq, to_near)
    far_in = lax.ppermute(chip3, seq, to_far)

    attended = call(
        attention_kernel,
        [(count, ROWS, WIDTH)],
        (q, kv, own1, own2, chip3, side, near_in, far_in),
        4 * 960 * 384 * 128 * 4,
        [pltpu.VMEM((2, 2, 384, WIDTH), BF16), pltpu.VMEM((2, 2, 128, WIDTH), BF16)],
    )
    attended = lax.all_to_all(attended, "head", 0, 0, tiled=True)
    return call(
        project_kernel,
        [(ROWS, WIDTH)],
        (attended, w_mine, w_other),
        2 * 512 * 512 * 2048,
        [pltpu.VMEM((count, WIDTH, WIDTH), BF16)],
    )


def solution(mesh):
    count = mesh.shape["head"]
    grid = Mesh(mesh.devices.reshape(4, mesh.shape["seq"] // 8, 2, count), ("x", "z", "core", "head"))
    rows = ("x", "z", "core")
    return jax.shard_map(
        on_device,
        mesh=grid,
        in_specs=(P(rows, "head"), P(rows, "head"), P(rows, "head"), P("head", rows)),
        out_specs=P(rows, "head"),
        check_vma=False,
    )
```

```python
import functools

import jax
import jax.numpy as jnp
from jax import lax
from jax.experimental import pallas as pl
from jax.experimental.pallas import tpu as pltpu
from jax.sharding import Mesh, PartitionSpec as P

HEAD_DIM = 128
BLOCK = 128
GROUP = 16
ROWS = 512
WIDTH = 512
HEADS_HERE = WIDTH // HEAD_DIM
SCALE2 = HEAD_DIM ** (-0.5) * 1.4426950408889634
MASKED = -1e30
F32 = jnp.float32
BF16 = jnp.bfloat16
VMEM_LIMIT = 24 * 1024 * 1024

NT = (((1,), (1,)), ((), ()))
NN = (((1,), (0,)), ((), ()))


def dot(a, b, dims=NN):
    return lax.dot_general(a, b, dims, preferred_element_type=F32)


def iota2(shape, dim):
    return lax.broadcasted_iota(jnp.int32, shape, dim)


def pair_average():
    row, col = iota2((64, 128), 0), iota2((64, 128), 1)
    return jnp.where((col >> 1) == 4 * (row & 15) + (row >> 4), 0.5, 0.0).astype(BF16)


def row_order():
    row, col = iota2((128, 128), 0), iota2((128, 128), 1)
    return jnp.where(col == 8 * (row & 15) + (row >> 4), 1.0, 0.0).astype(BF16)


def row_order_back():
    row, col = iota2((128, 128), 0), iota2((128, 128), 1)
    return jnp.where(row == 8 * (col & 15) + (col >> 4), 1.0, 0.0).astype(BF16)


def halve(x):
    wide = x.astype(F32)
    parts = [
        (wide[32 * i : 32 * i + 16] + wide[32 * i + 16 : 32 * i + 32]) * 0.5
        for i in range(x.shape[0] // 32)
    ]
    out = parts[0] if len(parts) == 1 else jnp.concatenate(parts, axis=0)
    return out.astype(BF16)


def double(x):
    parts = []
    for i in range(x.shape[0] // GROUP):
        piece = x[GROUP * i : GROUP * (i + 1)]
        parts += [piece, piece]
    return jnp.concatenate(parts, axis=0)


def coarsen_kernel(k_hbm, v_hbm, kv_ref, near_ref, side_ref, own1_ref, own2_ref, own3_ref, sems):
    core = lax.axis_index("core")
    copies = [
        pltpu.make_async_copy(source, kv_ref.at[which], sems.at[which])
        for which, source in enumerate((k_hbm, v_hbm))
    ]
    for copy in copies:
        copy.start()
    average = pair_average()
    for which, copy in enumerate(copies):
        copy.wait()
        own1 = [dot(average, kv_ref[which, 128 * n : 128 * n + 128, :]).astype(BF16) for n in range(4)]
        own2 = [halve(x) for x in own1]
        own3 = [halve(x) for x in own2]
        for n in range(4):
            own1_ref[which, 64 * n : 64 * n + 64, :] = own1[n]
            own2_ref[which, 32 * n : 32 * n + 32, :] = own2[n]
            own3_ref[which, 16 * n : 16 * n + 16, :] = own3[n]

        def edges(pack_ref, to_left):
            first, second, third, fourth = (0, 1, 2, 3) if to_left else (3, 2, 1, 0)
            pack_ref[which, 0:128, :] = kv_ref[which, 128 * first : 128 * first + 128, :]
            pack_ref[which, 128:192, :] = own1[second]
            pack_ref[which, 192:224, :] = own2[third]
            pack_ref[which, 224:256, :] = own2[fourth]

        def both_edges(near_is_left):
            edges(near_ref, near_is_left)
            edges(side_ref, not near_is_left)

        pl.when(core == 0)(functools.partial(both_edges, True))
        pl.when(core != 0)(functools.partial(both_edges, False))


def unpack(pack_ref, which, average, halo_ref, slot, chips_ref, chips_slot, start):
    edge = pack_ref[which, 0:128, :]
    edge1 = dot(average, edge).astype(BF16)
    next1 = pack_ref[which, 128:192, :]
    rest2 = pack_ref[which, 192:256, :]
    edge2, next2 = halve(edge1), halve(next1)
    pieces = ((0, edge), (128, edge1), (192, next1), (256, edge2), (288, next2), (320, rest2))
    for row, x in pieces:
        halo_ref[which, slot, row : row + x.shape[0], :] = x
    for row, x in ((0, halve(edge2)), (16, halve(next2)), (32, halve(rest2))):
        chips_ref[which, chips_slot, start + row : start + row + x.shape[0], :] = x


def prepare_kernel(pack_ref, near_own_ref, own3_ref, near_ref, chip_ref, side_ref):
    average = pair_average()
    for which in range(2):
        unpack(pack_ref, which, average, side_ref, 0, chip_ref, 0, 64)
        chip_ref[which, 0, 0:64, :] = own3_ref[which]
        near_ref[which, 0:256, :] = near_own_ref[which]
        near_ref[which, 256:320, :] = chip_ref[which, 0, 64:128, :]


def weigh(query, keys, values, bias_left, bias_right):
    scores = dot(query, jnp.concatenate(keys, axis=0), NT)
    if bias_left is not None:
        scores = jnp.concatenate([scores[:, :128] + bias_left, scores[:, 128:]], axis=1)
    if bias_right is not None:
        scores = jnp.concatenate([scores[:, :256], scores[:, 256:] + bias_right], axis=1)
    top = jnp.max(scores, axis=1, keepdims=True)
    probs = jnp.exp2((scores - top) * SCALE2).astype(BF16)
    wide = jnp.concatenate(values, axis=0)
    wide = jnp.concatenate([wide, jnp.ones_like(wide)], axis=1)
    return top, dot(probs, wide)


def merge(fine, coarse):
    fine_top, fine_sums = fine
    top, sums = double(coarse[0]), double(coarse[1])
    fall = jnp.exp2(-jnp.abs(fine_top - top) * SCALE2)
    higher = fine_top >= top
    fine_factor = jnp.where(higher, 1.0, fall)
    factor = jnp.where(higher, fall, 1.0)
    return jnp.maximum(fine_top, top), fine_sums * fine_factor + sums * factor


def attention_kernel(
    q_ref, kv_ref, own1_ref, own2_ref, chip_ref, side_ref, near_ref, far_ref,
    out_ref, halo_ref, chips_ref,
):
    core = lax.axis_index("core")
    chip = lax.axis_index(("x", "z_hi", "z_lo"))
    last = lax.axis_size(("x", "z_hi", "z_lo")) - 1
    left_chip = jnp.where(chip > 0, 0.0, MASKED).astype(F32)
    right_chip = jnp.where(chip < last, 0.0, MASKED).astype(F32)
    left_bias = jnp.where(core == 0, left_chip, 0.0)
    right_bias = jnp.where(core == 0, 0.0, right_chip)
    average = pair_average()
    order = row_order()
    back = row_order_back()
    side_slot, near_slot = 1 - core, core
    for which in range(2):
        halo_ref[which, side_slot] = side_ref[which, 0]
        unpack(near_ref, which, average, halo_ref, near_slot, chips_ref, near_slot, 0)
        chips_ref[which, near_slot, 64:128, :] = near_ref[which, 256:320, :]
        chips_ref[which, side_slot] = far_ref[which, 0]

    def one_head(head, carry):
        lanes = pl.ds(pl.multiple_of(head * HEAD_DIM, HEAD_DIM), HEAD_DIM)
        q0 = [dot(order, q_ref[128 * n : 128 * n + 128, lanes]).astype(BF16) for n in range(4)]
        q1 = [halve(x) for x in q0]
        q2 = [halve(x) for x in q1]
        q3 = [halve(x) for x in q2]

        def piece(own, which, level, index, count):
            if index < 0:
                return halo_ref[which, 0, 128 * level : 128 * level + 128, lanes]
            if index >= count:
                return halo_ref[which, 1, 128 * level : 128 * level + 128, lanes]
            return own(which, index)

        def own_0(which, index):
            return kv_ref[which, 128 * index : 128 * index + 128, lanes]

        def own_1(which, index):
            return own1_ref[which, 128 * index : 128 * index + 128, lanes]

        def own_2(which, index):
            return own2_ref[which, :, lanes]

        def tile(query, own, level, index, count):
            near = [index - 1, index, index + 1]
            return weigh(
                query,
                [piece(own, 0, level, i, count) for i in near],
                [piece(own, 1, level, i, count) for i in near],
                left_bias if index == 0 else None,
                right_bias if index == count - 1 else None,
            )

        at_3 = weigh(
            jnp.concatenate(q3, axis=0),
            [chips_ref[0, 0, :, lanes], chip_ref[0, 0, :, lanes], chips_ref[0, 1, :, lanes]],
            [chips_ref[1, 0, :, lanes], chip_ref[1, 0, :, lanes], chips_ref[1, 1, :, lanes]],
            left_chip,
            right_chip,
        )
        at_2 = merge(tile(jnp.concatenate(q2, axis=0), own_2, 2, 0, 1), at_3)
        for j in range(2):
            half_2 = tuple(x[64 * j : 64 * j + 64] for x in at_2)
            query_1 = jnp.concatenate(q1[2 * j : 2 * j + 2], axis=0)
            at_1 = merge(tile(query_1, own_1, 1, j, 2), half_2)
            for n in (2 * j, 2 * j + 1):
                start = 64 * (n - 2 * j)
                half_1 = tuple(x[start : start + 64] for x in at_1)
                _, sums = merge(tile(q0[n], own_0, 0, n, 4), half_1)
                attended = (sums[:, :128] / sums[:, 128:]).astype(BF16)
                out_ref[128 * n : 128 * n + 128, lanes] = dot(back, attended).astype(BF16)
        return carry

    lax.fori_loop(0, HEADS_HERE, one_head, 0)


def project_kernel(own_ref, one_ref, three_ref, upper_ref, lower_ref, mine_ref, other_ref, out_ref, w_ref):
    core = lax.axis_index("core")
    group = lax.axis_index("head")
    for ref, slot in ((mine_ref, core), (other_ref, 1 - core)):
        for place in range(4):
            source = group ^ place
            for z in range(16):
                row = pl.multiple_of(32 * z + 16 * slot, 16)
                start = 64 * (z % 4) + 16 * (z // 4)
                w_ref[place, pl.ds(row, 16), :] = ref[source, start : start + 16, :]
    for rows, across in ((slice(0, 256), upper_ref), (slice(256, 512), lower_ref)):
        total = dot(own_ref[rows, :], w_ref[0], NT)
        total += dot(one_ref[rows, :], w_ref[1], NT)
        total += dot(three_ref[rows, :], w_ref[3], NT)
        total += dot(across[...], w_ref[2], NT)
        out_ref[rows, :] = total.astype(BF16)


def call(kernel, outs, args, flops, scratch=(), in_specs=None):
    size = sum(a.size for a in args) * 2 + sum(2 * functools.reduce(lambda a, b: a * b, s, 1) for s in outs)
    shapes = [jax.ShapeDtypeStruct(s, BF16) for s in outs]
    return pl.pallas_call(
        kernel,
        out_shape=shapes if len(shapes) > 1 else shapes[0],
        in_specs=in_specs or [pl.BlockSpec(memory_space=pltpu.VMEM)] * len(args),
        scratch_shapes=list(scratch),
        cost_estimate=pl.CostEstimate(flops=flops, bytes_accessed=size, transcendentals=0),
        compiler_params=pltpu.CompilerParams(vmem_limit_bytes=VMEM_LIMIT),
    )(*args)


def swap_groups(x_size, z_size, count):
    pairs = [((a, b), (b, a)) for a in range(x_size) for b in range(a)]
    pairs += [((a, a), (a + 1, a + 1)) for a in range(0, x_size, 2)]
    return [
        [
            ((a * z_size + z) * 2 + core) * count + b
            for a, b in pair
            for z in range(z_lo, z_size, 4)
        ]
        for pair in [tuple(sorted(p)) for p in pairs]
        for z_lo in range(4)
        for core in range(2)
    ]


def all_to_all_copies(piece, groups, axis):
    peers = len(groups[0]) if groups else lax.axis_size(axis)
    copies = jnp.broadcast_to(piece[None], (peers,) + piece.shape)
    return lax.all_to_all(copies, axis, 0, 0, axis_index_groups=groups, tiled=True)


def on_device(q, k, v, w):
    x_size, z_size = lax.axis_size("x"), lax.axis_size("z_hi") * lax.axis_size("z_lo")
    count = lax.axis_size("head")
    devices = 2 * x_size * z_size
    seq = ("x", "z_hi", "z_lo", "core")
    swap = [(i, i ^ 1) for i in range(devices)]

    w_in = all_to_all_copies(w.T, swap_groups(x_size, z_size, count), ("x", "z_hi", "z_lo", "core", "head"))
    x, y = lax.axis_index("x"), lax.axis_index("head")
    first = jnp.where(x < y, 4, jnp.where(x > y, 0, 4 * (x % 2)))
    w_in = lax.dynamic_slice_in_dim(w_in, first, 4, axis=0)
    w_in = all_to_all_copies(w_in.reshape(-1, WIDTH), None, "z_lo").reshape(-1, WIDTH)
    w_mine = all_to_all_copies(w_in, None, "x")
    w_other = lax.ppermute(w_mine, seq, swap)

    kv, near_own, side_own, own1, own2, own3 = call(
        coarsen_kernel,
        [(2, ROWS, WIDTH), (2, 256, WIDTH), (2, 256, WIDTH), (2, 256, WIDTH), (2, 128, WIDTH), (2, 64, WIDTH)],
        (k, v),
        8 * 2 * 64 * 128 * 512,
        [pltpu.SemaphoreType.DMA((2,))],
        [pl.BlockSpec(memory_space=pltpu.HBM)] * 2,
    )
    pack_in = lax.ppermute(side_own, seq, swap)
    near, chip3, side = call(
        prepare_kernel,
        [(2, 320, WIDTH), (2, 1, 128, WIDTH), (2, 1, 384, WIDTH)],
        (pack_in, near_own, own3),
        2 * 2 * 64 * 128 * 512,
    )
    to_near = [(i, (i + 1 if i % 2 else i - 1) % devices) for i in range(devices)]
    to_far = [(i, (i - 3 if i % 2 else i + 3) % devices) for i in range(devices)]
    near_in = lax.ppermute(near, seq, to_near)
    far_in = lax.ppermute(chip3, seq, to_far)

    attended = call(
        attention_kernel,
        [(ROWS, WIDTH)],
        (q, kv, own1, own2, chip3, side, near_in, far_in),
        4 * 960 * 384 * 128 * 4,
        [pltpu.VMEM((2, 2, 384, WIDTH), BF16), pltpu.VMEM((2, 2, 128, WIDTH), BF16)],
    )

    one = [(i, i ^ 1) for i in range(count)]
    three = [(i, i ^ 3) for i in range(count)]
    half = ROWS // 2
    from_one = lax.ppermute(attended, "head", one)
    from_three = lax.ppermute(attended, "head", three)
    upper = lax.ppermute(from_one[:half], "head", three)
    lower = lax.ppermute(from_three[half:], "head", one)
    return call(
        project_kernel,
        [(ROWS, WIDTH)],
        (attended, from_one, from_three, upper, lower, w_mine, w_other),
        2 * 512 * 512 * 2048,
        [pltpu.VMEM((count, WIDTH, WIDTH), BF16)],
    )


def solution(mesh):
    count = mesh.shape["head"]
    rows = ("x", "z_hi", "z_lo", "core")
    grid = Mesh(mesh.devices.reshape(4, 4, 4, 2, count), rows + ("head",))
    return jax.shard_map(
        on_device,
        mesh=grid,
        in_specs=(P(rows, "head"), P(rows, "head"), P(rows, "head"), P("head", rows)),
        out_specs=P(rows, "head"),
        check_vma=False,
    )
```

```python
import functools

import jax
import jax.numpy as jnp
from jax import lax
from jax.experimental import pallas as pl
from jax.experimental.pallas import tpu as pltpu
from jax.sharding import Mesh, PartitionSpec as P

HEAD_DIM = 128
BLOCK = 128
GROUP = 16
ROWS = 512
WIDTH = 512
HEADS_HERE = WIDTH // HEAD_DIM
SCALE2 = HEAD_DIM ** (-0.5) * 1.4426950408889634
MASKED = -1e30
F32 = jnp.float32
BF16 = jnp.bfloat16
VMEM_LIMIT = 16 * 1024 * 1024
VMEM_ALL = 60 * 1024 * 1024

NT = (((1,), (1,)), ((), ()))
NN = (((1,), (0,)), ((), ()))


def dot(a, b, dims=NN):
    return lax.dot_general(a, b, dims, preferred_element_type=F32)


def iota2(shape, dim):
    return lax.broadcasted_iota(jnp.int32, shape, dim)


def pair_average():
    row, col = iota2((64, 128), 0), iota2((64, 128), 1)
    return jnp.where((col >> 1) == 4 * (row & 15) + (row >> 4), 0.5, 0.0).astype(BF16)


def row_order():
    row, col = iota2((128, 128), 0), iota2((128, 128), 1)
    return jnp.where(col == 8 * (row & 15) + (row >> 4), 1.0, 0.0).astype(BF16)


def row_order_back():
    row, col = iota2((128, 128), 0), iota2((128, 128), 1)
    return jnp.where(row == 8 * (col & 15) + (col >> 4), 1.0, 0.0).astype(BF16)


def halve(x):
    wide = x.astype(F32)
    parts = [
        (wide[32 * i : 32 * i + 16] + wide[32 * i + 16 : 32 * i + 32]) * 0.5
        for i in range(x.shape[0] // 32)
    ]
    out = parts[0] if len(parts) == 1 else jnp.concatenate(parts, axis=0)
    return out.astype(BF16)


def double(x):
    parts = []
    for i in range(x.shape[0] // GROUP):
        piece = x[GROUP * i : GROUP * (i + 1)]
        parts += [piece, piece]
    return jnp.concatenate(parts, axis=0)


def start_copies(sems, pairs):
    copies = [
        pltpu.make_async_copy(source, target, sems.at[i]) for i, (source, target) in enumerate(pairs)
    ]
    for copy in copies:
        copy.start()
    return copies


def coarsen_kernel(
    k_hbm, v_hbm, w_hbm, near_ref, side_ref, own1_ref, own2_ref, own3_ref, w_ref, kv_ref, sems
):
    core = lax.axis_index("core")
    pairs = ((k_hbm, kv_ref.at[0]), (v_hbm, kv_ref.at[1]), (w_hbm, w_ref))
    *copies, w_copy = start_copies(sems, pairs)
    average = pair_average()
    for which, copy in enumerate(copies):
        copy.wait()
        own1 = [dot(average, kv_ref[which, 128 * n : 128 * n + 128, :]).astype(BF16) for n in range(4)]
        own2 = [halve(x) for x in own1]
        own3 = [halve(x) for x in own2]
        for n in range(4):
            own1_ref[which, 64 * n : 64 * n + 64, :] = own1[n]
            own2_ref[which, 32 * n : 32 * n + 32, :] = own2[n]
            own3_ref[which, 16 * n : 16 * n + 16, :] = own3[n]

        def edges(pack_ref, to_left):
            first, second, third, fourth = (0, 1, 2, 3) if to_left else (3, 2, 1, 0)
            pack_ref[which, 0:128, :] = kv_ref[which, 128 * first : 128 * first + 128, :]
            pack_ref[which, 128:192, :] = own1[second]
            pack_ref[which, 192:224, :] = own2[third]
            pack_ref[which, 224:256, :] = own2[fourth]

        def both_edges(near_is_left):
            edges(near_ref, near_is_left)
            edges(side_ref, not near_is_left)

        pl.when(core == 0)(functools.partial(both_edges, True))
        pl.when(core != 0)(functools.partial(both_edges, False))
    w_copy.wait()


def unpack(pack_ref, which, average, halo_ref, slot, chips_ref, chips_slot, start):
    edge = pack_ref[which, 0:128, :]
    edge1 = dot(average, edge).astype(BF16)
    next1 = pack_ref[which, 128:192, :]
    rest2 = pack_ref[which, 192:256, :]
    edge2, next2 = halve(edge1), halve(next1)
    pieces = ((0, edge), (128, edge1), (192, next1), (256, edge2), (288, next2), (320, rest2))
    for row, x in pieces:
        halo_ref[which, slot, row : row + x.shape[0], :] = x
    for row, x in ((0, halve(edge2)), (16, halve(next2)), (32, halve(rest2))):
        chips_ref[which, chips_slot, start + row : start + row + x.shape[0], :] = x


def prepare_kernel(pack_hbm, near_own_hbm, own3_hbm, gate_hbm, near_ref, chip_ref, side_ref, pack_ref, sems):
    copies = start_copies(
        sems,
        (
            (pack_hbm, pack_ref),
            (near_own_hbm, near_ref.at[:, pl.ds(0, 256), :]),
            (own3_hbm, chip_ref.at[:, 0, pl.ds(0, 64), :]),
        ),
    )
    average = pair_average()
    copies[0].wait()
    for which in range(2):
        unpack(pack_ref, which, average, side_ref, 0, chip_ref, 0, 64)
        near_ref[which, 256:320, :] = chip_ref[which, 0, 64:128, :]
    copies[1].wait()
    copies[2].wait()


def copies_kernel(piece_ref, gate_hbm, out_ref):
    piece = piece_ref[...]
    for i in range(out_ref.shape[0]):
        out_ref[i] = piece


def gate_kernel(value_hbm, gate_hbm, out_hbm):
    pass


def stack_kernel(a_hbm, b_hbm, c_hbm, d_hbm, gate_1_hbm, gate_3_hbm, out_hbm, sems):
    sources = (a_hbm, b_hbm, c_hbm, d_hbm)
    for copy in start_copies(sems, [(x, out_hbm.at[i]) for i, x in enumerate(sources)]):
        copy.wait()


def weigh(query, keys, values, bias_left, bias_right):
    scores = dot(query, jnp.concatenate(keys, axis=0), NT)
    if bias_left is not None:
        scores = jnp.concatenate([scores[:, :128] + bias_left, scores[:, 128:]], axis=1)
    if bias_right is not None:
        scores = jnp.concatenate([scores[:, :256], scores[:, 256:] + bias_right], axis=1)
    top = jnp.max(scores, axis=1, keepdims=True)
    probs = jnp.exp2((scores - top) * SCALE2).astype(BF16)
    wide = jnp.concatenate(values, axis=0)
    wide = jnp.concatenate([wide, jnp.ones_like(wide)], axis=1)
    return top, dot(probs, wide)


def merge(fine, coarse):
    fine_top, fine_sums = fine
    top, sums = double(coarse[0]), double(coarse[1])
    fall = jnp.exp2(-jnp.abs(fine_top - top) * SCALE2)
    higher = fine_top >= top
    fine_factor = jnp.where(higher, 1.0, fall)
    factor = jnp.where(higher, fall, 1.0)
    return jnp.maximum(fine_top, top), fine_sums * fine_factor + sums * factor


def attention_kernel(
    q_hbm, k_hbm, v_hbm, own1_hbm, own2_hbm, chip_hbm, side_hbm, near_hbm, far_hbm,
    out_ref, q_ref, kv_ref, own1_ref, own2_ref, chip_ref, near_ref, halo_ref, chips_ref, sems,
):
    core = lax.axis_index("core")
    chip = lax.axis_index(("x", "z"))
    last = lax.axis_size(("x", "z")) - 1
    left_chip = jnp.where(chip > 0, 0.0, MASKED).astype(F32)
    right_chip = jnp.where(chip < last, 0.0, MASKED).astype(F32)
    left_bias = jnp.where(core == 0, left_chip, 0.0)
    right_bias = jnp.where(core == 0, 0.0, right_chip)
    average = pair_average()
    order = row_order()
    back = row_order_back()
    side_slot, near_slot = 1 - core, core
    copies = start_copies(
        sems,
        [(near_hbm, near_ref)]
        + [(side_hbm.at[i, 0], halo_ref.at[i, side_slot]) for i in range(2)]
        + [(far_hbm.at[i, 0], chips_ref.at[i, side_slot]) for i in range(2)]
        + [(q_hbm, q_ref), (k_hbm, kv_ref.at[0]), (v_hbm, kv_ref.at[1])]
        + [(own1_hbm, own1_ref), (own2_hbm, own2_ref), (chip_hbm, chip_ref)],
    )
    copies[0].wait()
    for which in range(2):
        unpack(near_ref, which, average, halo_ref, near_slot, chips_ref, near_slot, 0)
        chips_ref[which, near_slot, 64:128, :] = near_ref[which, 256:320, :]
    for copy in copies[1:]:
        copy.wait()

    def one_head(head, carry):
        lanes = pl.ds(pl.multiple_of(head * HEAD_DIM, HEAD_DIM), HEAD_DIM)
        q0 = [dot(order, q_ref[128 * n : 128 * n + 128, lanes]).astype(BF16) for n in range(4)]
        q1 = [halve(x) for x in q0]
        q2 = [halve(x) for x in q1]
        q3 = [halve(x) for x in q2]

        def piece(own, which, level, index, count):
            if index < 0:
                return halo_ref[which, 0, 128 * level : 128 * level + 128, lanes]
            if index >= count:
                return halo_ref[which, 1, 128 * level : 128 * level + 128, lanes]
            return own(which, index)

        def own_0(which, index):
            return kv_ref[which, 128 * index : 128 * index + 128, lanes]

        def own_1(which, index):
            return own1_ref[which, 128 * index : 128 * index + 128, lanes]

        def own_2(which, index):
            return own2_ref[which, :, lanes]

        def tile(query, own, level, index, count):
            near = [index - 1, index, index + 1]
            return weigh(
                query,
                [piece(own, 0, level, i, count) for i in near],
                [piece(own, 1, level, i, count) for i in near],
                left_bias if index == 0 else None,
                right_bias if index == count - 1 else None,
            )

        at_3 = weigh(
            jnp.concatenate(q3, axis=0),
            [chips_ref[0, 0, :, lanes], chip_ref[0, 0, :, lanes], chips_ref[0, 1, :, lanes]],
            [chips_ref[1, 0, :, lanes], chip_ref[1, 0, :, lanes], chips_ref[1, 1, :, lanes]],
            left_chip,
            right_chip,
        )
        at_2 = merge(tile(jnp.concatenate(q2, axis=0), own_2, 2, 0, 1), at_3)
        for j in range(2):
            half_2 = tuple(x[64 * j : 64 * j + 64] for x in at_2)
            query_1 = jnp.concatenate(q1[2 * j : 2 * j + 2], axis=0)
            at_1 = merge(tile(query_1, own_1, 1, j, 2), half_2)
            for n in (2 * j, 2 * j + 1):
                start = 64 * (n - 2 * j)
                half_1 = tuple(x[start : start + 64] for x in at_1)
                _, sums = merge(tile(q0[n], own_0, 0, n, 4), half_1)
                attended = (sums[:, :128] / sums[:, 128:]).astype(BF16)
                out_ref[128 * n : 128 * n + 128, lanes] = dot(back, attended).astype(BF16)
        return carry

    lax.fori_loop(0, HEADS_HERE, one_head, 0)


def project_kernel(
    own_hbm, one_hbm, three_hbm, upper_hbm, lower_hbm, mine_hbm, other_hbm,
    out_ref, own_ref, one_ref, three_ref, across_ref, w_ref, sems,
):
    core = lax.axis_index("core")
    twist = lax.axis_index("head") ^ lax.axis_index("x")
    half = ROWS // 2
    order = (0, 1, 3, 2)
    pairs = [
        (ref.at[twist ^ i], w_ref.at[i, :, slot])
        for i in order
        for ref, slot in ((mine_hbm, core), (other_hbm, 1 - core))
    ]
    pairs += [(own_hbm, own_ref), (one_hbm, one_ref), (three_hbm, three_ref)]
    pairs += [(upper_hbm, across_ref.at[pl.ds(0, half)]), (lower_hbm, across_ref.at[pl.ds(half, half)])]
    for copy in start_copies(sems, pairs):
        copy.wait()
    parts = (own_ref, one_ref, three_ref, across_ref)
    for rows in (slice(0, half), slice(half, ROWS)):
        total = None
        for ref, i in zip(parts, order):
            part = dot(ref[rows, :], w_ref[i].reshape(WIDTH, WIDTH), NT)
            total = part if total is None else total + part
        out_ref[rows, :] = total.astype(BF16)


def call(kernel, outs, args, work_us, scratch=(), copies=0, in_spec=pl.ANY, out_spec=pltpu.VMEM, aliases=None, limit=VMEM_LIMIT):
    shapes = [jax.ShapeDtypeStruct(s, BF16) for s in outs]
    one = len(shapes) == 1
    out_specs = [pl.BlockSpec(memory_space=out_spec)] * len(outs)
    return pl.pallas_call(
        kernel,
        out_shape=shapes[0] if one else shapes,
        in_specs=[pl.BlockSpec(memory_space=in_spec)] * len(args),
        out_specs=out_specs[0] if one else out_specs,
        scratch_shapes=[pltpu.VMEM(s, BF16) for s in scratch]
        + ([pltpu.SemaphoreType.DMA((copies,))] if copies else []),
        input_output_aliases=aliases or {},
        cost_estimate=pl.CostEstimate(flops=int(work_us * 1.1e9), bytes_accessed=0, transcendentals=0),
        compiler_params=pltpu.CompilerParams(vmem_limit_bytes=limit),
    )(*args)


def on_device(q, k, v, w):
    x_size, z_size = lax.axis_size("x"), lax.axis_size("z")
    count = lax.axis_size("head")
    devices = 2 * x_size * z_size
    seq = ("x", "z", "core")
    swap = [(i, i ^ 1) for i in range(devices)]

    near_own, side_own, own1, own2, own3, w_own = call(
        coarsen_kernel,
        [(2, 256, WIDTH), (2, 256, WIDTH), (2, 256, WIDTH), (2, 128, WIDTH), (2, 64, WIDTH), (16, WIDTH)],
        (k, v, w.T),
        3,
        [(2, ROWS, WIDTH)],
        3,
        limit=VMEM_ALL,
    )
    pack_in = lax.ppermute(side_own, seq, swap)
    turn = [(a * count + b, b * count + a) for a in range(x_size) for b in range(count)]
    w_turned = lax.ppermute(w_own, ("x", "head"), turn)

    near, chip3, side = call(
        prepare_kernel,
        [(2, 320, WIDTH), (2, 1, 128, WIDTH), (2, 1, 384, WIDTH)],
        (pack_in, near_own, own3, w_turned),
        2,
        [(2, 256, WIDTH)],
        3,
    )
    to_near = [(i, (i + 1 if i % 2 else i - 1) % devices) for i in range(devices)]
    to_far = [(i, (i - 3 if i % 2 else i + 3) % devices) for i in range(devices)]
    near_in = lax.ppermute(near, seq, to_near)
    far_in = lax.ppermute(chip3, seq, to_far)

    w_copies = pl.pallas_call(
        copies_kernel,
        out_shape=jax.ShapeDtypeStruct((z_size,) + w_turned.shape, BF16),
        in_specs=[pl.BlockSpec(memory_space=pltpu.VMEM), pl.BlockSpec(memory_space=pl.ANY)],
        cost_estimate=pl.CostEstimate(flops=10**8, bytes_accessed=0, transcendentals=0),
    )(w_turned, chip3)
    w_z = lax.all_to_all(w_copies, "z", 0, 0, tiled=True)

    attended = call(
        attention_kernel,
        [(ROWS, WIDTH)],
        (q, k, v, own1, own2, chip3, side, near_in, far_in),
        11,
        [
            (ROWS, WIDTH), (2, ROWS, WIDTH), (2, 256, WIDTH), (2, 128, WIDTH), (2, 1, 128, WIDTH),
            (2, 320, WIDTH), (2, 2, 384, WIDTH), (2, 2, 128, WIDTH),
        ],
        11,
    )

    one = [(i, i ^ 1) for i in range(count)]
    three = [(i, i ^ 3) for i in range(count)]
    half = ROWS // 2
    from_one = lax.ppermute(attended, "head", one)
    from_three = lax.ppermute(attended, "head", three)

    w_z = call(gate_kernel, [w_z.shape], (w_z, attended), 0.1, out_spec=pl.ANY, aliases={0: 0})
    w_x = [w_z] + [
        lax.ppermute(w_z, "x", [(i, i ^ j) for i in range(x_size)]) for j in range(1, x_size)
    ]
    w_mine = call(stack_kernel, [(x_size,) + w_z.shape], w_x + [from_one, from_three], 1, (), x_size, out_spec=pl.ANY)
    w_other = lax.ppermute(w_mine, seq, swap)

    upper = lax.ppermute(from_one[:half], "head", three)
    lower = lax.ppermute(from_three[half:], "head", one)
    return call(
        project_kernel,
        [(ROWS, WIDTH)],
        (attended, from_one, from_three, upper, lower, w_mine, w_other),
        3,
        [(ROWS, WIDTH)] * 4 + [(count, z_size, 2, 16, WIDTH)],
        13,
    )


def solution(mesh):
    count = mesh.shape["head"]
    rows = ("x", "z", "core")
    grid = Mesh(mesh.devices.reshape(4, mesh.shape["seq"] // 8, 2, count), rows + ("head",))
    return jax.shard_map(
        on_device,
        mesh=grid,
        in_specs=(P(rows, "head"), P(rows, "head"), P(rows, "head"), P("head", rows)),
        out_specs=P(rows, "head"),
        check_vma=False,
    )
```

```python
import functools

import jax
import jax.numpy as jnp
from jax import lax
from jax.experimental import pallas as pl
from jax.experimental.pallas import tpu as pltpu
from jax.sharding import Mesh, PartitionSpec as P

HEAD_DIM = 128
BLOCK = 128
GROUP = 16
ROWS = 512
WIDTH = 512
HEADS_HERE = WIDTH // HEAD_DIM
SCALE2 = HEAD_DIM ** (-0.5) * 1.4426950408889634
MASKED = -1e30
F32 = jnp.float32
BF16 = jnp.bfloat16
VMEM_LIMIT = 16 * 1024 * 1024
VMEM_ALL = 60 * 1024 * 1024

NT = (((1,), (1,)), ((), ()))
NN = (((1,), (0,)), ((), ()))


def dot(a, b, dims=NN):
    return lax.dot_general(a, b, dims, preferred_element_type=F32)


def iota2(shape, dim):
    return lax.broadcasted_iota(jnp.int32, shape, dim)


def pair_average():
    row, col = iota2((64, 128), 0), iota2((64, 128), 1)
    return jnp.where((col >> 1) == 4 * (row & 15) + (row >> 4), 0.5, 0.0).astype(BF16)


def row_order():
    row, col = iota2((128, 128), 0), iota2((128, 128), 1)
    return jnp.where(col == 8 * (row & 15) + (row >> 4), 1.0, 0.0).astype(BF16)


def row_order_back():
    row, col = iota2((128, 128), 0), iota2((128, 128), 1)
    return jnp.where(row == 8 * (col & 15) + (col >> 4), 1.0, 0.0).astype(BF16)


def halve(x):
    wide = x.astype(F32)
    parts = [
        (wide[32 * i : 32 * i + 16] + wide[32 * i + 16 : 32 * i + 32]) * 0.5
        for i in range(x.shape[0] // 32)
    ]
    out = parts[0] if len(parts) == 1 else jnp.concatenate(parts, axis=0)
    return out.astype(BF16)


def double(x):
    parts = []
    for i in range(x.shape[0] // GROUP):
        piece = x[GROUP * i : GROUP * (i + 1)]
        parts += [piece, piece]
    return jnp.concatenate(parts, axis=0)


def start_copies(sems, pairs):
    copies = [
        pltpu.make_async_copy(source, target, sems.at[i]) for i, (source, target) in enumerate(pairs)
    ]
    for copy in copies:
        copy.start()
    return copies


def coarsen_kernel(
    k_hbm, v_hbm, near_ref, side_ref, own1_ref, own2_ref, own3_ref, kv_ref, sems
):
    core = lax.axis_index("core")
    copies = start_copies(sems, ((k_hbm, kv_ref.at[0]), (v_hbm, kv_ref.at[1])))
    average = pair_average()
    for which, copy in enumerate(copies):
        copy.wait()
        own1 = [dot(average, kv_ref[which, 128 * n : 128 * n + 128, :]).astype(BF16) for n in range(4)]
        own2 = [halve(x) for x in own1]
        own3 = [halve(x) for x in own2]
        for n in range(4):
            own1_ref[which, 64 * n : 64 * n + 64, :] = own1[n]
            own2_ref[which, 32 * n : 32 * n + 32, :] = own2[n]
            own3_ref[which, 16 * n : 16 * n + 16, :] = own3[n]

        def edges(pack_ref, to_left):
            first, second, third, fourth = (0, 1, 2, 3) if to_left else (3, 2, 1, 0)
            pack_ref[which, 0:128, :] = kv_ref[which, 128 * first : 128 * first + 128, :]
            pack_ref[which, 128:192, :] = own1[second]
            pack_ref[which, 192:224, :] = own2[third]
            pack_ref[which, 224:256, :] = own2[fourth]

        def both_edges(near_is_left):
            edges(near_ref, near_is_left)
            edges(side_ref, not near_is_left)

        pl.when(core == 0)(functools.partial(both_edges, True))
        pl.when(core != 0)(functools.partial(both_edges, False))

def unpack(pack_ref, which, average, halo_ref, slot, chips_ref, chips_slot, start):
    edge = pack_ref[which, 0:128, :]
    edge1 = dot(average, edge).astype(BF16)
    next1 = pack_ref[which, 128:192, :]
    rest2 = pack_ref[which, 192:256, :]
    edge2, next2 = halve(edge1), halve(next1)
    pieces = ((0, edge), (128, edge1), (192, next1), (256, edge2), (288, next2), (320, rest2))
    for row, x in pieces:
        halo_ref[which, slot, row : row + x.shape[0], :] = x
    for row, x in ((0, halve(edge2)), (16, halve(next2)), (32, halve(rest2))):
        chips_ref[which, chips_slot, start + row : start + row + x.shape[0], :] = x


def prepare_kernel(pack_hbm, near_own_hbm, own3_hbm, near_ref, chip_ref, side_ref, pack_ref, sems):
    copies = start_copies(
        sems,
        (
            (pack_hbm, pack_ref),
            (near_own_hbm, near_ref.at[:, pl.ds(0, 256), :]),
            (own3_hbm, chip_ref.at[:, 0, pl.ds(0, 64), :]),
        ),
    )
    average = pair_average()
    copies[0].wait()
    for which in range(2):
        unpack(pack_ref, which, average, side_ref, 0, chip_ref, 0, 64)
        near_ref[which, 256:320, :] = chip_ref[which, 0, 64:128, :]
    copies[1].wait()
    copies[2].wait()


def weigh(query, keys, values, bias_left, bias_right):
    scores = dot(query, jnp.concatenate(keys, axis=0), NT)
    if bias_left is not None:
        scores = jnp.concatenate([scores[:, :128] + bias_left, scores[:, 128:]], axis=1)
    if bias_right is not None:
        scores = jnp.concatenate([scores[:, :256], scores[:, 256:] + bias_right], axis=1)
    top = jnp.max(scores, axis=1, keepdims=True)
    probs = jnp.exp2((scores - top) * SCALE2).astype(BF16)
    wide = jnp.concatenate(values, axis=0)
    wide = jnp.concatenate([wide, jnp.ones_like(wide)], axis=1)
    return top, dot(probs, wide)


def merge(fine, coarse):
    fine_top, fine_sums = fine
    top, sums = double(coarse[0]), double(coarse[1])
    fall = jnp.exp2(-jnp.abs(fine_top - top) * SCALE2)
    higher = fine_top >= top
    fine_factor = jnp.where(higher, 1.0, fall)
    factor = jnp.where(higher, fall, 1.0)
    return jnp.maximum(fine_top, top), fine_sums * fine_factor + sums * factor


def attention_kernel(
    q_hbm, k_hbm, v_hbm, own1_hbm, own2_hbm, chip_hbm, side_hbm, near_hbm, far_hbm,
    out_ref, q_ref, kv_ref, own1_ref, own2_ref, chip_ref, near_ref, halo_ref, chips_ref, sems,
):
    core = lax.axis_index("core")
    chip = lax.axis_index(("x", "z"))
    last = lax.axis_size(("x", "z")) - 1
    left_chip = jnp.where(chip > 0, 0.0, MASKED).astype(F32)
    right_chip = jnp.where(chip < last, 0.0, MASKED).astype(F32)
    left_bias = jnp.where(core == 0, left_chip, 0.0)
    right_bias = jnp.where(core == 0, 0.0, right_chip)
    average = pair_average()
    order = row_order()
    back = row_order_back()
    side_slot, near_slot = 1 - core, core
    copies = start_copies(
        sems,
        [(near_hbm, near_ref)]
        + [(side_hbm.at[i, 0], halo_ref.at[i, side_slot]) for i in range(2)]
        + [(far_hbm.at[i, 0], chips_ref.at[i, side_slot]) for i in range(2)]
        + [(q_hbm, q_ref), (k_hbm, kv_ref.at[0]), (v_hbm, kv_ref.at[1])]
        + [(own1_hbm, own1_ref), (own2_hbm, own2_ref), (chip_hbm, chip_ref)],
    )
    copies[0].wait()
    for which in range(2):
        unpack(near_ref, which, average, halo_ref, near_slot, chips_ref, near_slot, 0)
        chips_ref[which, near_slot, 64:128, :] = near_ref[which, 256:320, :]
    for copy in copies[1:]:
        copy.wait()

    def one_head(head, carry):
        lanes = pl.ds(pl.multiple_of(head * HEAD_DIM, HEAD_DIM), HEAD_DIM)
        q0 = [dot(order, q_ref[128 * n : 128 * n + 128, lanes]).astype(BF16) for n in range(4)]
        q1 = [halve(x) for x in q0]
        q2 = [halve(x) for x in q1]
        q3 = [halve(x) for x in q2]

        def piece(own, which, level, index, count):
            if index < 0:
                return halo_ref[which, 0, 128 * level : 128 * level + 128, lanes]
            if index >= count:
                return halo_ref[which, 1, 128 * level : 128 * level + 128, lanes]
            return own(which, index)

        def own_0(which, index):
            return kv_ref[which, 128 * index : 128 * index + 128, lanes]

        def own_1(which, index):
            return own1_ref[which, 128 * index : 128 * index + 128, lanes]

        def own_2(which, index):
            return own2_ref[which, :, lanes]

        def tile(query, own, level, index, count):
            near = [index - 1, index, index + 1]
            return weigh(
                query,
                [piece(own, 0, level, i, count) for i in near],
                [piece(own, 1, level, i, count) for i in near],
                left_bias if index == 0 else None,
                right_bias if index == count - 1 else None,
            )

        at_3 = weigh(
            jnp.concatenate(q3, axis=0),
            [chips_ref[0, 0, :, lanes], chip_ref[0, 0, :, lanes], chips_ref[0, 1, :, lanes]],
            [chips_ref[1, 0, :, lanes], chip_ref[1, 0, :, lanes], chips_ref[1, 1, :, lanes]],
            left_chip,
            right_chip,
        )
        at_2 = merge(tile(jnp.concatenate(q2, axis=0), own_2, 2, 0, 1), at_3)
        for j in range(2):
            half_2 = tuple(x[64 * j : 64 * j + 64] for x in at_2)
            query_1 = jnp.concatenate(q1[2 * j : 2 * j + 2], axis=0)
            at_1 = merge(tile(query_1, own_1, 1, j, 2), half_2)
            for n in (2 * j, 2 * j + 1):
                start = 64 * (n - 2 * j)
                half_1 = tuple(x[start : start + 64] for x in at_1)
                _, sums = merge(tile(q0[n], own_0, 0, n, 4), half_1)
                attended = (sums[:, :128] / sums[:, 128:]).astype(BF16)
                out_ref[128 * n : 128 * n + 128, lanes] = dot(back, attended).astype(BF16)
        return carry

    lax.fori_loop(0, HEADS_HERE, one_head, 0)


def project_kernel(
    own_hbm, one_hbm, three_hbm, upper_hbm, lower_hbm, w_hbm,
    out_ref, own_ref, one_ref, three_ref, across_ref, w_ref, sems,
):
    group = lax.axis_index("head")
    half = ROWS // 2
    order = (0, 1, 3, 2)
    pairs = [(w_hbm.at[:, group ^ i], w_ref.at[i]) for i in order]
    pairs += [(own_hbm, own_ref), (one_hbm, one_ref), (three_hbm, three_ref)]
    pairs += [(upper_hbm, across_ref.at[pl.ds(0, half)]), (lower_hbm, across_ref.at[pl.ds(half, half)])]
    for copy in start_copies(sems, pairs):
        copy.wait()
    parts = (own_ref, one_ref, three_ref, across_ref)
    for rows in (slice(0, half), slice(half, ROWS)):
        total = None
        for ref, i in zip(parts, order):
            part = dot(ref[rows, :], w_ref[i].reshape(WIDTH, WIDTH), NT)
            total = part if total is None else total + part
        out_ref[rows, :] = total.astype(BF16)


def call(kernel, outs, args, work_us, scratch=(), copies=0, in_spec=pl.ANY, out_spec=pltpu.VMEM, aliases=None, limit=VMEM_LIMIT):
    shapes = [jax.ShapeDtypeStruct(s, BF16) for s in outs]
    one = len(shapes) == 1
    out_specs = [pl.BlockSpec(memory_space=out_spec)] * len(outs)
    return pl.pallas_call(
        kernel,
        out_shape=shapes[0] if one else shapes,
        in_specs=[pl.BlockSpec(memory_space=in_spec)] * len(args),
        out_specs=out_specs[0] if one else out_specs,
        scratch_shapes=[pltpu.VMEM(s, BF16) for s in scratch]
        + ([pltpu.SemaphoreType.DMA((copies,))] if copies else []),
        input_output_aliases=aliases or {},
        cost_estimate=pl.CostEstimate(flops=int(work_us * 1.1e9), bytes_accessed=0, transcendentals=0),
        compiler_params=pltpu.CompilerParams(vmem_limit_bytes=limit),
    )(*args)


def on_device(q, k, v, w):
    x_size, z_size = lax.axis_size("x"), lax.axis_size("z")
    count = lax.axis_size("head")
    devices = 2 * x_size * z_size
    seq = ("x", "z", "core")
    swap = [(i, i ^ 1) for i in range(devices)]

    plane = ("x", "head")
    shards = jnp.broadcast_to(w.T[None], (x_size * count, 16, WIDTH))
    shards = lax.all_to_all(shards, plane, 0, 0, tiled=True)
    shards = lax.dynamic_slice_in_dim(shards, lax.axis_index("head") * count, count, axis=0)
    w_all = lax.all_gather(shards, ("z", "core"), axis=0)

    near_own, side_own, own1, own2, own3 = call(
        coarsen_kernel,
        [(2, 256, WIDTH), (2, 256, WIDTH), (2, 256, WIDTH), (2, 128, WIDTH), (2, 64, WIDTH)],
        (k, v),
        3,
        [(2, ROWS, WIDTH)],
        2,
        limit=VMEM_ALL,
    )
    pack_in = lax.ppermute(side_own, seq, swap)
    near, chip3, side = call(
        prepare_kernel,
        [(2, 320, WIDTH), (2, 1, 128, WIDTH), (2, 1, 384, WIDTH)],
        (pack_in, near_own, own3),
        2,
        [(2, 256, WIDTH)],
        3,
    )
    to_near = [(i, (i + 1 if i % 2 else i - 1) % devices) for i in range(devices)]
    to_far = [(i, (i - 3 if i % 2 else i + 3) % devices) for i in range(devices)]
    near_in = lax.ppermute(near, seq, to_near)
    far_in = lax.ppermute(chip3, seq, to_far)

    attended = call(
        attention_kernel,
        [(ROWS, WIDTH)],
        (q, k, v, own1, own2, chip3, side, near_in, far_in),
        11,
        [
            (ROWS, WIDTH), (2, ROWS, WIDTH), (2, 256, WIDTH), (2, 128, WIDTH), (2, 1, 128, WIDTH),
            (2, 320, WIDTH), (2, 2, 384, WIDTH), (2, 2, 128, WIDTH),
        ],
        11,
    )

    one = [(i, i ^ 1) for i in range(count)]
    three = [(i, i ^ 3) for i in range(count)]
    half = ROWS // 2
    from_one = lax.ppermute(attended, "head", one)
    from_three = lax.ppermute(attended, "head", three)

    upper = lax.ppermute(from_one[:half], "head", three)
    lower = lax.ppermute(from_three[half:], "head", one)
    return call(
        project_kernel,
        [(ROWS, WIDTH)],
        (attended, from_one, from_three, upper, lower, w_all),
        3,
        [(ROWS, WIDTH)] * 4 + [(count, 2 * z_size, 16, WIDTH)],
        9,
    )


def solution(mesh):
    count = mesh.shape["head"]
    rows = ("x", "z", "core")
    grid = Mesh(mesh.devices.reshape(4, mesh.shape["seq"] // 8, 2, count), rows + ("head",))
    return jax.shard_map(
        on_device,
        mesh=grid,
        in_specs=(P(rows, "head"), P(rows, "head"), P(rows, "head"), P("head", rows)),
        out_specs=P(rows, "head"),
        check_vma=False,
    )
```

```python
import functools

import jax
import jax.numpy as jnp
from jax import lax
from jax.experimental import pallas as pl
from jax.experimental.pallas import tpu as pltpu
from jax.sharding import Mesh, PartitionSpec as P

HEAD_DIM = 128
BLOCK = 128
GROUP = 16
ROWS = 512
WIDTH = 512
HEADS_HERE = WIDTH // HEAD_DIM
SCALE2 = HEAD_DIM ** (-0.5) * 1.4426950408889634
MASKED = -1e30
F32 = jnp.float32
BF16 = jnp.bfloat16
VMEM_LIMIT = 16 * 1024 * 1024

NT = (((1,), (1,)), ((), ()))
NN = (((1,), (0,)), ((), ()))


def dot(a, b, dims=NN):
    return lax.dot_general(a, b, dims, preferred_element_type=F32)


def iota2(shape, dim):
    return lax.broadcasted_iota(jnp.int32, shape, dim)


def pair_average():
    row, col = iota2((64, 128), 0), iota2((64, 128), 1)
    return jnp.where((col >> 1) == 4 * (row & 15) + (row >> 4), 0.5, 0.0).astype(BF16)


def row_order():
    row, col = iota2((128, 128), 0), iota2((128, 128), 1)
    return jnp.where(col == 8 * (row & 15) + (row >> 4), 1.0, 0.0).astype(BF16)


def row_order_back():
    row, col = iota2((128, 128), 0), iota2((128, 128), 1)
    return jnp.where(row == 8 * (col & 15) + (col >> 4), 1.0, 0.0).astype(BF16)


def halve(x):
    wide = x.astype(F32)
    parts = [
        (wide[32 * i : 32 * i + 16] + wide[32 * i + 16 : 32 * i + 32]) * 0.5
        for i in range(x.shape[0] // 32)
    ]
    out = parts[0] if len(parts) == 1 else jnp.concatenate(parts, axis=0)
    return out.astype(BF16)


def double(x):
    parts = []
    for i in range(x.shape[0] // GROUP):
        piece = x[GROUP * i : GROUP * (i + 1)]
        parts += [piece, piece]
    return jnp.concatenate(parts, axis=0)


def start_copies(sems, pairs):
    copies = [
        pltpu.make_async_copy(source, target, sems.at[i]) for i, (source, target) in enumerate(pairs)
    ]
    for copy in copies:
        copy.start()
    return copies


def coarsen_kernel(
    k_hbm, v_hbm, near_ref, side_ref, own3_ref, kv_ref, sems
):
    core = lax.axis_index("core")
    copies = start_copies(sems, ((k_hbm, kv_ref.at[0]), (v_hbm, kv_ref.at[1])))
    average = pair_average()
    for which, copy in enumerate(copies):
        copy.wait()
        own1 = [dot(average, kv_ref[which, 128 * n : 128 * n + 128, :]).astype(BF16) for n in range(4)]
        own2 = [halve(x) for x in own1]
        own3 = [halve(x) for x in own2]
        for n in range(4):
            own3_ref[which, 16 * n : 16 * n + 16, :] = own3[n]

        def edges(pack_ref, to_left):
            first, second, third, fourth = (0, 1, 2, 3) if to_left else (3, 2, 1, 0)
            pack_ref[which, 0:128, :] = kv_ref[which, 128 * first : 128 * first + 128, :]
            pack_ref[which, 128:192, :] = own1[second]
            pack_ref[which, 192:224, :] = own2[third]
            pack_ref[which, 224:256, :] = own2[fourth]

        def both_edges(near_is_left):
            edges(near_ref, near_is_left)
            edges(side_ref, not near_is_left)

        pl.when(core == 0)(functools.partial(both_edges, True))
        pl.when(core != 0)(functools.partial(both_edges, False))

def unpack(pack_ref, which, average, halo_ref, slot, chips_ref=None):
    edge = pack_ref[which, 0:128, :]
    edge1 = dot(average, edge).astype(BF16)
    next1 = pack_ref[which, 128:192, :]
    rest2 = pack_ref[which, 192:256, :]
    edge2, next2 = halve(edge1), halve(next1)
    pieces = ((0, edge), (128, edge1), (192, next1), (256, edge2), (288, next2), (320, rest2))
    for row, x in pieces:
        halo_ref[which, slot, row : row + x.shape[0], :] = x
    if chips_ref is not None:
        for row, x in ((0, halve(edge2)), (16, halve(next2)), (32, halve(rest2))):
            chips_ref[which, slot, row : row + x.shape[0], :] = x


def prepare_kernel(pack_ref, near_own_ref, own3_ref, near_ref, chip_ref):
    average = pair_average()
    for which in range(2):
        near_ref[which, 0:256, :] = near_own_ref[which]
        chip_ref[which, 0:64, :] = own3_ref[which]
        edge2 = halve(dot(average, pack_ref[which, 0:128, :]).astype(BF16))
        next2 = halve(pack_ref[which, 128:192, :])
        other3 = jnp.concatenate([halve(edge2), halve(next2), halve(pack_ref[which, 192:256, :])], axis=0)
        near_ref[which, 256:320, :] = other3
        chip_ref[which, 64:128, :] = other3


def copies_kernel(piece_ref, gate_hbm, out_ref):
    piece = piece_ref[...]
    for i in range(out_ref.shape[0]):
        out_ref[i] = piece


def weigh(query, keys, values, bias_left, bias_right):
    scores = dot(query, jnp.concatenate(keys, axis=0), NT)
    if bias_left is not None:
        scores = jnp.concatenate([scores[:, :128] + bias_left, scores[:, 128:]], axis=1)
    if bias_right is not None:
        scores = jnp.concatenate([scores[:, :256], scores[:, 256:] + bias_right], axis=1)
    top = jnp.max(scores, axis=1, keepdims=True)
    probs = jnp.exp2((scores - top) * SCALE2).astype(BF16)
    wide = jnp.concatenate(values, axis=0)
    wide = jnp.concatenate([wide, jnp.ones_like(wide)], axis=1)
    return top, dot(probs, wide)


def merge(fine, coarse):
    fine_top, fine_sums = fine
    top, sums = double(coarse[0]), double(coarse[1])
    fall = jnp.exp2(-jnp.abs(fine_top - top) * SCALE2)
    higher = fine_top >= top
    fine_factor = jnp.where(higher, 1.0, fall)
    factor = jnp.where(higher, fall, 1.0)
    return jnp.maximum(fine_top, top), fine_sums * fine_factor + sums * factor


def attention_kernel(
    q_hbm, k_hbm, v_hbm, side_hbm, chip_hbm, near_hbm, far_hbm, out_hbm,
    q_ref, kv_ref, side_ref, chip_ref, near_ref, own1_ref, own2_ref, halo_ref, chips_ref, out_ref,
    sems, out_sems,
):
    core = lax.axis_index("core")
    chip = lax.axis_index(("x", "z"))
    last = lax.axis_size(("x", "z")) - 1
    left_chip = jnp.where(chip > 0, 0.0, MASKED).astype(F32)
    right_chip = jnp.where(chip < last, 0.0, MASKED).astype(F32)
    left_bias = jnp.where(core == 0, left_chip, 0.0)
    right_bias = jnp.where(core == 0, 0.0, right_chip)
    average = pair_average()
    order = row_order()
    back = row_order_back()
    side_slot, near_slot = 1 - core, core
    copies = start_copies(
        sems,
        [
            (k_hbm, kv_ref.at[0]),
            (v_hbm, kv_ref.at[1]),
            (side_hbm, side_ref),
            (near_hbm, near_ref),
            (q_hbm, q_ref),
            (chip_hbm, chip_ref),
        ]
        + [(far_hbm.at[i], chips_ref.at[i, side_slot]) for i in range(2)],
    )
    for which in range(2):
        copies[which].wait()
        for n in range(4):
            own1 = dot(average, kv_ref[which, 128 * n : 128 * n + 128, :]).astype(BF16)
            own1_ref[which, 64 * n : 64 * n + 64, :] = own1
            own2_ref[which, 32 * n : 32 * n + 32, :] = halve(own1)
    copies[2].wait()
    copies[3].wait()
    for which in range(2):
        unpack(side_ref, which, average, halo_ref, side_slot)
        unpack(near_ref, which, average, halo_ref, near_slot, chips_ref)
        chips_ref[which, near_slot, 64:128, :] = near_ref[which, 256:320, :]
    for copy in copies[4:]:
        copy.wait()

    def one_head(head, carry):
        lanes = pl.ds(pl.multiple_of(head * HEAD_DIM, HEAD_DIM), HEAD_DIM)
        q0 = [dot(order, q_ref[128 * n : 128 * n + 128, lanes]).astype(BF16) for n in range(4)]
        q1 = [halve(x) for x in q0]
        q2 = [halve(x) for x in q1]
        q3 = [halve(x) for x in q2]

        def piece(own, which, level, index, count):
            if index < 0:
                return halo_ref[which, 0, 128 * level : 128 * level + 128, lanes]
            if index >= count:
                return halo_ref[which, 1, 128 * level : 128 * level + 128, lanes]
            return own(which, index)

        def own_0(which, index):
            return kv_ref[which, 128 * index : 128 * index + 128, lanes]

        def own_1(which, index):
            return own1_ref[which, 128 * index : 128 * index + 128, lanes]

        def own_2(which, index):
            return own2_ref[which, :, lanes]

        def tile(query, own, level, index, count):
            near = [index - 1, index, index + 1]
            return weigh(
                query,
                [piece(own, 0, level, i, count) for i in near],
                [piece(own, 1, level, i, count) for i in near],
                left_bias if index == 0 else None,
                right_bias if index == count - 1 else None,
            )

        at_3 = weigh(
            jnp.concatenate(q3, axis=0),
            [chips_ref[0, 0, :, lanes], chip_ref[0, :, lanes], chips_ref[0, 1, :, lanes]],
            [chips_ref[1, 0, :, lanes], chip_ref[1, :, lanes], chips_ref[1, 1, :, lanes]],
            left_chip,
            right_chip,
        )
        at_2 = merge(tile(jnp.concatenate(q2, axis=0), own_2, 2, 0, 1), at_3)
        for j in range(2):
            half_2 = tuple(x[64 * j : 64 * j + 64] for x in at_2)
            query_1 = jnp.concatenate(q1[2 * j : 2 * j + 2], axis=0)
            at_1 = merge(tile(query_1, own_1, 1, j, 2), half_2)
            for n in (2 * j, 2 * j + 1):
                start = 64 * (n - 2 * j)
                half_1 = tuple(x[start : start + 64] for x in at_1)
                _, sums = merge(tile(q0[n], own_0, 0, n, 4), half_1)
                attended = (sums[:, :128] / sums[:, 128:]).astype(BF16)
                out_ref[128 * n : 128 * n + 128, lanes] = dot(back, attended).astype(BF16)
        return carry

    lax.fori_loop(0, HEADS_HERE, one_head, 0)
    for copy in start_copies(out_sems, [(out_ref, out_hbm.at[i]) for i in range(out_hbm.shape[0])]):
        copy.wait()


def project_kernel(attended_hbm, mine_hbm, other_hbm, out_ref, attended_ref, w_ref, sems):
    core = lax.axis_index("core")
    groups = attended_hbm.shape[0]
    pairs = [(attended_hbm, attended_ref)]
    pairs += [
        (ref.at[g], w_ref.at[g, :, slot])
        for g in range(groups)
        for ref, slot in ((mine_hbm, core), (other_hbm, 1 - core))
    ]
    for copy in start_copies(sems, pairs):
        copy.wait()
    for start in range(0, ROWS, 256):
        total = None
        for g in range(groups):
            weight = w_ref[g].reshape(WIDTH, WIDTH)
            part = dot(attended_ref[g, start : start + 256, :], weight, NT)
            total = part if total is None else total + part
        out_ref[start : start + 256, :] = total.astype(BF16)


def call(kernel, outs, args, work_us, scratch=(), copies=(), specs=None, out_spec=pltpu.VMEM, limit=VMEM_LIMIT):
    shapes = [jax.ShapeDtypeStruct(s, BF16) for s in outs]
    one = len(shapes) == 1
    out_specs = [pl.BlockSpec(memory_space=out_spec)] * len(outs)
    return pl.pallas_call(
        kernel,
        out_shape=shapes[0] if one else shapes,
        in_specs=[pl.BlockSpec(memory_space=s) for s in specs or [pl.ANY] * len(args)],
        out_specs=out_specs[0] if one else out_specs,
        scratch_shapes=[pltpu.VMEM(s, BF16) for s in scratch]
        + [pltpu.SemaphoreType.DMA((n,)) for n in copies],
        cost_estimate=pl.CostEstimate(flops=int(work_us * 1.1e9), bytes_accessed=0, transcendentals=0),
        compiler_params=pltpu.CompilerParams(vmem_limit_bytes=limit),
    )(*args)


def to_all(piece, gate, axis):
    peers = lax.axis_size(axis)
    copies = call(
        copies_kernel,
        [(peers,) + piece.shape],
        (piece, gate),
        1,
        specs=(pltpu.VMEM, pl.ANY),
    )
    return lax.all_to_all(copies, axis, 0, 0, tiled=True)


def on_device(q, k, v, w):
    x_size, z_size = lax.axis_size("x"), lax.axis_size("z")
    count = lax.axis_size("head")
    devices = 2 * x_size * z_size
    seq = ("x", "z", "core")
    swap = [(i, i ^ 1) for i in range(devices)]

    near_own, side_own, own3 = call(
        coarsen_kernel,
        [(2, 256, WIDTH), (2, 256, WIDTH), (2, 64, WIDTH)],
        (k, v),
        3,
        [(2, ROWS, WIDTH)],
        (2,),
    )
    side = lax.ppermute(side_own, seq, swap)
    turn = [(a * count + b, b * count + a) for a in range(x_size) for b in range(count)]
    w_turned = lax.ppermute(w.T, ("x", "head"), turn)

    near, chip3 = call(
        prepare_kernel,
        [(2, 320, WIDTH), (2, 128, WIDTH)],
        (side, near_own, own3),
        2,
        specs=[pltpu.VMEM] * 3,
    )
    to_near = [(i, (i + 1 if i % 2 else i - 1) % devices) for i in range(devices)]
    to_far = [(i, (i - 3 if i % 2 else i + 3) % devices) for i in range(devices)]
    near_in = lax.ppermute(near, seq, to_near)
    far_in = lax.ppermute(chip3, seq, to_far)

    w_z = to_all(w_turned, chip3, "z")

    attended = call(
        attention_kernel,
        [(count, ROWS, WIDTH)],
        (q, k, v, side, chip3, near_in, far_in),
        11,
        [
            (ROWS, WIDTH), (2, ROWS, WIDTH), (2, 256, WIDTH), (2, 128, WIDTH), (2, 320, WIDTH),
            (2, 256, WIDTH), (2, 128, WIDTH), (2, 2, 384, WIDTH), (2, 2, 128, WIDTH), (ROWS, WIDTH),
        ],
        (8, count),
        out_spec=pl.ANY,
    )
    all_attended = lax.all_to_all(attended, "head", 0, 0, tiled=True)

    w_mine = to_all(w_z, attended, "x")
    w_other = lax.ppermute(w_mine, seq, swap)
    return call(
        project_kernel,
        [(ROWS, WIDTH)],
        (all_attended, w_mine, w_other),
        3,
        [(count, ROWS, WIDTH), (count, z_size, 2, 16, WIDTH)],
        (9,),
    )


def solution(mesh):
    count = mesh.shape["head"]
    rows = ("x", "z", "core")
    grid = Mesh(mesh.devices.reshape(4, mesh.shape["seq"] // 8, 2, count), rows + ("head",))
    return jax.shard_map(
        on_device,
        mesh=grid,
        in_specs=(P(rows, "head"), P(rows, "head"), P(rows, "head"), P("head", rows)),
        out_specs=P(rows, "head"),
        check_vma=False,
    )
```

```python
import functools

import jax
import jax.numpy as jnp
from jax import lax
from jax.experimental import pallas as pl
from jax.experimental.pallas import tpu as pltpu
from jax.sharding import Mesh, PartitionSpec as P

HEAD_DIM = 128
BLOCK = 128
GROUP = 16
ROWS = 512
WIDTH = 512
HEADS_HERE = WIDTH // HEAD_DIM
SCALE2 = HEAD_DIM ** (-0.5) * 1.4426950408889634
MASKED = -1e30
F32 = jnp.float32
BF16 = jnp.bfloat16
VMEM_LIMIT = 16 * 1024 * 1024

NT = (((1,), (1,)), ((), ()))
NN = (((1,), (0,)), ((), ()))


def dot(a, b, dims=NN):
    return lax.dot_general(a, b, dims, preferred_element_type=F32)


def iota2(shape, dim):
    return lax.broadcasted_iota(jnp.int32, shape, dim)


def pair_average():
    row, col = iota2((64, 128), 0), iota2((64, 128), 1)
    return jnp.where((col >> 1) == 4 * (row & 15) + (row >> 4), 0.5, 0.0).astype(BF16)


def row_order():
    row, col = iota2((128, 128), 0), iota2((128, 128), 1)
    return jnp.where(col == 8 * (row & 15) + (row >> 4), 1.0, 0.0).astype(BF16)


def row_order_back():
    row, col = iota2((128, 128), 0), iota2((128, 128), 1)
    return jnp.where(row == 8 * (col & 15) + (col >> 4), 1.0, 0.0).astype(BF16)


def halve(x):
    wide = x.astype(F32)
    parts = [
        (wide[32 * i : 32 * i + 16] + wide[32 * i + 16 : 32 * i + 32]) * 0.5
        for i in range(x.shape[0] // 32)
    ]
    out = parts[0] if len(parts) == 1 else jnp.concatenate(parts, axis=0)
    return out.astype(BF16)


def double(x):
    parts = []
    for i in range(x.shape[0] // GROUP):
        piece = x[GROUP * i : GROUP * (i + 1)]
        parts += [piece, piece]
    return jnp.concatenate(parts, axis=0)


def start_copies(sems, pairs):
    copies = [
        pltpu.make_async_copy(source, target, sems.at[i]) for i, (source, target) in enumerate(pairs)
    ]
    for copy in copies:
        copy.start()
    return copies


def coarsen_kernel(
    k_hbm, v_hbm, near_ref, side_ref, own3_ref, kv_ref, sems
):
    core = lax.axis_index("core")
    copies = start_copies(sems, ((k_hbm, kv_ref.at[0]), (v_hbm, kv_ref.at[1])))
    average = pair_average()
    for which, copy in enumerate(copies):
        copy.wait()
        own1 = [dot(average, kv_ref[which, 128 * n : 128 * n + 128, :]).astype(BF16) for n in range(4)]
        own2 = [halve(x) for x in own1]
        own3 = [halve(x) for x in own2]
        for n in range(4):
            own3_ref[which, 16 * n : 16 * n + 16, :] = own3[n]

        def edges(pack_ref, to_left):
            first, second, third, fourth = (0, 1, 2, 3) if to_left else (3, 2, 1, 0)
            pack_ref[which, 0:128, :] = kv_ref[which, 128 * first : 128 * first + 128, :]
            pack_ref[which, 128:192, :] = own1[second]
            pack_ref[which, 192:224, :] = own2[third]
            pack_ref[which, 224:256, :] = own2[fourth]

        def both_edges(near_is_left):
            edges(near_ref, near_is_left)
            edges(side_ref, not near_is_left)

        pl.when(core == 0)(functools.partial(both_edges, True))
        pl.when(core != 0)(functools.partial(both_edges, False))

def unpack(pack_ref, which, average, halo_ref, slot, chips_ref=None):
    edge = pack_ref[which, 0:128, :]
    edge1 = dot(average, edge).astype(BF16)
    next1 = pack_ref[which, 128:192, :]
    rest2 = pack_ref[which, 192:256, :]
    edge2, next2 = halve(edge1), halve(next1)
    pieces = ((0, edge), (128, edge1), (192, next1), (256, edge2), (288, next2), (320, rest2))
    for row, x in pieces:
        halo_ref[which, slot, row : row + x.shape[0], :] = x
    if chips_ref is not None:
        for row, x in ((0, halve(edge2)), (16, halve(next2)), (32, halve(rest2))):
            chips_ref[which, slot, row : row + x.shape[0], :] = x


def prepare_kernel(pack_ref, near_own_ref, own3_ref, near_ref, chip_ref):
    average = pair_average()
    for which in range(2):
        near_ref[which, 0:256, :] = near_own_ref[which]
        chip_ref[which, 0:64, :] = own3_ref[which]
        edge2 = halve(dot(average, pack_ref[which, 0:128, :]).astype(BF16))
        next2 = halve(pack_ref[which, 128:192, :])
        other3 = jnp.concatenate([halve(edge2), halve(next2), halve(pack_ref[which, 192:256, :])], axis=0)
        near_ref[which, 256:320, :] = other3
        chip_ref[which, 64:128, :] = other3


def copies_kernel(piece_ref, gate_hbm, out_ref):
    piece = piece_ref[...]
    for i in range(out_ref.shape[0]):
        out_ref[i] = piece


def gate_kernel(value_hbm, out_hbm):
    pass


def weigh(query, keys, values, bias_left, bias_right):
    scores = dot(query, jnp.concatenate(keys, axis=0), NT)
    if bias_left is not None:
        scores = jnp.concatenate([scores[:, :128] + bias_left, scores[:, 128:]], axis=1)
    if bias_right is not None:
        scores = jnp.concatenate([scores[:, :256], scores[:, 256:] + bias_right], axis=1)
    top = jnp.max(scores, axis=1, keepdims=True)
    probs = jnp.exp2((scores - top) * SCALE2).astype(BF16)
    wide = jnp.concatenate(values, axis=0)
    wide = jnp.concatenate([wide, jnp.ones_like(wide)], axis=1)
    return top, dot(probs, wide)


def merge(fine, coarse):
    fine_top, fine_sums = fine
    top, sums = double(coarse[0]), double(coarse[1])
    fall = jnp.exp2(-jnp.abs(fine_top - top) * SCALE2)
    higher = fine_top >= top
    fine_factor = jnp.where(higher, 1.0, fall)
    factor = jnp.where(higher, fall, 1.0)
    return jnp.maximum(fine_top, top), fine_sums * fine_factor + sums * factor


def attention_kernel(
    q_hbm, k_hbm, v_hbm, side_hbm, chip_hbm, near_hbm, far_hbm, out_hbm,
    q_ref, kv_ref, side_ref, chip_ref, near_ref, own1_ref, own2_ref, halo_ref, chips_ref, out_ref,
    sems, out_sems,
):
    core = lax.axis_index("core")
    chip = lax.axis_index(("x", "z"))
    last = lax.axis_size(("x", "z")) - 1
    left_chip = jnp.where(chip > 0, 0.0, MASKED).astype(F32)
    right_chip = jnp.where(chip < last, 0.0, MASKED).astype(F32)
    left_bias = jnp.where(core == 0, left_chip, 0.0)
    right_bias = jnp.where(core == 0, 0.0, right_chip)
    average = pair_average()
    order = row_order()
    back = row_order_back()
    side_slot, near_slot = 1 - core, core
    copies = start_copies(
        sems,
        [
            (k_hbm, kv_ref.at[0]),
            (v_hbm, kv_ref.at[1]),
            (side_hbm, side_ref),
            (near_hbm, near_ref),
            (q_hbm, q_ref),
            (chip_hbm, chip_ref),
        ]
        + [(far_hbm.at[i], chips_ref.at[i, side_slot]) for i in range(2)],
    )
    for which in range(2):
        copies[which].wait()
        for n in range(4):
            own1 = dot(average, kv_ref[which, 128 * n : 128 * n + 128, :]).astype(BF16)
            own1_ref[which, 64 * n : 64 * n + 64, :] = own1
            own2_ref[which, 32 * n : 32 * n + 32, :] = halve(own1)
    copies[2].wait()
    copies[3].wait()
    for which in range(2):
        unpack(side_ref, which, average, halo_ref, side_slot)
        unpack(near_ref, which, average, halo_ref, near_slot, chips_ref)
        chips_ref[which, near_slot, 64:128, :] = near_ref[which, 256:320, :]
    for copy in copies[4:]:
        copy.wait()

    def one_head(head, carry):
        lanes = pl.ds(pl.multiple_of(head * HEAD_DIM, HEAD_DIM), HEAD_DIM)
        q0 = [dot(order, q_ref[128 * n : 128 * n + 128, lanes]).astype(BF16) for n in range(4)]
        q1 = [halve(x) for x in q0]
        q2 = [halve(x) for x in q1]
        q3 = [halve(x) for x in q2]

        def piece(own, which, level, index, count):
            if index < 0:
                return halo_ref[which, 0, 128 * level : 128 * level + 128, lanes]
            if index >= count:
                return halo_ref[which, 1, 128 * level : 128 * level + 128, lanes]
            return own(which, index)

        def own_0(which, index):
            return kv_ref[which, 128 * index : 128 * index + 128, lanes]

        def own_1(which, index):
            return own1_ref[which, 128 * index : 128 * index + 128, lanes]

        def own_2(which, index):
            return own2_ref[which, :, lanes]

        def tile(query, own, level, index, count):
            near = [index - 1, index, index + 1]
            return weigh(
                query,
                [piece(own, 0, level, i, count) for i in near],
                [piece(own, 1, level, i, count) for i in near],
                left_bias if index == 0 else None,
                right_bias if index == count - 1 else None,
            )

        at_3 = weigh(
            jnp.concatenate(q3, axis=0),
            [chips_ref[0, 0, :, lanes], chip_ref[0, :, lanes], chips_ref[0, 1, :, lanes]],
            [chips_ref[1, 0, :, lanes], chip_ref[1, :, lanes], chips_ref[1, 1, :, lanes]],
            left_chip,
            right_chip,
        )
        at_2 = merge(tile(jnp.concatenate(q2, axis=0), own_2, 2, 0, 1), at_3)
        for j in range(2):
            half_2 = tuple(x[64 * j : 64 * j + 64] for x in at_2)
            query_1 = jnp.concatenate(q1[2 * j : 2 * j + 2], axis=0)
            at_1 = merge(tile(query_1, own_1, 1, j, 2), half_2)
            for n in (2 * j, 2 * j + 1):
                start = 64 * (n - 2 * j)
                half_1 = tuple(x[start : start + 64] for x in at_1)
                _, sums = merge(tile(q0[n], own_0, 0, n, 4), half_1)
                attended = (sums[:, :128] / sums[:, 128:]).astype(BF16)
                out_ref[128 * n : 128 * n + 128, lanes] = dot(back, attended).astype(BF16)
        return carry

    lax.fori_loop(0, HEADS_HERE, one_head, 0)
    for copy in start_copies(out_sems, [(out_ref, out_hbm.at[i]) for i in range(out_hbm.shape[0])]):
        copy.wait()


def project_kernel(attended_hbm, mine_hbm, other_hbm, out_ref, attended_ref, w_ref, sems):
    core = lax.axis_index("core")
    groups = attended_hbm.shape[0]
    pairs = [
        pair
        for g in range(groups)
        for pair in (
            (mine_hbm.at[g], w_ref.at[g, :, core]),
            (other_hbm.at[g], w_ref.at[g, :, 1 - core]),
            (attended_hbm.at[g], attended_ref.at[g]),
        )
    ]
    copies = start_copies(sems, pairs)
    for start in range(0, ROWS, 256):
        total = None
        for g in range(groups):
            if start == 0:
                for copy in copies[3 * g : 3 * g + 3]:
                    copy.wait()
            weight = w_ref[g].reshape(WIDTH, WIDTH)
            part = dot(attended_ref[g, start : start + 256, :], weight, NT)
            total = part if total is None else total + part
        out_ref[start : start + 256, :] = total.astype(BF16)


def call(kernel, outs, args, work_us, scratch=(), copies=(), specs=None, out_spec=pltpu.VMEM, limit=VMEM_LIMIT, aliases=None):
    shapes = [jax.ShapeDtypeStruct(s, BF16) for s in outs]
    one = len(shapes) == 1
    out_specs = [pl.BlockSpec(memory_space=out_spec)] * len(outs)
    return pl.pallas_call(
        kernel,
        out_shape=shapes[0] if one else shapes,
        in_specs=[pl.BlockSpec(memory_space=s) for s in specs or [pl.ANY] * len(args)],
        out_specs=out_specs[0] if one else out_specs,
        scratch_shapes=[pltpu.VMEM(s, BF16) for s in scratch]
        + [pltpu.SemaphoreType.DMA((n,)) for n in copies],
        input_output_aliases=aliases or {},
        cost_estimate=pl.CostEstimate(flops=int(work_us * 1.1e9), bytes_accessed=0, transcendentals=0),
        compiler_params=pltpu.CompilerParams(vmem_limit_bytes=limit),
    )(*args)


def to_all(piece, gate, axis):
    peers = lax.axis_size(axis)
    copies = call(
        copies_kernel,
        [(peers,) + piece.shape],
        (piece, gate),
        1,
        specs=(pltpu.VMEM, pl.ANY),
    )
    return lax.all_to_all(copies, axis, 0, 0, tiled=True)


def on_device(q, k, v, w):
    x_size, z_size = lax.axis_size("x"), lax.axis_size("z")
    count = lax.axis_size("head")
    devices = 2 * x_size * z_size
    seq = ("x", "z", "core")
    swap = [(i, i ^ 1) for i in range(devices)]

    near_own, side_own, own3 = call(
        coarsen_kernel,
        [(2, 256, WIDTH), (2, 256, WIDTH), (2, 64, WIDTH)],
        (k, v),
        3,
        [(2, ROWS, WIDTH)],
        (2,),
    )
    side = lax.ppermute(side_own, seq, swap)
    turn = [(a * count + b, b * count + a) for a in range(x_size) for b in range(count)]
    w_turned = lax.ppermute(w.T, ("x", "head"), turn)

    near, chip3 = call(
        prepare_kernel,
        [(2, 320, WIDTH), (2, 128, WIDTH)],
        (side, near_own, own3),
        2,
        specs=[pltpu.VMEM] * 3,
    )
    to_near = [(i, (i + 1 if i % 2 else i - 1) % devices) for i in range(devices)]
    to_far = [(i, (i - 3 if i % 2 else i + 3) % devices) for i in range(devices)]
    near_in = lax.ppermute(near, seq, to_near)
    far_in = lax.ppermute(chip3, seq, to_far)

    w_z = to_all(w_turned, chip3, "z")

    attended = call(
        attention_kernel,
        [(count, ROWS, WIDTH)],
        (q, k, v, side, chip3, near_in, far_in),
        11,
        [
            (ROWS, WIDTH), (2, ROWS, WIDTH), (2, 256, WIDTH), (2, 128, WIDTH), (2, 320, WIDTH),
            (2, 256, WIDTH), (2, 128, WIDTH), (2, 2, 384, WIDTH), (2, 2, 128, WIDTH), (ROWS, WIDTH),
        ],
        (8, count),
        out_spec=pl.ANY,
    )
    all_attended = lax.all_to_all(attended, "head", 0, 0, tiled=True)
    all_attended = call(gate_kernel, [attended.shape], (all_attended,), 3, out_spec=pl.ANY, aliases={0: 0})

    w_mine = to_all(w_z, attended, "x")
    w_other = lax.ppermute(w_mine, seq, swap)
    return call(
        project_kernel,
        [(ROWS, WIDTH)],
        (all_attended, w_mine, w_other),
        3,
        [(count, ROWS, WIDTH), (count, z_size, 2, 16, WIDTH)],
        (3 * count,),
    )


def solution(mesh):
    count = mesh.shape["head"]
    rows = ("x", "z", "core")
    grid = Mesh(mesh.devices.reshape(4, mesh.shape["seq"] // 8, 2, count), rows + ("head",))
    return jax.shard_map(
        on_device,
        mesh=grid,
        in_specs=(P(rows, "head"), P(rows, "head"), P(rows, "head"), P("head", rows)),
        out_specs=P(rows, "head"),
        check_vma=False,
    )
```

```python
import functools

import jax
import jax.numpy as jnp
from jax import lax
from jax.experimental import pallas as pl
from jax.experimental.pallas import tpu as pltpu
from jax.sharding import Mesh, PartitionSpec as P

HEAD_DIM = 128
BLOCK = 128
GROUP = 16
ROWS = 512
WIDTH = 512
HEADS_HERE = WIDTH // HEAD_DIM
SCALE2 = HEAD_DIM ** (-0.5) * 1.4426950408889634
MASKED = -1e30
F32 = jnp.float32
BF16 = jnp.bfloat16
VMEM_LIMIT = 16 * 1024 * 1024

NT = (((1,), (1,)), ((), ()))
NN = (((1,), (0,)), ((), ()))


def dot(a, b, dims=NN):
    return lax.dot_general(a, b, dims, preferred_element_type=F32)


def iota2(shape, dim):
    return lax.broadcasted_iota(jnp.int32, shape, dim)


def pair_average():
    row, col = iota2((64, 128), 0), iota2((64, 128), 1)
    return jnp.where((col >> 1) == 4 * (row & 15) + (row >> 4), 0.5, 0.0).astype(BF16)


def row_order():
    row, col = iota2((128, 128), 0), iota2((128, 128), 1)
    return jnp.where(col == 8 * (row & 15) + (row >> 4), 1.0, 0.0).astype(BF16)


def row_order_back():
    row, col = iota2((128, 128), 0), iota2((128, 128), 1)
    return jnp.where(row == 8 * (col & 15) + (col >> 4), 1.0, 0.0).astype(BF16)


def halve(x):
    wide = x.astype(F32)
    parts = [
        (wide[32 * i : 32 * i + 16] + wide[32 * i + 16 : 32 * i + 32]) * 0.5
        for i in range(x.shape[0] // 32)
    ]
    out = parts[0] if len(parts) == 1 else jnp.concatenate(parts, axis=0)
    return out.astype(BF16)


def double(x):
    parts = []
    for i in range(x.shape[0] // GROUP):
        piece = x[GROUP * i : GROUP * (i + 1)]
        parts += [piece, piece]
    return jnp.concatenate(parts, axis=0)


def start_copies(sems, pairs):
    copies = [
        pltpu.make_async_copy(source, target, sems.at[i]) for i, (source, target) in enumerate(pairs)
    ]
    for copy in copies:
        copy.start()
    return copies


def coarsen_kernel(
    k_hbm, v_hbm, near_ref, side_ref, own3_ref, kv_ref, sems
):
    core = lax.axis_index("core")
    copies = start_copies(sems, ((k_hbm, kv_ref.at[0]), (v_hbm, kv_ref.at[1])))
    average = pair_average()
    for which, copy in enumerate(copies):
        copy.wait()
        own1 = [dot(average, kv_ref[which, 128 * n : 128 * n + 128, :]).astype(BF16) for n in range(4)]
        own2 = [halve(x) for x in own1]
        own3 = [halve(x) for x in own2]
        for n in range(4):
            own3_ref[which, 16 * n : 16 * n + 16, :] = own3[n]

        def edges(pack_ref, to_left):
            first, second, third, fourth = (0, 1, 2, 3) if to_left else (3, 2, 1, 0)
            pack_ref[which, 0:128, :] = kv_ref[which, 128 * first : 128 * first + 128, :]
            pack_ref[which, 128:192, :] = own1[second]
            pack_ref[which, 192:224, :] = own2[third]
            pack_ref[which, 224:256, :] = own2[fourth]

        def both_edges(near_is_left):
            edges(near_ref, near_is_left)
            edges(side_ref, not near_is_left)

        pl.when(core == 0)(functools.partial(both_edges, True))
        pl.when(core != 0)(functools.partial(both_edges, False))

def unpack(pack_ref, which, average, halo_ref, slot, chips_ref=None):
    edge = pack_ref[which, 0:128, :]
    edge1 = dot(average, edge).astype(BF16)
    next1 = pack_ref[which, 128:192, :]
    rest2 = pack_ref[which, 192:256, :]
    edge2, next2 = halve(edge1), halve(next1)
    pieces = ((0, edge), (128, edge1), (192, next1), (256, edge2), (288, next2), (320, rest2))
    for row, x in pieces:
        halo_ref[which, slot, row : row + x.shape[0], :] = x
    if chips_ref is not None:
        for row, x in ((0, halve(edge2)), (16, halve(next2)), (32, halve(rest2))):
            chips_ref[which, slot, row : row + x.shape[0], :] = x


def prepare_kernel(pack_ref, near_own_ref, own3_ref, near_ref, chip_ref):
    average = pair_average()
    for which in range(2):
        near_ref[which, 0:256, :] = near_own_ref[which]
        chip_ref[which, 0:64, :] = own3_ref[which]
        edge2 = halve(dot(average, pack_ref[which, 0:128, :]).astype(BF16))
        next2 = halve(pack_ref[which, 128:192, :])
        other3 = jnp.concatenate([halve(edge2), halve(next2), halve(pack_ref[which, 192:256, :])], axis=0)
        near_ref[which, 256:320, :] = other3
        chip_ref[which, 64:128, :] = other3


def copies_kernel(piece_ref, gate_hbm, out_ref):
    piece = piece_ref[...]
    for i in range(out_ref.shape[0]):
        out_ref[i] = piece


def gate_kernel(upper_hbm, lower_hbm, upper_out_hbm, lower_out_hbm):
    pass


def stack_kernel(a_hbm, b_hbm, c_hbm, d_hbm, gate_1_hbm, gate_3_hbm, out_hbm, sems):
    sources = (a_hbm, b_hbm, c_hbm, d_hbm)
    for copy in start_copies(sems, [(x, out_hbm.at[i]) for i, x in enumerate(sources)]):
        copy.wait()


def weigh(query, keys, values, bias_left, bias_right):
    scores = dot(query, jnp.concatenate(keys, axis=0), NT)
    if bias_left is not None:
        scores = jnp.concatenate([scores[:, :128] + bias_left, scores[:, 128:]], axis=1)
    if bias_right is not None:
        scores = jnp.concatenate([scores[:, :256], scores[:, 256:] + bias_right], axis=1)
    top = jnp.max(scores, axis=1, keepdims=True)
    probs = jnp.exp2((scores - top) * SCALE2).astype(BF16)
    wide = jnp.concatenate(values, axis=0)
    wide = jnp.concatenate([wide, jnp.ones_like(wide)], axis=1)
    return top, dot(probs, wide)


def merge(fine, coarse):
    fine_top, fine_sums = fine
    top, sums = double(coarse[0]), double(coarse[1])
    fall = jnp.exp2(-jnp.abs(fine_top - top) * SCALE2)
    higher = fine_top >= top
    fine_factor = jnp.where(higher, 1.0, fall)
    factor = jnp.where(higher, fall, 1.0)
    return jnp.maximum(fine_top, top), fine_sums * fine_factor + sums * factor


def attention_kernel(
    q_hbm, k_hbm, v_hbm, side_hbm, chip_hbm, near_hbm, far_hbm, out_ref,
    q_ref, kv_ref, side_ref, chip_ref, near_ref, own1_ref, own2_ref, halo_ref, chips_ref, sems,
):
    core = lax.axis_index("core")
    chip = lax.axis_index(("x", "z"))
    last = lax.axis_size(("x", "z")) - 1
    left_chip = jnp.where(chip > 0, 0.0, MASKED).astype(F32)
    right_chip = jnp.where(chip < last, 0.0, MASKED).astype(F32)
    left_bias = jnp.where(core == 0, left_chip, 0.0)
    right_bias = jnp.where(core == 0, 0.0, right_chip)
    average = pair_average()
    order = row_order()
    back = row_order_back()
    side_slot, near_slot = 1 - core, core
    copies = start_copies(
        sems,
        [
            (k_hbm, kv_ref.at[0]),
            (v_hbm, kv_ref.at[1]),
            (side_hbm, side_ref),
            (near_hbm, near_ref),
            (q_hbm, q_ref),
            (chip_hbm, chip_ref),
        ]
        + [(far_hbm.at[i], chips_ref.at[i, side_slot]) for i in range(2)],
    )
    for which in range(2):
        copies[which].wait()
        for n in range(4):
            own1 = dot(average, kv_ref[which, 128 * n : 128 * n + 128, :]).astype(BF16)
            own1_ref[which, 64 * n : 64 * n + 64, :] = own1
            own2_ref[which, 32 * n : 32 * n + 32, :] = halve(own1)
    copies[2].wait()
    copies[3].wait()
    for which in range(2):
        unpack(side_ref, which, average, halo_ref, side_slot)
        unpack(near_ref, which, average, halo_ref, near_slot, chips_ref)
        chips_ref[which, near_slot, 64:128, :] = near_ref[which, 256:320, :]
    for copy in copies[4:]:
        copy.wait()

    def one_head(head, carry):
        lanes = pl.ds(pl.multiple_of(head * HEAD_DIM, HEAD_DIM), HEAD_DIM)
        q0 = [dot(order, q_ref[128 * n : 128 * n + 128, lanes]).astype(BF16) for n in range(4)]
        q1 = [halve(x) for x in q0]
        q2 = [halve(x) for x in q1]
        q3 = [halve(x) for x in q2]

        def piece(own, which, level, index, count):
            if index < 0:
                return halo_ref[which, 0, 128 * level : 128 * level + 128, lanes]
            if index >= count:
                return halo_ref[which, 1, 128 * level : 128 * level + 128, lanes]
            return own(which, index)

        def own_0(which, index):
            return kv_ref[which, 128 * index : 128 * index + 128, lanes]

        def own_1(which, index):
            return own1_ref[which, 128 * index : 128 * index + 128, lanes]

        def own_2(which, index):
            return own2_ref[which, :, lanes]

        def tile(query, own, level, index, count):
            near = [index - 1, index, index + 1]
            return weigh(
                query,
                [piece(own, 0, level, i, count) for i in near],
                [piece(own, 1, level, i, count) for i in near],
                left_bias if index == 0 else None,
                right_bias if index == count - 1 else None,
            )

        at_3 = weigh(
            jnp.concatenate(q3, axis=0),
            [chips_ref[0, 0, :, lanes], chip_ref[0, :, lanes], chips_ref[0, 1, :, lanes]],
            [chips_ref[1, 0, :, lanes], chip_ref[1, :, lanes], chips_ref[1, 1, :, lanes]],
            left_chip,
            right_chip,
        )
        at_2 = merge(tile(jnp.concatenate(q2, axis=0), own_2, 2, 0, 1), at_3)
        for j in range(2):
            half_2 = tuple(x[64 * j : 64 * j + 64] for x in at_2)
            query_1 = jnp.concatenate(q1[2 * j : 2 * j + 2], axis=0)
            at_1 = merge(tile(query_1, own_1, 1, j, 2), half_2)
            for n in (2 * j, 2 * j + 1):
                start = 64 * (n - 2 * j)
                half_1 = tuple(x[start : start + 64] for x in at_1)
                _, sums = merge(tile(q0[n], own_0, 0, n, 4), half_1)
                attended = (sums[:, :128] / sums[:, 128:]).astype(BF16)
                out_ref[128 * n : 128 * n + 128, lanes] = dot(back, attended).astype(BF16)
        return carry

    lax.fori_loop(0, HEADS_HERE, one_head, 0)


def project_kernel(
    own_hbm, one_hbm, three_hbm, upper_hbm, lower_hbm, mine_hbm, other_hbm,
    out_ref, own_ref, one_ref, three_ref, across_ref, w_ref, sems,
):
    core = lax.axis_index("core")
    twist = lax.axis_index("head") ^ lax.axis_index("x")
    half = ROWS // 2
    order = (0, 1, 3, 2)
    parts = (own_ref, one_ref, three_ref, across_ref)
    stages = [[], [], [], []]
    for stage, i in zip(stages, order):
        for ref, slot in ((mine_hbm, core), (other_hbm, 1 - core)):
            stage.append((ref.at[twist ^ i], w_ref.at[i, :, slot]))
    stages[0].append((own_hbm, own_ref))
    stages[1].append((one_hbm, one_ref))
    stages[2].append((three_hbm, three_ref))
    stages[3].append((upper_hbm, across_ref.at[pl.ds(0, half)]))
    stages[3].append((lower_hbm, across_ref.at[pl.ds(half, half)]))
    copies = start_copies(sems, sum(stages, []))
    for start in (0, half):
        rows = slice(start, start + half)
        total = None
        for at, (ref, i) in enumerate(zip(parts, order)):
            if start == 0:
                for copy in copies[3 * at : 3 * at + len(stages[at])]:
                    copy.wait()
            part = dot(ref[rows, :], w_ref[i].reshape(WIDTH, WIDTH), NT)
            total = part if total is None else total + part
        out_ref[rows, :] = total.astype(BF16)


def call(kernel, outs, args, work_us, scratch=(), copies=(), specs=None, out_spec=pltpu.VMEM, limit=VMEM_LIMIT, aliases=None):
    shapes = [jax.ShapeDtypeStruct(s, BF16) for s in outs]
    one = len(shapes) == 1
    out_specs = [pl.BlockSpec(memory_space=out_spec)] * len(outs)
    return pl.pallas_call(
        kernel,
        out_shape=shapes[0] if one else shapes,
        in_specs=[pl.BlockSpec(memory_space=s) for s in specs or [pl.ANY] * len(args)],
        out_specs=out_specs[0] if one else out_specs,
        scratch_shapes=[pltpu.VMEM(s, BF16) for s in scratch]
        + [pltpu.SemaphoreType.DMA((n,)) for n in copies],
        input_output_aliases=aliases or {},
        cost_estimate=pl.CostEstimate(flops=int(work_us * 1.1e9), bytes_accessed=0, transcendentals=0),
        compiler_params=pltpu.CompilerParams(vmem_limit_bytes=limit),
    )(*args)


def to_all(piece, gate, axis):
    peers = lax.axis_size(axis)
    copies = call(
        copies_kernel,
        [(peers,) + piece.shape],
        (piece, gate),
        1,
        specs=(pltpu.VMEM, pl.ANY),
    )
    return lax.all_to_all(copies, axis, 0, 0, tiled=True)


def on_device(q, k, v, w):
    x_size, z_size = lax.axis_size("x"), lax.axis_size("z")
    count = lax.axis_size("head")
    devices = 2 * x_size * z_size
    seq = ("x", "z", "core")
    swap = [(i, i ^ 1) for i in range(devices)]

    near_own, side_own, own3 = call(
        coarsen_kernel,
        [(2, 256, WIDTH), (2, 256, WIDTH), (2, 64, WIDTH)],
        (k, v),
        3,
        [(2, ROWS, WIDTH)],
        (2,),
    )
    side = lax.ppermute(side_own, seq, swap)
    turn = [(a * count + b, b * count + a) for a in range(x_size) for b in range(count)]
    w_turned = lax.ppermute(w.T, ("x", "head"), turn)

    near, chip3 = call(
        prepare_kernel,
        [(2, 320, WIDTH), (2, 128, WIDTH)],
        (side, near_own, own3),
        2,
        specs=[pltpu.VMEM] * 3,
    )
    to_near = [(i, (i + 1 if i % 2 else i - 1) % devices) for i in range(devices)]
    to_far = [(i, (i - 3 if i % 2 else i + 3) % devices) for i in range(devices)]
    near_in = lax.ppermute(near, seq, to_near)
    far_in = lax.ppermute(chip3, seq, to_far)

    w_z = to_all(w_turned, chip3, "z")

    attended = call(
        attention_kernel,
        [(ROWS, WIDTH)],
        (q, k, v, side, chip3, near_in, far_in),
        11,
        [
            (ROWS, WIDTH), (2, ROWS, WIDTH), (2, 256, WIDTH), (2, 128, WIDTH), (2, 320, WIDTH),
            (2, 256, WIDTH), (2, 128, WIDTH), (2, 2, 384, WIDTH), (2, 2, 128, WIDTH),
        ],
        (8,),
    )
    one = [(i, i ^ 1) for i in range(count)]
    three = [(i, i ^ 3) for i in range(count)]
    half = ROWS // 2
    from_one = lax.ppermute(attended, "head", one)
    from_three = lax.ppermute(attended, "head", three)

    w_x = [w_z] + [
        lax.ppermute(w_z, "x", [(i, i ^ j) for i in range(x_size)]) for j in range(1, x_size)
    ]
    w_mine = call(
        stack_kernel, [(x_size,) + w_z.shape], w_x + [from_one, from_three], 1, (), (x_size,), out_spec=pl.ANY
    )
    w_other = lax.ppermute(w_mine, seq, swap)

    upper = lax.ppermute(from_one[:half], "head", three)
    lower = lax.ppermute(from_three[half:], "head", one)
    upper, lower = call(
        gate_kernel, [upper.shape] * 2, (upper, lower), 8, out_spec=pl.ANY, aliases={0: 0, 1: 1}
    )
    return call(
        project_kernel,
        [(ROWS, WIDTH)],
        (attended, from_one, from_three, upper, lower, w_mine, w_other),
        3,
        [(ROWS, WIDTH)] * 4 + [(count, z_size, 2, 16, WIDTH)],
        (13,),
    )


def solution(mesh):
    count = mesh.shape["head"]
    rows = ("x", "z", "core")
    grid = Mesh(mesh.devices.reshape(4, mesh.shape["seq"] // 8, 2, count), rows + ("head",))
    return jax.shard_map(
        on_device,
        mesh=grid,
        in_specs=(P(rows, "head"), P(rows, "head"), P(rows, "head"), P("head", rows)),
        out_specs=P(rows, "head"),
        check_vma=False,
    )
```

```python
import functools

import jax
import jax.numpy as jnp
from jax import lax
from jax.experimental import pallas as pl
from jax.experimental.pallas import tpu as pltpu
from jax.sharding import Mesh, PartitionSpec as P

HEAD_DIM = 128
BLOCK = 128
GROUP = 16
ROWS = 512
WIDTH = 512
HEADS_HERE = WIDTH // HEAD_DIM
SCALE2 = HEAD_DIM ** (-0.5) * 1.4426950408889634
MASKED = -1e30
F32 = jnp.float32
BF16 = jnp.bfloat16
VMEM_LIMIT = 16 * 1024 * 1024

NT = (((1,), (1,)), ((), ()))
NN = (((1,), (0,)), ((), ()))


def dot(a, b, dims=NN):
    return lax.dot_general(a, b, dims, preferred_element_type=F32)


def iota2(shape, dim):
    return lax.broadcasted_iota(jnp.int32, shape, dim)


def pair_average():
    row, col = iota2((64, 128), 0), iota2((64, 128), 1)
    return jnp.where((col >> 1) == 4 * (row & 15) + (row >> 4), 0.5, 0.0).astype(BF16)


def row_order():
    row, col = iota2((128, 128), 0), iota2((128, 128), 1)
    return jnp.where(col == 8 * (row & 15) + (row >> 4), 1.0, 0.0).astype(BF16)


def row_order_back():
    row, col = iota2((128, 128), 0), iota2((128, 128), 1)
    return jnp.where(row == 8 * (col & 15) + (col >> 4), 1.0, 0.0).astype(BF16)


def halve(x):
    wide = x.astype(F32)
    parts = [
        (wide[32 * i : 32 * i + 16] + wide[32 * i + 16 : 32 * i + 32]) * 0.5
        for i in range(x.shape[0] // 32)
    ]
    out = parts[0] if len(parts) == 1 else jnp.concatenate(parts, axis=0)
    return out.astype(BF16)


def double(x):
    parts = []
    for i in range(x.shape[0] // GROUP):
        piece = x[GROUP * i : GROUP * (i + 1)]
        parts += [piece, piece]
    return jnp.concatenate(parts, axis=0)


def start_copies(sems, pairs):
    copies = [
        pltpu.make_async_copy(source, target, sems.at[i]) for i, (source, target) in enumerate(pairs)
    ]
    for copy in copies:
        copy.start()
    return copies


def coarsen_kernel(
    k_hbm, v_hbm, near_ref, side_ref, own3_ref, kv_ref, sems
):
    core = lax.axis_index("core")
    copies = start_copies(sems, ((k_hbm, kv_ref.at[0]), (v_hbm, kv_ref.at[1])))
    average = pair_average()
    for which, copy in enumerate(copies):
        copy.wait()
        own1 = [dot(average, kv_ref[which, 128 * n : 128 * n + 128, :]).astype(BF16) for n in range(4)]
        own2 = [halve(x) for x in own1]
        own3 = [halve(x) for x in own2]
        for n in range(4):
            own3_ref[which, 16 * n : 16 * n + 16, :] = own3[n]

        def edges(pack_ref, to_left):
            first, second, third, fourth = (0, 1, 2, 3) if to_left else (3, 2, 1, 0)
            pack_ref[which, 0:128, :] = kv_ref[which, 128 * first : 128 * first + 128, :]
            pack_ref[which, 128:192, :] = own1[second]
            pack_ref[which, 192:224, :] = own2[third]
            pack_ref[which, 224:256, :] = own2[fourth]

        def both_edges(near_is_left):
            edges(near_ref, near_is_left)
            edges(side_ref, not near_is_left)

        pl.when(core == 0)(functools.partial(both_edges, True))
        pl.when(core != 0)(functools.partial(both_edges, False))

def unpack(pack_ref, which, average, halo_ref, slot, chips_ref=None):
    edge = pack_ref[which, 0:128, :]
    edge1 = dot(average, edge).astype(BF16)
    next1 = pack_ref[which, 128:192, :]
    rest2 = pack_ref[which, 192:256, :]
    edge2, next2 = halve(edge1), halve(next1)
    pieces = ((0, edge), (128, edge1), (192, next1), (256, edge2), (288, next2), (320, rest2))
    for row, x in pieces:
        halo_ref[which, slot, row : row + x.shape[0], :] = x
    if chips_ref is not None:
        for row, x in ((0, halve(edge2)), (16, halve(next2)), (32, halve(rest2))):
            chips_ref[which, slot, row : row + x.shape[0], :] = x


def prepare_kernel(pack_ref, near_own_ref, own3_ref, near_ref, chip_ref):
    average = pair_average()
    for which in range(2):
        near_ref[which, 0:256, :] = near_own_ref[which]
        chip_ref[which, 0:64, :] = own3_ref[which]
        edge2 = halve(dot(average, pack_ref[which, 0:128, :]).astype(BF16))
        next2 = halve(pack_ref[which, 128:192, :])
        other3 = jnp.concatenate([halve(edge2), halve(next2), halve(pack_ref[which, 192:256, :])], axis=0)
        near_ref[which, 256:320, :] = other3
        chip_ref[which, 64:128, :] = other3


def copies_kernel(piece_ref, gate_hbm, out_ref):
    piece = piece_ref[...]
    for i in range(out_ref.shape[0]):
        out_ref[i] = piece


def gate_kernel(upper_hbm, lower_hbm, upper_out_hbm, lower_out_hbm):
    pass


def stack_kernel(a_hbm, b_hbm, c_hbm, d_hbm, gate_1_hbm, gate_3_hbm, out_hbm, sems):
    sources = (a_hbm, b_hbm, c_hbm, d_hbm)
    for copy in start_copies(sems, [(x, out_hbm.at[i]) for i, x in enumerate(sources)]):
        copy.wait()


def weigh(query, keys, values, bias_left, bias_right):
    scores = dot(query, jnp.concatenate(keys, axis=0), NT)
    if bias_left is not None:
        scores = jnp.concatenate([scores[:, :128] + bias_left, scores[:, 128:]], axis=1)
    if bias_right is not None:
        scores = jnp.concatenate([scores[:, :256], scores[:, 256:] + bias_right], axis=1)
    top = jnp.max(scores, axis=1, keepdims=True)
    probs = jnp.exp2((scores - top) * SCALE2).astype(BF16)
    wide = jnp.concatenate(values, axis=0)
    wide = jnp.concatenate([wide, jnp.ones_like(wide)], axis=1)
    return top, dot(probs, wide)


def merge(fine, coarse):
    fine_top, fine_sums = fine
    top, sums = double(coarse[0]), double(coarse[1])
    fall = jnp.exp2(-jnp.abs(fine_top - top) * SCALE2)
    higher = fine_top >= top
    fine_factor = jnp.where(higher, 1.0, fall)
    factor = jnp.where(higher, fall, 1.0)
    return jnp.maximum(fine_top, top), fine_sums * fine_factor + sums * factor


def attention_kernel(
    q_ref, k_ref, v_ref, side_ref, chip_ref, near_ref, far_ref, out_ref,
    own1_ref, own2_ref, halo_ref, chips_ref,
):
    core = lax.axis_index("core")
    chip = lax.axis_index(("x", "z"))
    last = lax.axis_size(("x", "z")) - 1
    left_chip = jnp.where(chip > 0, 0.0, MASKED).astype(F32)
    right_chip = jnp.where(chip < last, 0.0, MASKED).astype(F32)
    left_bias = jnp.where(core == 0, left_chip, 0.0)
    right_bias = jnp.where(core == 0, 0.0, right_chip)
    average = pair_average()
    order = row_order()
    back = row_order_back()
    side_slot, near_slot = 1 - core, core
    for which, ref in enumerate((k_ref, v_ref)):
        for n in range(4):
            own1 = dot(average, ref[128 * n : 128 * n + 128, :]).astype(BF16)
            own1_ref[which, 64 * n : 64 * n + 64, :] = own1
            own2_ref[which, 32 * n : 32 * n + 32, :] = halve(own1)
        unpack(side_ref, which, average, halo_ref, side_slot)
        unpack(near_ref, which, average, halo_ref, near_slot, chips_ref)
        chips_ref[which, near_slot, 64:128, :] = near_ref[which, 256:320, :]
        chips_ref[which, side_slot] = far_ref[which]

    def one_head(head, carry):
        lanes = pl.ds(pl.multiple_of(head * HEAD_DIM, HEAD_DIM), HEAD_DIM)
        q0 = [dot(order, q_ref[128 * n : 128 * n + 128, lanes]).astype(BF16) for n in range(4)]
        q1 = [halve(x) for x in q0]
        q2 = [halve(x) for x in q1]
        q3 = [halve(x) for x in q2]

        def piece(own, which, level, index, count):
            if index < 0:
                return halo_ref[which, 0, 128 * level : 128 * level + 128, lanes]
            if index >= count:
                return halo_ref[which, 1, 128 * level : 128 * level + 128, lanes]
            return own(which, index)

        def own_0(which, index):
            return (k_ref, v_ref)[which][128 * index : 128 * index + 128, lanes]

        def own_1(which, index):
            return own1_ref[which, 128 * index : 128 * index + 128, lanes]

        def own_2(which, index):
            return own2_ref[which, :, lanes]

        def tile(query, own, level, index, count):
            near = [index - 1, index, index + 1]
            return weigh(
                query,
                [piece(own, 0, level, i, count) for i in near],
                [piece(own, 1, level, i, count) for i in near],
                left_bias if index == 0 else None,
                right_bias if index == count - 1 else None,
            )

        at_3 = weigh(
            jnp.concatenate(q3, axis=0),
            [chips_ref[0, 0, :, lanes], chip_ref[0, :, lanes], chips_ref[0, 1, :, lanes]],
            [chips_ref[1, 0, :, lanes], chip_ref[1, :, lanes], chips_ref[1, 1, :, lanes]],
            left_chip,
            right_chip,
        )
        at_2 = merge(tile(jnp.concatenate(q2, axis=0), own_2, 2, 0, 1), at_3)
        for j in range(2):
            half_2 = tuple(x[64 * j : 64 * j + 64] for x in at_2)
            query_1 = jnp.concatenate(q1[2 * j : 2 * j + 2], axis=0)
            at_1 = merge(tile(query_1, own_1, 1, j, 2), half_2)
            for n in (2 * j, 2 * j + 1):
                start = 64 * (n - 2 * j)
                half_1 = tuple(x[start : start + 64] for x in at_1)
                _, sums = merge(tile(q0[n], own_0, 0, n, 4), half_1)
                attended = (sums[:, :128] / sums[:, 128:]).astype(BF16)
                out_ref[128 * n : 128 * n + 128, lanes] = dot(back, attended).astype(BF16)
        return carry

    lax.fori_loop(0, HEADS_HERE, one_head, 0, unroll=2)


def project_kernel(
    own_ref, one_ref, three_ref, upper_ref, lower_ref, mine_ref, other_ref, out_ref
):
    core = lax.axis_index("core")
    twist = lax.axis_index("head") ^ lax.axis_index("x")
    half = ROWS // 2

    def run(first, second):
        def weight(i):
            return jnp.concatenate(
                [ref[twist ^ i, z] for z in range(first.shape[1]) for ref in (first, second)], axis=0
            )

        weights = [weight(i) for i in range(4)]
        for start, across in ((0, upper_ref), (half, lower_ref)):
            rows = slice(start, start + half)
            total = dot(own_ref[rows, :], weights[0], NT)
            total += dot(one_ref[rows, :], weights[1], NT)
            total += dot(three_ref[rows, :], weights[3], NT)
            total += dot(across[...], weights[2], NT)
            out_ref[rows, :] = total.astype(BF16)

    pl.when(core == 0)(functools.partial(run, mine_ref, other_ref))
    pl.when(core != 0)(functools.partial(run, other_ref, mine_ref))


def call(kernel, outs, args, work_us, scratch=(), copies=(), specs=None, out_spec=pltpu.VMEM, limit=VMEM_LIMIT, aliases=None):
    shapes = [jax.ShapeDtypeStruct(s, BF16) for s in outs]
    one = len(shapes) == 1
    out_specs = [pl.BlockSpec(memory_space=out_spec)] * len(outs)
    return pl.pallas_call(
        kernel,
        out_shape=shapes[0] if one else shapes,
        in_specs=[pl.BlockSpec(memory_space=s) for s in specs or [pl.ANY] * len(args)],
        out_specs=out_specs[0] if one else out_specs,
        scratch_shapes=[pltpu.VMEM(s, BF16) for s in scratch]
        + [pltpu.SemaphoreType.DMA((n,)) for n in copies],
        input_output_aliases=aliases or {},
        cost_estimate=pl.CostEstimate(flops=int(work_us * 1.1e9), bytes_accessed=0, transcendentals=0),
        compiler_params=pltpu.CompilerParams(vmem_limit_bytes=limit),
    )(*args)


def to_all(piece, gate, axis):
    peers = lax.axis_size(axis)
    copies = call(
        copies_kernel,
        [(peers,) + piece.shape],
        (piece, gate),
        1,
        specs=(pltpu.VMEM, pl.ANY),
    )
    return lax.all_to_all(copies, axis, 0, 0, tiled=True)


def on_device(q, k, v, w):
    x_size, z_size = lax.axis_size("x"), lax.axis_size("z")
    count = lax.axis_size("head")
    devices = 2 * x_size * z_size
    seq = ("x", "z", "core")
    swap = [(i, i ^ 1) for i in range(devices)]

    near_own, side_own, own3 = call(
        coarsen_kernel,
        [(2, 256, WIDTH), (2, 256, WIDTH), (2, 64, WIDTH)],
        (k, v),
        3,
        [(2, ROWS, WIDTH)],
        (2,),
    )
    side = lax.ppermute(side_own, seq, swap)
    turn = [(a * count + b, b * count + a) for a in range(x_size) for b in range(count)]
    w_turned = lax.ppermute(w.T, ("x", "head"), turn)

    near, chip3 = call(
        prepare_kernel,
        [(2, 320, WIDTH), (2, 128, WIDTH)],
        (side, near_own, own3),
        2,
        specs=[pltpu.VMEM] * 3,
    )
    to_near = [(i, (i + 1 if i % 2 else i - 1) % devices) for i in range(devices)]
    to_far = [(i, (i - 3 if i % 2 else i + 3) % devices) for i in range(devices)]
    near_in = lax.ppermute(near, seq, to_near)
    far_in = lax.ppermute(chip3, seq, to_far)

    w_z = to_all(w_turned, chip3, "z")

    attended = call(
        attention_kernel,
        [(ROWS, WIDTH)],
        (q, k, v, side, chip3, near_in, far_in),
        11,
        [(2, 256, WIDTH), (2, 128, WIDTH), (2, 2, 384, WIDTH), (2, 2, 128, WIDTH)],
        specs=[pltpu.VMEM] * 7,
    )

    one = [(i, i ^ 1) for i in range(count)]
    three = [(i, i ^ 3) for i in range(count)]
    half = ROWS // 2
    from_one = lax.ppermute(attended, "head", one)
    from_three = lax.ppermute(attended, "head", three)

    w_x = [w_z] + [
        lax.ppermute(w_z, "x", [(i, i ^ j) for i in range(x_size)]) for j in range(1, x_size)
    ]
    w_mine = call(
        stack_kernel, [(x_size,) + w_z.shape], w_x + [from_one, from_three], 1, (), (x_size,), out_spec=pl.ANY
    )
    w_other = lax.ppermute(w_mine, seq, swap)

    upper = lax.ppermute(from_one[:half], "head", three)
    lower = lax.ppermute(from_three[half:], "head", one)
    upper, lower = call(
        gate_kernel, [upper.shape] * 2, (upper, lower), 8, out_spec=pl.ANY, aliases={0: 0, 1: 1}
    )
    return call(
        project_kernel,
        [(ROWS, WIDTH)],
        (attended, from_one, from_three, upper, lower, w_mine, w_other),
        3,
        specs=[pltpu.VMEM] * 7,
    )


def solution(mesh):
    count = mesh.shape["head"]
    rows = ("x", "z", "core")
    grid = Mesh(mesh.devices.reshape(4, mesh.shape["seq"] // 8, 2, count), rows + ("head",))
    return jax.shard_map(
        on_device,
        mesh=grid,
        in_specs=(P(rows, "head"), P(rows, "head"), P(rows, "head"), P("head", rows)),
        out_specs=P(rows, "head"),
        check_vma=False,
    )
```

```python
import functools

import jax
import jax.numpy as jnp
from jax import lax
from jax.experimental import pallas as pl
from jax.experimental.pallas import tpu as pltpu
from jax.sharding import Mesh, PartitionSpec as P

HEAD_DIM = 128
BLOCK = 128
GROUP = 16
ROWS = 512
WIDTH = 512
HEADS_HERE = WIDTH // HEAD_DIM
SCALE2 = HEAD_DIM ** (-0.5) * 1.4426950408889634
MASKED = -1e30
F32 = jnp.float32
BF16 = jnp.bfloat16
VMEM_LIMIT = 16 * 1024 * 1024

NT = (((1,), (1,)), ((), ()))
NN = (((1,), (0,)), ((), ()))


def dot(a, b, dims=NN):
    return lax.dot_general(a, b, dims, preferred_element_type=F32)


def iota2(shape, dim):
    return lax.broadcasted_iota(jnp.int32, shape, dim)


def pair_average():
    row, col = iota2((64, 128), 0), iota2((64, 128), 1)
    return jnp.where((col >> 1) == 4 * (row & 15) + (row >> 4), 0.5, 0.0).astype(BF16)


def row_order():
    row, col = iota2((128, 128), 0), iota2((128, 128), 1)
    return jnp.where(col == 8 * (row & 15) + (row >> 4), 1.0, 0.0).astype(BF16)


def row_order_back():
    row, col = iota2((128, 128), 0), iota2((128, 128), 1)
    return jnp.where(row == 8 * (col & 15) + (col >> 4), 1.0, 0.0).astype(BF16)


def halve(x):
    wide = x.astype(F32)
    parts = [
        (wide[32 * i : 32 * i + 16] + wide[32 * i + 16 : 32 * i + 32]) * 0.5
        for i in range(x.shape[0] // 32)
    ]
    out = parts[0] if len(parts) == 1 else jnp.concatenate(parts, axis=0)
    return out.astype(BF16)


def spread(part):
    row, col = iota2((128, 128), 0), iota2((128, 128), 1)
    return jnp.where(row == 64 * part + 16 * (col >> 5) + (col & 15), 1.0, 0.0).astype(BF16)


def start_copies(sems, pairs):
    copies = [
        pltpu.make_async_copy(source, target, sems.at[i]) for i, (source, target) in enumerate(pairs)
    ]
    for copy in copies:
        copy.start()
    return copies


def coarsen_kernel(
    k_hbm, v_hbm, near_ref, side_ref, own3_ref, kv_ref, sems
):
    core = lax.axis_index("core")
    copies = start_copies(sems, ((k_hbm, kv_ref.at[0]), (v_hbm, kv_ref.at[1])))
    average = pair_average()
    for which, copy in enumerate(copies):
        copy.wait()
        own1 = [dot(average, kv_ref[which, 128 * n : 128 * n + 128, :]).astype(BF16) for n in range(4)]
        own2 = [halve(x) for x in own1]
        own3 = [halve(x) for x in own2]
        for n in range(4):
            own3_ref[which, 16 * n : 16 * n + 16, :] = own3[n]

        def edges(pack_ref, to_left):
            first, second, third, fourth = (0, 1, 2, 3) if to_left else (3, 2, 1, 0)
            pack_ref[which, 0:128, :] = kv_ref[which, 128 * first : 128 * first + 128, :]
            pack_ref[which, 128:192, :] = own1[second]
            pack_ref[which, 192:224, :] = own2[third]
            pack_ref[which, 224:256, :] = own2[fourth]

        def both_edges(near_is_left):
            edges(near_ref, near_is_left)
            edges(side_ref, not near_is_left)

        pl.when(core == 0)(functools.partial(both_edges, True))
        pl.when(core != 0)(functools.partial(both_edges, False))

def unpack(pack_ref, which, average, halo_ref, slot, chips_ref=None):
    edge = pack_ref[which, 0:128, :]
    edge1 = dot(average, edge).astype(BF16)
    next1 = pack_ref[which, 128:192, :]
    rest2 = pack_ref[which, 192:256, :]
    edge2, next2 = halve(edge1), halve(next1)
    pieces = ((0, edge), (128, edge1), (192, next1), (256, edge2), (288, next2), (320, rest2))
    for row, x in pieces:
        halo_ref[which, slot, row : row + x.shape[0], :] = x
    if chips_ref is not None:
        for row, x in ((0, halve(edge2)), (16, halve(next2)), (32, halve(rest2))):
            chips_ref[which, slot, row : row + x.shape[0], :] = x


def prepare_kernel(pack_ref, near_own_ref, own3_ref, near_ref, chip_ref):
    average = pair_average()
    for which in range(2):
        near_ref[which, 0:256, :] = near_own_ref[which]
        chip_ref[which, 0:64, :] = own3_ref[which]
        edge2 = halve(dot(average, pack_ref[which, 0:128, :]).astype(BF16))
        next2 = halve(pack_ref[which, 128:192, :])
        other3 = jnp.concatenate([halve(edge2), halve(next2), halve(pack_ref[which, 192:256, :])], axis=0)
        near_ref[which, 256:320, :] = other3
        chip_ref[which, 64:128, :] = other3


def copies_kernel(piece_ref, gate_hbm, out_ref):
    piece = piece_ref[...]
    for i in range(out_ref.shape[0]):
        out_ref[i] = piece


def gate_kernel(upper_hbm, lower_hbm, upper_out_hbm, lower_out_hbm):
    pass


def stack_kernel(a_hbm, b_hbm, c_hbm, d_hbm, gate_1_hbm, gate_3_hbm, out_hbm, sems):
    sources = (a_hbm, b_hbm, c_hbm, d_hbm)
    for copy in start_copies(sems, [(x, out_hbm.at[i]) for i, x in enumerate(sources)]):
        copy.wait()


def weigh(query, keys, values, bias_left, bias_right):
    scores = dot(jnp.concatenate(keys, axis=0), query, NT)
    if bias_left is not None:
        scores = jnp.concatenate([scores[:128] + bias_left, scores[128:]], axis=0)
    if bias_right is not None:
        scores = jnp.concatenate([scores[:256], scores[256:] + bias_right], axis=0)
    top = jnp.max(scores, axis=0, keepdims=True)
    probs = jnp.exp2((scores - top) * SCALE2).astype(BF16)
    wide = jnp.concatenate(values, axis=1)
    wide = jnp.concatenate([wide, jnp.ones((16, wide.shape[1]), BF16)], axis=0)
    return top, dot(wide, probs)


def parts_of(x, count):
    parts = []
    for _ in range(count):
        part = x.astype(BF16)
        parts.append(part)
        x = x - part.astype(F32)
    return parts


def merge(fine, coarse, spreading):
    fine_top, fine_sums = fine
    rows = fine_sums.shape[0]
    tops = jnp.broadcast_to(coarse[0], (16,) + coarse[0].shape[1:])
    doubled = dot(jnp.concatenate(parts_of(coarse[1], 2) + parts_of(tops, 3), axis=0), spreading)
    sums = doubled[:rows] + doubled[rows : 2 * rows]
    at = 2 * rows
    top = doubled[at : at + 1] + doubled[at + 16 : at + 17] + doubled[at + 32 : at + 33]
    fall = jnp.exp2(-jnp.abs(fine_top - top) * SCALE2)
    higher = fine_top >= top
    fine_factor = jnp.where(higher, 1.0, fall)
    factor = jnp.where(higher, fall, 1.0)
    return jnp.maximum(fine_top, top), fine_sums * fine_factor + sums * factor


def attention_kernel(
    q_ref, k_ref, v_ref, side_ref, chip_ref, near_ref, far_ref, out_ref,
    own1_ref, own2_ref, halo_ref, chips_ref,
):
    core = lax.axis_index("core")
    chip = lax.axis_index(("x", "z"))
    last = lax.axis_size(("x", "z")) - 1
    left_chip = jnp.where(chip > 0, 0.0, MASKED).astype(F32)
    right_chip = jnp.where(chip < last, 0.0, MASKED).astype(F32)
    left_bias = jnp.where(core == 0, left_chip, 0.0)
    right_bias = jnp.where(core == 0, 0.0, right_chip)
    average = pair_average()
    order = row_order()
    back = row_order_back()
    row, col = iota2((128, 128), 0), iota2((128, 128), 1)
    same = jnp.where(row == col, 1.0, 0.0).astype(BF16)
    spreads = [spread(part) for part in range(2)]
    side_slot, near_slot = 1 - core, core
    for which, ref in enumerate((k_ref, v_ref)):
        for n in range(4):
            own1 = dot(average, ref[128 * n : 128 * n + 128, :]).astype(BF16)
            own1_ref[which, 64 * n : 64 * n + 64, :] = own1
            own2_ref[which, 32 * n : 32 * n + 32, :] = halve(own1)
        unpack(side_ref, which, average, halo_ref, side_slot)
        unpack(near_ref, which, average, halo_ref, near_slot, chips_ref)
        chips_ref[which, near_slot, 64:128, :] = near_ref[which, 256:320, :]
        chips_ref[which, side_slot] = far_ref[which]

    def one_head(head, carry):
        lanes = pl.ds(pl.multiple_of(head * HEAD_DIM, HEAD_DIM), HEAD_DIM)
        q0 = [dot(order, q_ref[128 * n : 128 * n + 128, lanes]).astype(BF16) for n in range(4)]
        q1 = [halve(x) for x in q0]
        q2 = [halve(x) for x in q1]
        q3 = [halve(x) for x in q2]

        def own(which, level, index):
            if level == 0:
                return (k_ref, v_ref)[which][128 * index : 128 * index + 128, lanes]
            if level == 1:
                return own1_ref[which, 128 * index : 128 * index + 128, lanes]
            return own2_ref[which, :, lanes]

        def piece(which, level, index, count):
            if level == 3:
                return chip_ref[which, :, lanes] if index == 0 else chips_ref[which, (index + 1) // 2, :, lanes]
            if index < 0:
                return halo_ref[which, 0, 128 * level : 128 * level + 128, lanes]
            if index >= count:
                return halo_ref[which, 1, 128 * level : 128 * level + 128, lanes]
            return own(which, level, index)

        turned = {}

        def values(level, index, count):
            if (level, index) not in turned:
                turned[level, index] = dot(same, piece(1, level, index, count), NT).astype(BF16)
            return turned[level, index]

        def tile(query, level, index, count, left=left_bias, right=right_bias):
            near = [index - 1, index, index + 1]
            return weigh(
                query,
                [piece(0, level, i, count) for i in near],
                [values(level, i, count) for i in near],
                left if index == 0 else None,
                right if index == count - 1 else None,
            )

        at_3 = tile(jnp.concatenate(q3, axis=0), 3, 0, 1, left_chip, right_chip)
        at_2 = merge(tile(jnp.concatenate(q2, axis=0), 2, 0, 1), at_3, spreads[0][:64])
        for j in range(2):
            query_1 = jnp.concatenate(q1[2 * j : 2 * j + 2], axis=0)
            at_1 = merge(tile(query_1, 1, j, 2), at_2, spreads[j])
            for n in (2 * j, 2 * j + 1):
                _, sums = merge(tile(q0[n], 0, n, 4), at_1, spreads[n - 2 * j])
                attended = (sums[:128] / sums[128:129]).astype(BF16)
                out_ref[128 * n : 128 * n + 128, lanes] = dot(back, attended, NT).astype(BF16)
        return carry

    lax.fori_loop(0, HEADS_HERE, one_head, 0)


def project_kernel(
    own_ref, one_ref, three_ref, upper_ref, lower_ref, mine_ref, other_ref, out_ref
):
    core = lax.axis_index("core")
    twist = lax.axis_index("head") ^ lax.axis_index("x")
    half = ROWS // 2

    def run(first, second):
        def weight(i):
            return jnp.concatenate(
                [ref[twist ^ i, z] for z in range(first.shape[1]) for ref in (first, second)], axis=0
            )

        weights = [weight(i) for i in range(4)]
        for start, across in ((0, upper_ref), (half, lower_ref)):
            rows = slice(start, start + half)
            total = dot(own_ref[rows, :], weights[0], NT)
            total += dot(one_ref[rows, :], weights[1], NT)
            total += dot(three_ref[rows, :], weights[3], NT)
            total += dot(across[...], weights[2], NT)
            out_ref[rows, :] = total.astype(BF16)

    pl.when(core == 0)(functools.partial(run, mine_ref, other_ref))
    pl.when(core != 0)(functools.partial(run, other_ref, mine_ref))


def call(kernel, outs, args, work_us, scratch=(), copies=(), specs=None, out_spec=pltpu.VMEM, limit=VMEM_LIMIT, aliases=None):
    shapes = [jax.ShapeDtypeStruct(s, BF16) for s in outs]
    one = len(shapes) == 1
    out_specs = [pl.BlockSpec(memory_space=out_spec)] * len(outs)
    return pl.pallas_call(
        kernel,
        out_shape=shapes[0] if one else shapes,
        in_specs=[pl.BlockSpec(memory_space=s) for s in specs or [pl.ANY] * len(args)],
        out_specs=out_specs[0] if one else out_specs,
        scratch_shapes=[pltpu.VMEM(s, BF16) for s in scratch]
        + [pltpu.SemaphoreType.DMA((n,)) for n in copies],
        input_output_aliases=aliases or {},
        cost_estimate=pl.CostEstimate(flops=int(work_us * 1.1e9), bytes_accessed=0, transcendentals=0),
        compiler_params=pltpu.CompilerParams(vmem_limit_bytes=limit),
    )(*args)


def to_all(piece, gate, axis):
    peers = lax.axis_size(axis)
    copies = call(
        copies_kernel,
        [(peers,) + piece.shape],
        (piece, gate),
        1,
        specs=(pltpu.VMEM, pl.ANY),
    )
    return lax.all_to_all(copies, axis, 0, 0, tiled=True)


def on_device(q, k, v, w):
    x_size, z_size = lax.axis_size("x"), lax.axis_size("z")
    count = lax.axis_size("head")
    devices = 2 * x_size * z_size
    seq = ("x", "z", "core")
    swap = [(i, i ^ 1) for i in range(devices)]

    near_own, side_own, own3 = call(
        coarsen_kernel,
        [(2, 256, WIDTH), (2, 256, WIDTH), (2, 64, WIDTH)],
        (k, v),
        3,
        [(2, ROWS, WIDTH)],
        (2,),
    )
    side = lax.ppermute(side_own, seq, swap)
    turn = [(a * count + b, b * count + a) for a in range(x_size) for b in range(count)]
    w_turned = lax.ppermute(w.T, ("x", "head"), turn)

    near, chip3 = call(
        prepare_kernel,
        [(2, 320, WIDTH), (2, 128, WIDTH)],
        (side, near_own, own3),
        2,
        specs=[pltpu.VMEM] * 3,
    )
    to_near = [(i, (i + 1 if i % 2 else i - 1) % devices) for i in range(devices)]
    to_far = [(i, (i - 3 if i % 2 else i + 3) % devices) for i in range(devices)]
    near_in = lax.ppermute(near, seq, to_near)
    far_in = lax.ppermute(chip3, seq, to_far)

    w_z = to_all(w_turned, chip3, "z")

    attended = call(
        attention_kernel,
        [(ROWS, WIDTH)],
        (q, k, v, side, chip3, near_in, far_in),
        11,
        [(2, 256, WIDTH), (2, 128, WIDTH), (2, 2, 384, WIDTH), (2, 2, 128, WIDTH)],
        specs=[pltpu.VMEM] * 7,
    )

    one = [(i, i ^ 1) for i in range(count)]
    three = [(i, i ^ 3) for i in range(count)]
    half = ROWS // 2
    from_one = lax.ppermute(attended, "head", one)
    from_three = lax.ppermute(attended, "head", three)

    w_x = [w_z] + [
        lax.ppermute(w_z, "x", [(i, i ^ j) for i in range(x_size)]) for j in range(1, x_size)
    ]
    w_mine = call(
        stack_kernel, [(x_size,) + w_z.shape], w_x + [from_one, from_three], 1, (), (x_size,), out_spec=pl.ANY
    )
    w_other = lax.ppermute(w_mine, seq, swap)

    upper = lax.ppermute(from_one[:half], "head", three)
    lower = lax.ppermute(from_three[half:], "head", one)
    upper, lower = call(
        gate_kernel, [upper.shape] * 2, (upper, lower), 8, out_spec=pl.ANY, aliases={0: 0, 1: 1}
    )
    return call(
        project_kernel,
        [(ROWS, WIDTH)],
        (attended, from_one, from_three, upper, lower, w_mine, w_other),
        3,
        specs=[pltpu.VMEM] * 7,
    )


def solution(mesh):
    count = mesh.shape["head"]
    rows = ("x", "z", "core")
    grid = Mesh(mesh.devices.reshape(4, mesh.shape["seq"] // 8, 2, count), rows + ("head",))
    return jax.shard_map(
        on_device,
        mesh=grid,
        in_specs=(P(rows, "head"), P(rows, "head"), P(rows, "head"), P("head", rows)),
        out_specs=P(rows, "head"),
        check_vma=False,
    )
```

```python
import functools

import jax
import jax.numpy as jnp
from jax import lax
from jax.experimental import pallas as pl
from jax.experimental.pallas import tpu as pltpu
from jax.sharding import Mesh, PartitionSpec as P

HEAD_DIM = 128
BLOCK = 128
GROUP = 16
ROWS = 512
WIDTH = 512
HEADS_HERE = WIDTH // HEAD_DIM
SCALE2 = HEAD_DIM ** (-0.5) * 1.4426950408889634
MASKED = -1e30
F32 = jnp.float32
BF16 = jnp.bfloat16
VMEM_LIMIT = 16 * 1024 * 1024

NT = (((1,), (1,)), ((), ()))
NN = (((1,), (0,)), ((), ()))


def dot(a, b, dims=NN):
    return lax.dot_general(a, b, dims, preferred_element_type=F32)


def iota2(shape, dim):
    return lax.broadcasted_iota(jnp.int32, shape, dim)


def pair_average():
    row, col = iota2((64, 128), 0), iota2((64, 128), 1)
    return jnp.where((col >> 1) == 4 * (row & 15) + (row >> 4), 0.5, 0.0).astype(BF16)


def row_order():
    row, col = iota2((128, 128), 0), iota2((128, 128), 1)
    return jnp.where(col == 8 * (row & 15) + (row >> 4), 1.0, 0.0).astype(BF16)


def row_order_back():
    row, col = iota2((128, 128), 0), iota2((128, 128), 1)
    return jnp.where(row == 8 * (col & 15) + (col >> 4), 1.0, 0.0).astype(BF16)


def halve(x):
    wide = x.astype(F32)
    parts = [
        (wide[32 * i : 32 * i + 16] + wide[32 * i + 16 : 32 * i + 32]) * 0.5
        for i in range(x.shape[0] // 32)
    ]
    out = parts[0] if len(parts) == 1 else jnp.concatenate(parts, axis=0)
    return out.astype(BF16)


def double(x):
    parts = []
    for i in range(x.shape[0] // GROUP):
        piece = x[GROUP * i : GROUP * (i + 1)]
        parts += [piece, piece]
    return jnp.concatenate(parts, axis=0)


def start_copies(sems, pairs):
    copies = [
        pltpu.make_async_copy(source, target, sems.at[i]) for i, (source, target) in enumerate(pairs)
    ]
    for copy in copies:
        copy.start()
    return copies


def coarsen_kernel(
    k_hbm, v_hbm, near_ref, side_ref, own3_ref, kv_ref, sems
):
    core = lax.axis_index("core")
    copies = start_copies(sems, ((k_hbm, kv_ref.at[0]), (v_hbm, kv_ref.at[1])))
    average = pair_average()
    for which, copy in enumerate(copies):
        copy.wait()
        own1 = [dot(average, kv_ref[which, 128 * n : 128 * n + 128, :]).astype(BF16) for n in range(4)]
        own2 = [halve(x) for x in own1]
        own3 = [halve(x) for x in own2]
        for n in range(4):
            own3_ref[which, 16 * n : 16 * n + 16, :] = own3[n]

        def edges(pack_ref, to_left):
            first, second, third, fourth = (0, 1, 2, 3) if to_left else (3, 2, 1, 0)
            pack_ref[which, 0:128, :] = kv_ref[which, 128 * first : 128 * first + 128, :]
            pack_ref[which, 128:192, :] = own1[second]
            pack_ref[which, 192:224, :] = own2[third]
            pack_ref[which, 224:256, :] = own2[fourth]

        def both_edges(near_is_left):
            edges(near_ref, near_is_left)
            edges(side_ref, not near_is_left)

        pl.when(core == 0)(functools.partial(both_edges, True))
        pl.when(core != 0)(functools.partial(both_edges, False))

def unpack(pack_ref, which, average, halo_ref, slot, chips_ref=None):
    edge = pack_ref[which, 0:128, :]
    edge1 = dot(average, edge).astype(BF16)
    next1 = pack_ref[which, 128:192, :]
    rest2 = pack_ref[which, 192:256, :]
    edge2, next2 = halve(edge1), halve(next1)
    pieces = ((0, edge), (128, edge1), (192, next1), (256, edge2), (288, next2), (320, rest2))
    for row, x in pieces:
        halo_ref[which, slot, row : row + x.shape[0], :] = x
    if chips_ref is not None:
        for row, x in ((0, halve(edge2)), (16, halve(next2)), (32, halve(rest2))):
            chips_ref[which, slot, row : row + x.shape[0], :] = x


def prepare_kernel(pack_ref, near_own_ref, own3_ref, near_ref, chip_ref):
    average = pair_average()
    for which in range(2):
        near_ref[which, 0:256, :] = near_own_ref[which]
        chip_ref[which, 0:64, :] = own3_ref[which]
        edge2 = halve(dot(average, pack_ref[which, 0:128, :]).astype(BF16))
        next2 = halve(pack_ref[which, 128:192, :])
        other3 = jnp.concatenate([halve(edge2), halve(next2), halve(pack_ref[which, 192:256, :])], axis=0)
        near_ref[which, 256:320, :] = other3
        chip_ref[which, 64:128, :] = other3


def copies_kernel(piece_ref, gate_hbm, out_ref):
    piece = piece_ref[...]
    for i in range(out_ref.shape[0]):
        out_ref[i] = piece


def gate_kernel(upper_hbm, lower_hbm, upper_out_hbm, lower_out_hbm):
    pass


def hold_kernel(value_hbm, gate_hbm, out_hbm):
    pass


def stack_kernel(a_hbm, b_hbm, c_hbm, d_hbm, gate_1_hbm, gate_3_hbm, out_hbm, sems):
    sources = (a_hbm, b_hbm, c_hbm, d_hbm)
    for copy in start_copies(sems, [(x, out_hbm.at[i]) for i, x in enumerate(sources)]):
        copy.wait()


def weigh(query, keys, values, bias_left, bias_right):
    scores = dot(query, jnp.concatenate(keys, axis=0), NT)
    if bias_left is not None:
        scores = jnp.concatenate([scores[:, :128] + bias_left, scores[:, 128:]], axis=1)
    if bias_right is not None:
        scores = jnp.concatenate([scores[:, :256], scores[:, 256:] + bias_right], axis=1)
    top = jnp.max(scores, axis=1, keepdims=True)
    probs = jnp.exp2((scores - top) * SCALE2).astype(BF16)
    wide = jnp.concatenate(values, axis=0)
    wide = jnp.concatenate([wide, jnp.ones_like(wide)], axis=1)
    return top, dot(probs, wide)


def merge(fine, coarse):
    fine_top, fine_sums = fine
    top, sums = double(coarse[0]), double(coarse[1])
    fall = jnp.exp2(-jnp.abs(fine_top - top) * SCALE2)
    higher = fine_top >= top
    fine_factor = jnp.where(higher, 1.0, fall)
    factor = jnp.where(higher, fall, 1.0)
    return jnp.maximum(fine_top, top), fine_sums * fine_factor + sums * factor


def attention_kernel(
    q_ref, k_ref, v_ref, side_ref, chip_ref, near_ref, far_ref, out_ref,
    own1_ref, own2_ref, halo_ref, chips_ref,
):
    core = lax.axis_index("core")
    chip = lax.axis_index(("x", "z"))
    last = lax.axis_size(("x", "z")) - 1
    left_chip = jnp.where(chip > 0, 0.0, MASKED).astype(F32)
    right_chip = jnp.where(chip < last, 0.0, MASKED).astype(F32)
    left_bias = jnp.where(core == 0, left_chip, 0.0)
    right_bias = jnp.where(core == 0, 0.0, right_chip)
    average = pair_average()
    order = row_order()
    back = row_order_back()
    side_slot, near_slot = 1 - core, core
    for which, ref in enumerate((k_ref, v_ref)):
        for n in range(4):
            own1 = dot(average, ref[128 * n : 128 * n + 128, :]).astype(BF16)
            own1_ref[which, 64 * n : 64 * n + 64, :] = own1
            own2_ref[which, 32 * n : 32 * n + 32, :] = halve(own1)
        unpack(side_ref, which, average, halo_ref, side_slot)
        unpack(near_ref, which, average, halo_ref, near_slot, chips_ref)
        chips_ref[which, near_slot, 64:128, :] = near_ref[which, 256:320, :]
        chips_ref[which, side_slot] = far_ref[which]

    def one_head(head, carry):
        lanes = pl.ds(pl.multiple_of(head * HEAD_DIM, HEAD_DIM), HEAD_DIM)
        q0 = [dot(order, q_ref[128 * n : 128 * n + 128, lanes]).astype(BF16) for n in range(4)]
        q1 = [halve(x) for x in q0]
        q2 = [halve(x) for x in q1]
        q3 = [halve(x) for x in q2]

        def piece(own, which, level, index, count):
            if index < 0:
                return halo_ref[which, 0, 128 * level : 128 * level + 128, lanes]
            if index >= count:
                return halo_ref[which, 1, 128 * level : 128 * level + 128, lanes]
            return own(which, index)

        def own_0(which, index):
            return (k_ref, v_ref)[which][128 * index : 128 * index + 128, lanes]

        def own_1(which, index):
            return own1_ref[which, 128 * index : 128 * index + 128, lanes]

        def own_2(which, index):
            return own2_ref[which, :, lanes]

        def tile(query, own, level, index, count):
            near = [index - 1, index, index + 1]
            return weigh(
                query,
                [piece(own, 0, level, i, count) for i in near],
                [piece(own, 1, level, i, count) for i in near],
                left_bias if index == 0 else None,
                right_bias if index == count - 1 else None,
            )

        at_3 = weigh(
            jnp.concatenate(q3, axis=0),
            [chips_ref[0, 0, :, lanes], chip_ref[0, :, lanes], chips_ref[0, 1, :, lanes]],
            [chips_ref[1, 0, :, lanes], chip_ref[1, :, lanes], chips_ref[1, 1, :, lanes]],
            left_chip,
            right_chip,
        )
        at_2 = merge(tile(jnp.concatenate(q2, axis=0), own_2, 2, 0, 1), at_3)
        for j in range(2):
            half_2 = tuple(x[64 * j : 64 * j + 64] for x in at_2)
            query_1 = jnp.concatenate(q1[2 * j : 2 * j + 2], axis=0)
            at_1 = merge(tile(query_1, own_1, 1, j, 2), half_2)
            for n in (2 * j, 2 * j + 1):
                start = 64 * (n - 2 * j)
                half_1 = tuple(x[start : start + 64] for x in at_1)
                _, sums = merge(tile(q0[n], own_0, 0, n, 4), half_1)
                attended = (sums[:, :128] / sums[:, 128:]).astype(BF16)
                out_ref[128 * n : 128 * n + 128, lanes] = dot(back, attended).astype(BF16)
        return carry

    lax.fori_loop(0, HEADS_HERE, one_head, 0)


def project_kernel(
    own_ref, one_ref, three_ref, upper_ref, lower_ref, mine_ref, other_ref, out_ref
):
    core = lax.axis_index("core")
    twist = lax.axis_index("head") ^ lax.axis_index("x")
    half = ROWS // 2

    def run(first, second):
        def weight(i):
            return jnp.concatenate(
                [ref[twist ^ i, z] for z in range(first.shape[1]) for ref in (first, second)], axis=0
            )

        weights = [weight(i) for i in range(4)]
        for start, across in ((0, upper_ref), (half, lower_ref)):
            rows = slice(start, start + half)
            total = dot(own_ref[rows, :], weights[0], NT)
            total += dot(one_ref[rows, :], weights[1], NT)
            total += dot(three_ref[rows, :], weights[3], NT)
            total += dot(across[...], weights[2], NT)
            out_ref[rows, :] = total.astype(BF16)

    pl.when(core == 0)(functools.partial(run, mine_ref, other_ref))
    pl.when(core != 0)(functools.partial(run, other_ref, mine_ref))


def call(kernel, outs, args, work_us, scratch=(), copies=(), specs=None, out_spec=pltpu.VMEM, limit=VMEM_LIMIT, aliases=None):
    shapes = [jax.ShapeDtypeStruct(s, BF16) for s in outs]
    one = len(shapes) == 1
    out_specs = [pl.BlockSpec(memory_space=out_spec)] * len(outs)
    return pl.pallas_call(
        kernel,
        out_shape=shapes[0] if one else shapes,
        in_specs=[pl.BlockSpec(memory_space=s) for s in specs or [pl.ANY] * len(args)],
        out_specs=out_specs[0] if one else out_specs,
        scratch_shapes=[pltpu.VMEM(s, BF16) for s in scratch]
        + [pltpu.SemaphoreType.DMA((n,)) for n in copies],
        input_output_aliases=aliases or {},
        cost_estimate=pl.CostEstimate(flops=int(work_us * 1.1e9), bytes_accessed=0, transcendentals=0),
        compiler_params=pltpu.CompilerParams(vmem_limit_bytes=limit),
    )(*args)


def to_all(piece, gate, axis):
    peers = lax.axis_size(axis)
    copies = call(
        copies_kernel,
        [(peers,) + piece.shape],
        (piece, gate),
        1,
        specs=(pltpu.VMEM, pl.ANY),
    )
    return lax.all_to_all(copies, axis, 0, 0, tiled=True)


def on_device(q, k, v, w):
    x_size, z_size = lax.axis_size("x"), lax.axis_size("z")
    count = lax.axis_size("head")
    devices = 2 * x_size * z_size
    seq = ("x", "z", "core")
    swap = [(i, i ^ 1) for i in range(devices)]

    near_own, side_own, own3 = call(
        coarsen_kernel,
        [(2, 256, WIDTH), (2, 256, WIDTH), (2, 64, WIDTH)],
        (k, v),
        3,
        [(2, ROWS, WIDTH)],
        (2,),
    )
    side = lax.ppermute(side_own, seq, swap)
    turn = [(a * count + b, b * count + a) for a in range(x_size) for b in range(count)]
    w_turned = lax.ppermute(w.T, ("x", "head"), turn)

    near, chip3 = call(
        prepare_kernel,
        [(2, 320, WIDTH), (2, 128, WIDTH)],
        (side, near_own, own3),
        2,
        specs=[pltpu.VMEM] * 3,
    )
    to_near = [(i, (i + 1 if i % 2 else i - 1) % devices) for i in range(devices)]
    to_far = [(i, (i - 3 if i % 2 else i + 3) % devices) for i in range(devices)]
    near_in = lax.ppermute(near, seq, to_near)
    chip3 = call(hold_kernel, [chip3.shape], (chip3, w_turned), 0.1, out_spec=pl.ANY, aliases={0: 0})
    far_in = lax.ppermute(chip3, seq, to_far)

    w_z = to_all(w_turned, chip3, "z")

    attended = call(
        attention_kernel,
        [(ROWS, WIDTH)],
        (q, k, v, side, chip3, near_in, far_in),
        11,
        [(2, 256, WIDTH), (2, 128, WIDTH), (2, 2, 384, WIDTH), (2, 2, 128, WIDTH)],
        specs=[pltpu.VMEM] * 7,
    )

    one = [(i, i ^ 1) for i in range(count)]
    three = [(i, i ^ 3) for i in range(count)]
    half = ROWS // 2
    from_one = lax.ppermute(attended, "head", one)
    from_three = lax.ppermute(attended, "head", three)

    w_x = [w_z] + [
        lax.ppermute(w_z, "x", [(i, i ^ j) for i in range(x_size)]) for j in range(1, x_size)
    ]
    w_mine = call(
        stack_kernel, [(x_size,) + w_z.shape], w_x + [from_one, from_three], 1, (), (x_size,), out_spec=pl.ANY
    )
    w_other = lax.ppermute(w_mine, seq, swap)

    upper = lax.ppermute(from_one[:half], "head", three)
    lower = lax.ppermute(from_three[half:], "head", one)
    upper, lower = call(
        gate_kernel, [upper.shape] * 2, (upper, lower), 8, out_spec=pl.ANY, aliases={0: 0, 1: 1}
    )
    return call(
        project_kernel,
        [(ROWS, WIDTH)],
        (attended, from_one, from_three, upper, lower, w_mine, w_other),
        3,
        specs=[pltpu.VMEM] * 7,
    )


def solution(mesh):
    count = mesh.shape["head"]
    rows = ("x", "z", "core")
    grid = Mesh(mesh.devices.reshape(4, mesh.shape["seq"] // 8, 2, count), rows + ("head",))
    return jax.shard_map(
        on_device,
        mesh=grid,
        in_specs=(P(rows, "head"), P(rows, "head"), P(rows, "head"), P("head", rows)),
        out_specs=P(rows, "head"),
        check_vma=False,
    )
```

```python
import functools

import jax
import jax.numpy as jnp
from jax import lax
from jax.experimental import pallas as pl
from jax.experimental.pallas import tpu as pltpu
from jax.sharding import Mesh, PartitionSpec as P

HEAD_DIM = 128
BLOCK = 128
GROUP = 16
ROWS = 512
WIDTH = 512
HEADS_HERE = WIDTH // HEAD_DIM
SCALE2 = HEAD_DIM ** (-0.5) * 1.4426950408889634
MASKED = -1e30
F32 = jnp.float32
BF16 = jnp.bfloat16
VMEM_LIMIT = 16 * 1024 * 1024

NT = (((1,), (1,)), ((), ()))
NN = (((1,), (0,)), ((), ()))


def dot(a, b, dims=NN):
    return lax.dot_general(a, b, dims, preferred_element_type=F32)


def iota2(shape, dim):
    return lax.broadcasted_iota(jnp.int32, shape, dim)


def pair_average():
    row, col = iota2((64, 128), 0), iota2((64, 128), 1)
    return jnp.where((col >> 1) == 4 * (row & 15) + (row >> 4), 0.5, 0.0).astype(BF16)


def row_order():
    row, col = iota2((128, 128), 0), iota2((128, 128), 1)
    return jnp.where(col == 8 * (row & 15) + (row >> 4), 1.0, 0.0).astype(BF16)


def row_order_back():
    row, col = iota2((128, 128), 0), iota2((128, 128), 1)
    return jnp.where(row == 8 * (col & 15) + (col >> 4), 1.0, 0.0).astype(BF16)


def halve(x):
    wide = x.astype(F32)
    parts = [
        (wide[32 * i : 32 * i + 16] + wide[32 * i + 16 : 32 * i + 32]) * 0.5
        for i in range(x.shape[0] // 32)
    ]
    out = parts[0] if len(parts) == 1 else jnp.concatenate(parts, axis=0)
    return out.astype(BF16)


def double(x):
    parts = []
    for i in range(x.shape[0] // GROUP):
        piece = x[GROUP * i : GROUP * (i + 1)]
        parts += [piece, piece]
    return jnp.concatenate(parts, axis=0)


def start_copies(sems, pairs):
    copies = [
        pltpu.make_async_copy(source, target, sems.at[i]) for i, (source, target) in enumerate(pairs)
    ]
    for copy in copies:
        copy.start()
    return copies


def coarsen_kernel(
    k_hbm, v_hbm, near_ref, side_ref, own3_ref, kv_ref, sems
):
    core = lax.axis_index("core")
    copies = start_copies(sems, ((k_hbm, kv_ref.at[0]), (v_hbm, kv_ref.at[1])))
    average = pair_average()
    for which, copy in enumerate(copies):
        copy.wait()
        own1 = [dot(average, kv_ref[which, 128 * n : 128 * n + 128, :]).astype(BF16) for n in range(4)]
        own2 = [halve(x) for x in own1]
        own3 = [halve(x) for x in own2]
        for n in range(4):
            own3_ref[which, 16 * n : 16 * n + 16, :] = own3[n]

        def edges(pack_ref, to_left):
            first, second, third, fourth = (0, 1, 2, 3) if to_left else (3, 2, 1, 0)
            pack_ref[which, 0:128, :] = kv_ref[which, 128 * first : 128 * first + 128, :]
            pack_ref[which, 128:192, :] = own1[second]
            pack_ref[which, 192:224, :] = own2[third]
            pack_ref[which, 224:256, :] = own2[fourth]

        def both_edges(near_is_left):
            edges(near_ref, near_is_left)
            edges(side_ref, not near_is_left)

        pl.when(core == 0)(functools.partial(both_edges, True))
        pl.when(core != 0)(functools.partial(both_edges, False))

def unpack(pack_ref, which, average, halo_ref, slot, chips_ref=None):
    edge = pack_ref[which, 0:128, :]
    edge1 = dot(average, edge).astype(BF16)
    next1 = pack_ref[which, 128:192, :]
    rest2 = pack_ref[which, 192:256, :]
    edge2, next2 = halve(edge1), halve(next1)
    pieces = ((0, edge), (128, edge1), (192, next1), (256, edge2), (288, next2), (320, rest2))
    for row, x in pieces:
        halo_ref[which, slot, row : row + x.shape[0], :] = x
    if chips_ref is not None:
        for row, x in ((0, halve(edge2)), (16, halve(next2)), (32, halve(rest2))):
            chips_ref[which, slot, row : row + x.shape[0], :] = x


def prepare_kernel(pack_ref, near_own_ref, own3_ref, near_ref, chip_ref):
    average = pair_average()
    for which in range(2):
        near_ref[which, 0:256, :] = near_own_ref[which]
        chip_ref[which, 0:64, :] = own3_ref[which]
        edge2 = halve(dot(average, pack_ref[which, 0:128, :]).astype(BF16))
        next2 = halve(pack_ref[which, 128:192, :])
        other3 = jnp.concatenate([halve(edge2), halve(next2), halve(pack_ref[which, 192:256, :])], axis=0)
        near_ref[which, 256:320, :] = other3
        chip_ref[which, 64:128, :] = other3


def copies_kernel(piece_ref, gate_hbm, out_ref):
    piece = piece_ref[...]
    for i in range(out_ref.shape[0]):
        out_ref[i] = piece


def gate_kernel(upper_hbm, lower_hbm, upper_out_hbm, lower_out_hbm):
    pass


def hold_kernel(value_hbm, out_hbm):
    pass


def stack_kernel(a_hbm, b_hbm, c_hbm, d_hbm, gate_1_hbm, gate_3_hbm, out_hbm, sems):
    sources = (a_hbm, b_hbm, c_hbm, d_hbm)
    for copy in start_copies(sems, [(x, out_hbm.at[i]) for i, x in enumerate(sources)]):
        copy.wait()


def weigh(query, keys, values, bias_left, bias_right):
    scores = dot(query, jnp.concatenate(keys, axis=0), NT)
    if bias_left is not None:
        scores = jnp.concatenate([scores[:, :128] + bias_left, scores[:, 128:]], axis=1)
    if bias_right is not None:
        scores = jnp.concatenate([scores[:, :256], scores[:, 256:] + bias_right], axis=1)
    top = jnp.max(scores, axis=1, keepdims=True)
    weights = jnp.exp2((scores - top) * SCALE2)
    total = jnp.sum(weights, axis=1, keepdims=True)
    return top, total, dot(weights.astype(BF16), jnp.concatenate(values, axis=0))


def merge(fine, coarse):
    fine_top, fine_total, fine_numerator = fine
    top, total, numerator = (double(x) for x in coarse)
    fall = jnp.exp2(-jnp.abs(fine_top - top) * SCALE2)
    higher = fine_top >= top
    fine_factor = jnp.where(higher, 1.0, fall)
    factor = jnp.where(higher, fall, 1.0)
    return (
        jnp.maximum(fine_top, top),
        fine_total * fine_factor + total * factor,
        fine_numerator * fine_factor + numerator * factor,
    )


def attention_kernel(
    q_ref, k_ref, v_ref, side_ref, chip_ref, near_ref, far_ref, out_ref,
    own1_ref, own2_ref, halo_ref, chips_ref,
):
    core = lax.axis_index("core")
    chip = lax.axis_index(("x", "z"))
    last = lax.axis_size(("x", "z")) - 1
    left_chip = jnp.where(chip > 0, 0.0, MASKED).astype(F32)
    right_chip = jnp.where(chip < last, 0.0, MASKED).astype(F32)
    left_bias = jnp.where(core == 0, left_chip, 0.0)
    right_bias = jnp.where(core == 0, 0.0, right_chip)
    average = pair_average()
    order = row_order()
    back = row_order_back()
    side_slot, near_slot = 1 - core, core
    for which, ref in enumerate((k_ref, v_ref)):
        for n in range(4):
            own1 = dot(average, ref[128 * n : 128 * n + 128, :]).astype(BF16)
            own1_ref[which, 64 * n : 64 * n + 64, :] = own1
            own2_ref[which, 32 * n : 32 * n + 32, :] = halve(own1)
        unpack(side_ref, which, average, halo_ref, side_slot)
        unpack(near_ref, which, average, halo_ref, near_slot, chips_ref)
        chips_ref[which, near_slot, 64:128, :] = near_ref[which, 256:320, :]
        chips_ref[which, side_slot] = far_ref[which]

    def one_head(head, carry):
        lanes = pl.ds(pl.multiple_of(head * HEAD_DIM, HEAD_DIM), HEAD_DIM)
        q0 = [dot(order, q_ref[128 * n : 128 * n + 128, lanes]).astype(BF16) for n in range(4)]
        q1 = [halve(x) for x in q0]
        q2 = [halve(x) for x in q1]
        q3 = [halve(x) for x in q2]

        def piece(own, which, level, index, count):
            if index < 0:
                return halo_ref[which, 0, 128 * level : 128 * level + 128, lanes]
            if index >= count:
                return halo_ref[which, 1, 128 * level : 128 * level + 128, lanes]
            return own(which, index)

        def own_0(which, index):
            return (k_ref, v_ref)[which][128 * index : 128 * index + 128, lanes]

        def own_1(which, index):
            return own1_ref[which, 128 * index : 128 * index + 128, lanes]

        def own_2(which, index):
            return own2_ref[which, :, lanes]

        def tile(query, own, level, index, count):
            near = [index - 1, index, index + 1]
            return weigh(
                query,
                [piece(own, 0, level, i, count) for i in near],
                [piece(own, 1, level, i, count) for i in near],
                left_bias if index == 0 else None,
                right_bias if index == count - 1 else None,
            )

        at_3 = weigh(
            jnp.concatenate(q3, axis=0),
            [chips_ref[0, 0, :, lanes], chip_ref[0, :, lanes], chips_ref[0, 1, :, lanes]],
            [chips_ref[1, 0, :, lanes], chip_ref[1, :, lanes], chips_ref[1, 1, :, lanes]],
            left_chip,
            right_chip,
        )
        at_2 = merge(tile(jnp.concatenate(q2, axis=0), own_2, 2, 0, 1), at_3)
        for j in range(2):
            half_2 = tuple(x[64 * j : 64 * j + 64] for x in at_2)
            query_1 = jnp.concatenate(q1[2 * j : 2 * j + 2], axis=0)
            at_1 = merge(tile(query_1, own_1, 1, j, 2), half_2)
            for n in (2 * j, 2 * j + 1):
                start = 64 * (n - 2 * j)
                half_1 = tuple(x[start : start + 64] for x in at_1)
                _, total, numerator = merge(tile(q0[n], own_0, 0, n, 4), half_1)
                attended = (numerator / total).astype(BF16)
                out_ref[128 * n : 128 * n + 128, lanes] = dot(back, attended).astype(BF16)
        return carry

    lax.fori_loop(0, HEADS_HERE, one_head, 0)


def project_kernel(
    own_ref, one_ref, three_ref, upper_ref, lower_ref, mine_ref, other_ref, out_ref
):
    core = lax.axis_index("core")
    twist = lax.axis_index("head") ^ lax.axis_index("x")
    half = ROWS // 2

    def run(first, second):
        def weight(i):
            return jnp.concatenate(
                [ref[twist ^ i, z] for z in range(first.shape[1]) for ref in (first, second)], axis=0
            )

        weights = [weight(i) for i in range(4)]
        for start, across in ((0, upper_ref), (half, lower_ref)):
            rows = slice(start, start + half)
            total = dot(own_ref[rows, :], weights[0], NT)
            total += dot(one_ref[rows, :], weights[1], NT)
            total += dot(three_ref[rows, :], weights[3], NT)
            total += dot(across[...], weights[2], NT)
            out_ref[rows, :] = total.astype(BF16)

    pl.when(core == 0)(functools.partial(run, mine_ref, other_ref))
    pl.when(core != 0)(functools.partial(run, other_ref, mine_ref))


def call(kernel, outs, args, work_us, scratch=(), copies=(), specs=None, out_spec=pltpu.VMEM, limit=VMEM_LIMIT, aliases=None):
    shapes = [jax.ShapeDtypeStruct(s, BF16) for s in outs]
    one = len(shapes) == 1
    out_specs = [pl.BlockSpec(memory_space=out_spec)] * len(outs)
    return pl.pallas_call(
        kernel,
        out_shape=shapes[0] if one else shapes,
        in_specs=[pl.BlockSpec(memory_space=s) for s in specs or [pl.ANY] * len(args)],
        out_specs=out_specs[0] if one else out_specs,
        scratch_shapes=[pltpu.VMEM(s, BF16) for s in scratch]
        + [pltpu.SemaphoreType.DMA((n,)) for n in copies],
        input_output_aliases=aliases or {},
        cost_estimate=pl.CostEstimate(flops=int(work_us * 1.1e9), bytes_accessed=0, transcendentals=0),
        compiler_params=pltpu.CompilerParams(vmem_limit_bytes=limit),
    )(*args)


def to_all(piece, gate, axis):
    peers = lax.axis_size(axis)
    copies = call(
        copies_kernel,
        [(peers,) + piece.shape],
        (piece, gate),
        1,
        specs=(pltpu.VMEM, pl.ANY),
    )
    return lax.all_to_all(copies, axis, 0, 0, tiled=True)


def on_device(q, k, v, w):
    x_size, z_size = lax.axis_size("x"), lax.axis_size("z")
    count = lax.axis_size("head")
    devices = 2 * x_size * z_size
    seq = ("x", "z", "core")
    swap = [(i, i ^ 1) for i in range(devices)]

    near_own, side_own, own3 = call(
        coarsen_kernel,
        [(2, 256, WIDTH), (2, 256, WIDTH), (2, 64, WIDTH)],
        (k, v),
        3,
        [(2, ROWS, WIDTH)],
        (2,),
    )
    side = lax.ppermute(side_own, seq, swap)
    turn = [(a * count + b, b * count + a) for a in range(x_size) for b in range(count)]
    w_turned = lax.ppermute(w.T, ("x", "head"), turn)
    w_turned = call(hold_kernel, [w_turned.shape], (w_turned,), 20, out_spec=pl.ANY, aliases={0: 0})

    near, chip3 = call(
        prepare_kernel,
        [(2, 320, WIDTH), (2, 128, WIDTH)],
        (side, near_own, own3),
        2,
        specs=[pltpu.VMEM] * 3,
    )
    to_near = [(i, (i + 1 if i % 2 else i - 1) % devices) for i in range(devices)]
    to_far = [(i, (i - 3 if i % 2 else i + 3) % devices) for i in range(devices)]
    near_in = lax.ppermute(near, seq, to_near)
    far_in = lax.ppermute(chip3, seq, to_far)

    w_z = to_all(w_turned, chip3, "z")

    attended = call(
        attention_kernel,
        [(ROWS, WIDTH)],
        (q, k, v, side, chip3, near_in, far_in),
        11,
        [(2, 256, WIDTH), (2, 128, WIDTH), (2, 2, 384, WIDTH), (2, 2, 128, WIDTH)],
        specs=[pltpu.VMEM] * 7,
    )

    one = [(i, i ^ 1) for i in range(count)]
    three = [(i, i ^ 3) for i in range(count)]
    half = ROWS // 2
    from_one = lax.ppermute(attended, "head", one)
    from_three = lax.ppermute(attended, "head", three)

    w_x = [w_z] + [
        lax.ppermute(w_z, "x", [(i, i ^ j) for i in range(x_size)]) for j in range(1, x_size)
    ]
    w_mine = call(
        stack_kernel, [(x_size,) + w_z.shape], w_x + [from_one, from_three], 1, (), (x_size,), out_spec=pl.ANY
    )
    w_other = lax.ppermute(w_mine, seq, swap)

    upper = lax.ppermute(from_one[:half], "head", three)
    lower = lax.ppermute(from_three[half:], "head", one)
    upper, lower = call(
        gate_kernel, [upper.shape] * 2, (upper, lower), 8, out_spec=pl.ANY, aliases={0: 0, 1: 1}
    )
    return call(
        project_kernel,
        [(ROWS, WIDTH)],
        (attended, from_one, from_three, upper, lower, w_mine, w_other),
        3,
        specs=[pltpu.VMEM] * 7,
    )


def solution(mesh):
    count = mesh.shape["head"]
    rows = ("x", "z", "core")
    grid = Mesh(mesh.devices.reshape(4, mesh.shape["seq"] // 8, 2, count), rows + ("head",))
    return jax.shard_map(
        on_device,
        mesh=grid,
        in_specs=(P(rows, "head"), P(rows, "head"), P(rows, "head"), P("head", rows)),
        out_specs=P(rows, "head"),
        check_vma=False,
    )
```

```python
import functools

import jax
import jax.numpy as jnp
from jax import lax
from jax.experimental import pallas as pl
from jax.experimental.pallas import tpu as pltpu
from jax.sharding import Mesh, PartitionSpec as P

HEAD_DIM = 128
BLOCK = 128
GROUP = 16
ROWS = 512
WIDTH = 512
HEADS_HERE = WIDTH // HEAD_DIM
SCALE2 = HEAD_DIM ** (-0.5) * 1.4426950408889634
MASKED = -1e30
F32 = jnp.float32
BF16 = jnp.bfloat16
VMEM_LIMIT = 16 * 1024 * 1024

NT = (((1,), (1,)), ((), ()))
NN = (((1,), (0,)), ((), ()))


def dot(a, b, dims=NN):
    return lax.dot_general(a, b, dims, preferred_element_type=F32)


def iota2(shape, dim):
    return lax.broadcasted_iota(jnp.int32, shape, dim)


def pair_average():
    row, col = iota2((64, 128), 0), iota2((64, 128), 1)
    return jnp.where((col >> 1) == 4 * (row & 15) + (row >> 4), 0.5, 0.0).astype(BF16)


def row_order():
    row, col = iota2((128, 128), 0), iota2((128, 128), 1)
    return jnp.where(col == 8 * (row & 15) + (row >> 4), 1.0, 0.0).astype(BF16)


def row_order_back():
    row, col = iota2((128, 128), 0), iota2((128, 128), 1)
    return jnp.where(row == 8 * (col & 15) + (col >> 4), 1.0, 0.0).astype(BF16)


def halve(x):
    wide = x.astype(F32)
    parts = [
        (wide[32 * i : 32 * i + 16] + wide[32 * i + 16 : 32 * i + 32]) * 0.5
        for i in range(x.shape[0] // 32)
    ]
    out = parts[0] if len(parts) == 1 else jnp.concatenate(parts, axis=0)
    return out.astype(BF16)


def double(x):
    parts = []
    for i in range(x.shape[0] // GROUP):
        piece = x[GROUP * i : GROUP * (i + 1)]
        parts += [piece, piece]
    return jnp.concatenate(parts, axis=0)


def start_copies(sems, pairs):
    copies = [
        pltpu.make_async_copy(source, target, sems.at[i]) for i, (source, target) in enumerate(pairs)
    ]
    for copy in copies:
        copy.start()
    return copies


def coarsen_kernel(
    k_hbm, v_hbm, near_ref, side_ref, own3_ref, kv_ref, sems
):
    core = lax.axis_index("core")
    copies = start_copies(sems, ((k_hbm, kv_ref.at[0]), (v_hbm, kv_ref.at[1])))
    average = pair_average()
    for which, copy in enumerate(copies):
        copy.wait()
        own1 = [dot(average, kv_ref[which, 128 * n : 128 * n + 128, :]).astype(BF16) for n in range(4)]
        own2 = [halve(x) for x in own1]
        own3 = [halve(x) for x in own2]
        for n in range(4):
            own3_ref[which, 16 * n : 16 * n + 16, :] = own3[n]

        def edges(pack_ref, to_left):
            first, second, third, fourth = (0, 1, 2, 3) if to_left else (3, 2, 1, 0)
            pack_ref[which, 0:128, :] = kv_ref[which, 128 * first : 128 * first + 128, :]
            pack_ref[which, 128:192, :] = own1[second]
            pack_ref[which, 192:224, :] = own2[third]
            pack_ref[which, 224:256, :] = own2[fourth]

        def both_edges(near_is_left):
            edges(near_ref, near_is_left)
            edges(side_ref, not near_is_left)

        pl.when(core == 0)(functools.partial(both_edges, True))
        pl.when(core != 0)(functools.partial(both_edges, False))

def unpack(pack_ref, which, average, halo_ref, slot, chips_ref=None):
    edge = pack_ref[which, 0:128, :]
    edge1 = dot(average, edge).astype(BF16)
    next1 = pack_ref[which, 128:192, :]
    rest2 = pack_ref[which, 192:256, :]
    edge2, next2 = halve(edge1), halve(next1)
    pieces = ((0, edge), (128, edge1), (192, next1), (256, edge2), (288, next2), (320, rest2))
    for row, x in pieces:
        halo_ref[which, slot, row : row + x.shape[0], :] = x
    if chips_ref is not None:
        for row, x in ((0, halve(edge2)), (16, halve(next2)), (32, halve(rest2))):
            chips_ref[which, slot, row : row + x.shape[0], :] = x


def prepare_kernel(pack_ref, near_own_ref, own3_ref, near_ref, chip_ref):
    average = pair_average()
    for which in range(2):
        near_ref[which, 0:256, :] = near_own_ref[which]
        chip_ref[which, 0:64, :] = own3_ref[which]
        edge2 = halve(dot(average, pack_ref[which, 0:128, :]).astype(BF16))
        next2 = halve(pack_ref[which, 128:192, :])
        other3 = jnp.concatenate([halve(edge2), halve(next2), halve(pack_ref[which, 192:256, :])], axis=0)
        near_ref[which, 256:320, :] = other3
        chip_ref[which, 64:128, :] = other3


def copies_kernel(piece_ref, gate_hbm, out_ref):
    piece = piece_ref[...]
    for i in range(out_ref.shape[0]):
        out_ref[i] = piece


def gate_kernel(upper_hbm, lower_hbm, upper_out_hbm, lower_out_hbm):
    pass


def hold_kernel(value_hbm, out_hbm):
    pass


def stack_kernel(a_hbm, b_hbm, c_hbm, d_hbm, gate_1_hbm, gate_3_hbm, out_hbm, sems):
    sources = (a_hbm, b_hbm, c_hbm, d_hbm)
    for copy in start_copies(sems, [(x, out_hbm.at[i]) for i, x in enumerate(sources)]):
        copy.wait()


def weigh(query, keys, values, bias_left, bias_right):
    scores = dot(query, jnp.concatenate(keys, axis=0), NT)
    if bias_left is not None:
        scores = jnp.concatenate([scores[:, :128] + bias_left, scores[:, 128:]], axis=1)
    if bias_right is not None:
        scores = jnp.concatenate([scores[:, :256], scores[:, 256:] + bias_right], axis=1)
    top = jnp.max(scores, axis=1, keepdims=True)
    probs = jnp.exp2((scores - top) * SCALE2).astype(BF16)
    wide = jnp.concatenate(values, axis=0)
    wide = jnp.concatenate([wide, jnp.ones_like(wide)], axis=1)
    return top, dot(probs, wide)


def merge(fine, coarse):
    fine_top, fine_sums = fine
    top, sums = double(coarse[0]), double(coarse[1])
    fall = jnp.exp2(-jnp.abs(fine_top - top) * SCALE2)
    higher = fine_top >= top
    fine_factor = jnp.where(higher, 1.0, fall)
    factor = jnp.where(higher, fall, 1.0)
    return jnp.maximum(fine_top, top), fine_sums * fine_factor + sums * factor


def attention_kernel(
    q_ref, k_ref, v_ref, side_ref, chip_ref, near_ref, far_ref, out_ref,
    own1_ref, own2_ref, halo_ref, chips_ref,
):
    core = lax.axis_index("core")
    chip = lax.axis_index(("x", "z"))
    last = lax.axis_size(("x", "z")) - 1
    left_chip = jnp.where(chip > 0, 0.0, MASKED).astype(F32)
    right_chip = jnp.where(chip < last, 0.0, MASKED).astype(F32)
    left_bias = jnp.where(core == 0, left_chip, 0.0)
    right_bias = jnp.where(core == 0, 0.0, right_chip)
    average = pair_average()
    order = row_order()
    back = row_order_back()
    side_slot, near_slot = 1 - core, core
    for which, ref in enumerate((k_ref, v_ref)):
        for n in range(4):
            own1 = dot(average, ref[128 * n : 128 * n + 128, :]).astype(BF16)
            own1_ref[which, 64 * n : 64 * n + 64, :] = own1
            own2_ref[which, 32 * n : 32 * n + 32, :] = halve(own1)
        unpack(side_ref, which, average, halo_ref, side_slot)
        unpack(near_ref, which, average, halo_ref, near_slot, chips_ref)
        chips_ref[which, near_slot, 64:128, :] = near_ref[which, 256:320, :]
        chips_ref[which, side_slot] = far_ref[which]

    def one_head(head, carry):
        lanes = pl.ds(pl.multiple_of(head * HEAD_DIM, HEAD_DIM), HEAD_DIM)
        q0 = [dot(order, q_ref[128 * n : 128 * n + 128, lanes]).astype(BF16) for n in range(4)]
        q1 = [halve(x) for x in q0]
        q2 = [halve(x) for x in q1]
        q3 = [halve(x) for x in q2]

        def piece(own, which, level, index, count):
            if index < 0:
                return halo_ref[which, 0, 128 * level : 128 * level + 128, lanes]
            if index >= count:
                return halo_ref[which, 1, 128 * level : 128 * level + 128, lanes]
            return own(which, index)

        def own_0(which, index):
            return (k_ref, v_ref)[which][128 * index : 128 * index + 128, lanes]

        def own_1(which, index):
            return own1_ref[which, 128 * index : 128 * index + 128, lanes]

        def own_2(which, index):
            return own2_ref[which, :, lanes]

        def tile(query, own, level, index, count):
            near = [index - 1, index, index + 1]
            return weigh(
                query,
                [piece(own, 0, level, i, count) for i in near],
                [piece(own, 1, level, i, count) for i in near],
                left_bias if index == 0 else None,
                right_bias if index == count - 1 else None,
            )

        at_3 = weigh(
            jnp.concatenate(q3, axis=0),
            [chips_ref[0, 0, :, lanes], chip_ref[0, :, lanes], chips_ref[0, 1, :, lanes]],
            [chips_ref[1, 0, :, lanes], chip_ref[1, :, lanes], chips_ref[1, 1, :, lanes]],
            left_chip,
            right_chip,
        )
        at_2 = merge(tile(jnp.concatenate(q2, axis=0), own_2, 2, 0, 1), at_3)
        for j in range(2):
            half_2 = tuple(x[64 * j : 64 * j + 64] for x in at_2)
            query_1 = jnp.concatenate(q1[2 * j : 2 * j + 2], axis=0)
            at_1 = merge(tile(query_1, own_1, 1, j, 2), half_2)
            for n in (2 * j, 2 * j + 1):
                start = 64 * (n - 2 * j)
                half_1 = tuple(x[start : start + 64] for x in at_1)
                _, sums = merge(tile(q0[n], own_0, 0, n, 4), half_1)
                attended = (sums[:, :128] / sums[:, 128:]).astype(BF16)
                out_ref[128 * n : 128 * n + 128, lanes] = dot(back, attended).astype(BF16)
        return carry

    lax.fori_loop(0, HEADS_HERE, one_head, 0, unroll=2)


def project_kernel(
    own_ref, one_ref, three_ref, upper_ref, lower_ref, mine_ref, other_ref, out_ref
):
    core = lax.axis_index("core")
    twist = lax.axis_index("head") ^ lax.axis_index("x")
    half = ROWS // 2

    def run(first, second):
        def weight(i):
            return jnp.concatenate(
                [ref[twist ^ i, z] for z in range(first.shape[1]) for ref in (first, second)], axis=0
            )

        weights = [weight(i) for i in range(4)]
        for start, across in ((0, upper_ref), (half, lower_ref)):
            rows = slice(start, start + half)
            total = dot(own_ref[rows, :], weights[0], NT)
            total += dot(one_ref[rows, :], weights[1], NT)
            total += dot(three_ref[rows, :], weights[3], NT)
            total += dot(across[...], weights[2], NT)
            out_ref[rows, :] = total.astype(BF16)

    pl.when(core == 0)(functools.partial(run, mine_ref, other_ref))
    pl.when(core != 0)(functools.partial(run, other_ref, mine_ref))


def call(kernel, outs, args, work_us, scratch=(), copies=(), specs=None, out_spec=pltpu.VMEM, limit=VMEM_LIMIT, aliases=None):
    shapes = [jax.ShapeDtypeStruct(s, BF16) for s in outs]
    one = len(shapes) == 1
    out_specs = [pl.BlockSpec(memory_space=out_spec)] * len(outs)
    return pl.pallas_call(
        kernel,
        out_shape=shapes[0] if one else shapes,
        in_specs=[pl.BlockSpec(memory_space=s) for s in specs or [pl.ANY] * len(args)],
        out_specs=out_specs[0] if one else out_specs,
        scratch_shapes=[pltpu.VMEM(s, BF16) for s in scratch]
        + [pltpu.SemaphoreType.DMA((n,)) for n in copies],
        input_output_aliases=aliases or {},
        cost_estimate=pl.CostEstimate(flops=int(work_us * 1.1e9), bytes_accessed=0, transcendentals=0),
        compiler_params=pltpu.CompilerParams(vmem_limit_bytes=limit),
    )(*args)


def to_all(piece, gate, axis):
    peers = lax.axis_size(axis)
    copies = call(
        copies_kernel,
        [(peers,) + piece.shape],
        (piece, gate),
        1,
        specs=(pltpu.VMEM, pl.ANY),
    )
    return lax.all_to_all(copies, axis, 0, 0, tiled=True)


def on_device(q, k, v, w):
    x_size, z_size = lax.axis_size("x"), lax.axis_size("z")
    count = lax.axis_size("head")
    devices = 2 * x_size * z_size
    seq = ("x", "z", "core")
    swap = [(i, i ^ 1) for i in range(devices)]

    near_own, side_own, own3 = call(
        coarsen_kernel,
        [(2, 256, WIDTH), (2, 256, WIDTH), (2, 64, WIDTH)],
        (k, v),
        3,
        [(2, ROWS, WIDTH)],
        (2,),
    )
    side = lax.ppermute(side_own, seq, swap)
    turn = [(a * count + b, b * count + a) for a in range(x_size) for b in range(count)]
    w_turned = lax.ppermute(w.T, ("x", "head"), turn)
    w_turned = call(hold_kernel, [w_turned.shape], (w_turned,), 3, out_spec=pl.ANY, aliases={0: 0})

    near, chip3 = call(
        prepare_kernel,
        [(2, 320, WIDTH), (2, 128, WIDTH)],
        (side, near_own, own3),
        2,
        specs=[pltpu.VMEM] * 3,
    )
    to_near = [(i, i + 1 if i % 2 else i - 1) for i in range(1, devices - 1)]
    to_far = [(i, j) for i in range(devices) for j in [i - 3 if i % 2 else i + 3] if 0 <= j < devices]
    far_in = lax.ppermute(chip3, seq, to_far)
    near_in = lax.ppermute(near, seq, to_near)

    w_z = to_all(w_turned, chip3, "z")

    attended = call(
        attention_kernel,
        [(ROWS, WIDTH)],
        (q, k, v, side, chip3, near_in, far_in),
        11,
        [(2, 256, WIDTH), (2, 128, WIDTH), (2, 2, 384, WIDTH), (2, 2, 128, WIDTH)],
        specs=[pltpu.VMEM] * 7,
    )

    one = [(i, i ^ 1) for i in range(count)]
    three = [(i, i ^ 3) for i in range(count)]
    half = ROWS // 2
    from_one = lax.ppermute(attended, "head", one)
    from_three = lax.ppermute(attended, "head", three)

    w_x = [w_z] + [
        lax.ppermute(w_z, "x", [(i, i ^ j) for i in range(x_size)]) for j in range(1, x_size)
    ]
    w_mine = call(
        stack_kernel, [(x_size,) + w_z.shape], w_x + [from_one, from_three], 1, (), (x_size,), out_spec=pl.ANY
    )
    w_other = lax.ppermute(w_mine, seq, swap)

    upper = lax.ppermute(from_one[:half], "head", three)
    lower = lax.ppermute(from_three[half:], "head", one)
    upper, lower = call(
        gate_kernel, [upper.shape] * 2, (upper, lower), 8, out_spec=pl.ANY, aliases={0: 0, 1: 1}
    )
    return call(
        project_kernel,
        [(ROWS, WIDTH)],
        (attended, from_one, from_three, upper, lower, w_mine, w_other),
        3,
        specs=[pltpu.VMEM] * 7,
    )


def solution(mesh):
    count = mesh.shape["head"]
    rows = ("x", "z", "core")
    grid = Mesh(mesh.devices.reshape(4, mesh.shape["seq"] // 8, 2, count), rows + ("head",))
    return jax.shard_map(
        on_device,
        mesh=grid,
        in_specs=(P(rows, "head"), P(rows, "head"), P(rows, "head"), P("head", rows)),
        out_specs=P(rows, "head"),
        check_vma=False,
    )
```

```python
import functools

import jax
import jax.numpy as jnp
from jax import lax
from jax.experimental import pallas as pl
from jax.experimental.pallas import tpu as pltpu
from jax.sharding import Mesh, PartitionSpec as P

HEAD_DIM = 128
BLOCK = 128
GROUP = 16
ROWS = 512
WIDTH = 512
HEADS_HERE = WIDTH // HEAD_DIM
SCALE2 = HEAD_DIM ** (-0.5) * 1.4426950408889634
MASKED = -1e30
F32 = jnp.float32
BF16 = jnp.bfloat16
VMEM_LIMIT = 16 * 1024 * 1024

NT = (((1,), (1,)), ((), ()))
NN = (((1,), (0,)), ((), ()))


def dot(a, b, dims=NN):
    return lax.dot_general(a, b, dims, preferred_element_type=F32)


def iota2(shape, dim):
    return lax.broadcasted_iota(jnp.int32, shape, dim)


def pair_average():
    row, col = iota2((64, 128), 0), iota2((64, 128), 1)
    return jnp.where((col >> 1) == 4 * (row & 15) + (row >> 4), 0.5, 0.0).astype(BF16)


def row_order():
    row, col = iota2((128, 128), 0), iota2((128, 128), 1)
    return jnp.where(col == 8 * (row & 15) + (row >> 4), 1.0, 0.0).astype(BF16)


def row_order_back():
    row, col = iota2((128, 128), 0), iota2((128, 128), 1)
    return jnp.where(row == 8 * (col & 15) + (col >> 4), 1.0, 0.0).astype(BF16)


def halve(x):
    wide = x.astype(F32)
    parts = [
        (wide[32 * i : 32 * i + 16] + wide[32 * i + 16 : 32 * i + 32]) * 0.5
        for i in range(x.shape[0] // 32)
    ]
    out = parts[0] if len(parts) == 1 else jnp.concatenate(parts, axis=0)
    return out.astype(BF16)


def double(x):
    parts = []
    for i in range(x.shape[0] // GROUP):
        piece = x[GROUP * i : GROUP * (i + 1)]
        parts += [piece, piece]
    return jnp.concatenate(parts, axis=0)


def start_copies(sems, pairs):
    copies = [
        pltpu.make_async_copy(source, target, sems.at[i]) for i, (source, target) in enumerate(pairs)
    ]
    for copy in copies:
        copy.start()
    return copies


def coarsen_kernel(
    k_hbm, v_hbm, near_ref, side_ref, own3_ref, kv_ref, sems
):
    core = lax.axis_index("core")
    copies = start_copies(sems, ((k_hbm, kv_ref.at[0]), (v_hbm, kv_ref.at[1])))
    average = pair_average()
    for which, copy in enumerate(copies):
        copy.wait()
        own1 = [dot(average, kv_ref[which, 128 * n : 128 * n + 128, :]).astype(BF16) for n in range(4)]
        own2 = [halve(x) for x in own1]
        own3 = [halve(x) for x in own2]
        for n in range(4):
            own3_ref[which, 16 * n : 16 * n + 16, :] = own3[n]

        def edges(pack_ref, to_left):
            first, second, third, fourth = (0, 1, 2, 3) if to_left else (3, 2, 1, 0)
            pack_ref[which, 0:128, :] = kv_ref[which, 128 * first : 128 * first + 128, :]
            pack_ref[which, 128:192, :] = own1[second]
            pack_ref[which, 192:224, :] = own2[third]
            pack_ref[which, 224:256, :] = own2[fourth]

        def both_edges(near_is_left):
            edges(near_ref, near_is_left)
            edges(side_ref, not near_is_left)

        pl.when(core == 0)(functools.partial(both_edges, True))
        pl.when(core != 0)(functools.partial(both_edges, False))

def unpack(pack_ref, which, average, halo_ref, slot, chips_ref=None):
    edge = pack_ref[which, 0:128, :]
    edge1 = dot(average, edge).astype(BF16)
    next1 = pack_ref[which, 128:192, :]
    rest2 = pack_ref[which, 192:256, :]
    edge2, next2 = halve(edge1), halve(next1)
    pieces = ((0, edge), (128, edge1), (192, next1), (256, edge2), (288, next2), (320, rest2))
    for row, x in pieces:
        halo_ref[which, slot, row : row + x.shape[0], :] = x
    if chips_ref is not None:
        for row, x in ((0, halve(edge2)), (16, halve(next2)), (32, halve(rest2))):
            chips_ref[which, slot, row : row + x.shape[0], :] = x


def prepare_kernel(pack_ref, near_own_ref, own3_ref, near_ref, chip_ref):
    average = pair_average()
    for which in range(2):
        near_ref[which, 0:256, :] = near_own_ref[which]
        chip_ref[which, 0:64, :] = own3_ref[which]
        edge2 = halve(dot(average, pack_ref[which, 0:128, :]).astype(BF16))
        next2 = halve(pack_ref[which, 128:192, :])
        other3 = jnp.concatenate([halve(edge2), halve(next2), halve(pack_ref[which, 192:256, :])], axis=0)
        near_ref[which, 256:320, :] = other3
        chip_ref[which, 64:128, :] = other3


def copies_kernel(piece_ref, gate_hbm, out_ref):
    piece = piece_ref[...]
    for i in range(out_ref.shape[0]):
        out_ref[i] = piece


def gate_kernel(upper_hbm, lower_hbm, upper_out_hbm, lower_out_hbm):
    pass


def hold_kernel(value_hbm, out_hbm):
    pass


def stack_kernel(a_hbm, b_hbm, c_hbm, d_hbm, gate_1_hbm, gate_3_hbm, out_hbm, sems):
    sources = (a_hbm, b_hbm, c_hbm, d_hbm)
    for copy in start_copies(sems, [(x, out_hbm.at[i]) for i, x in enumerate(sources)]):
        copy.wait()


def weigh(query, keys, values, bias_left, bias_right):
    scores = dot(query, jnp.concatenate(keys, axis=0), NT)
    if bias_left is not None:
        scores = jnp.concatenate([scores[:, :128] + bias_left, scores[:, 128:]], axis=1)
    if bias_right is not None:
        scores = jnp.concatenate([scores[:, :256], scores[:, 256:] + bias_right], axis=1)
    top = jnp.broadcast_to(jnp.max(scores, axis=1, keepdims=True), (scores.shape[0], 128))
    probs = jnp.exp2((scores - jnp.concatenate([top] * 3, axis=1)) * SCALE2).astype(BF16)
    wide = jnp.concatenate(values, axis=0)
    wide = jnp.concatenate([wide, jnp.ones_like(wide)], axis=1)
    return top, dot(probs, wide)


def merge(fine, coarse):
    fine_top, fine_sums = fine
    top, sums = double(coarse[0]), double(coarse[1])
    fall = jnp.exp2(-jnp.abs(fine_top - top) * SCALE2)
    higher = fine_top >= top
    fine_factor = jnp.where(higher, 1.0, fall)
    factor = jnp.where(higher, fall, 1.0)
    fine_factor = jnp.concatenate([fine_factor] * 2, axis=1)
    factor = jnp.concatenate([factor] * 2, axis=1)
    return jnp.maximum(fine_top, top), fine_sums * fine_factor + sums * factor


def attention_kernel(
    q_ref, k_ref, v_ref, side_ref, chip_ref, near_ref, far_ref, out_ref,
    own1_ref, own2_ref, halo_ref, chips_ref,
):
    core = lax.axis_index("core")
    chip = lax.axis_index(("x", "z"))
    last = lax.axis_size(("x", "z")) - 1
    left_chip = jnp.where(chip > 0, 0.0, MASKED).astype(F32)
    right_chip = jnp.where(chip < last, 0.0, MASKED).astype(F32)
    left_bias = jnp.where(core == 0, left_chip, 0.0)
    right_bias = jnp.where(core == 0, 0.0, right_chip)
    average = pair_average()
    order = row_order()
    back = row_order_back()
    side_slot, near_slot = 1 - core, core
    for which, ref in enumerate((k_ref, v_ref)):
        for n in range(4):
            own1 = dot(average, ref[128 * n : 128 * n + 128, :]).astype(BF16)
            own1_ref[which, 64 * n : 64 * n + 64, :] = own1
            own2_ref[which, 32 * n : 32 * n + 32, :] = halve(own1)
        unpack(side_ref, which, average, halo_ref, side_slot)
        unpack(near_ref, which, average, halo_ref, near_slot, chips_ref)
        chips_ref[which, near_slot, 64:128, :] = near_ref[which, 256:320, :]
        chips_ref[which, side_slot] = far_ref[which]

    def one_head(head, carry):
        lanes = pl.ds(pl.multiple_of(head * HEAD_DIM, HEAD_DIM), HEAD_DIM)
        q0 = [dot(order, q_ref[128 * n : 128 * n + 128, lanes]).astype(BF16) for n in range(4)]
        q1 = [halve(x) for x in q0]
        q2 = [halve(x) for x in q1]
        q3 = [halve(x) for x in q2]

        def piece(own, which, level, index, count):
            if index < 0:
                return halo_ref[which, 0, 128 * level : 128 * level + 128, lanes]
            if index >= count:
                return halo_ref[which, 1, 128 * level : 128 * level + 128, lanes]
            return own(which, index)

        def own_0(which, index):
            return (k_ref, v_ref)[which][128 * index : 128 * index + 128, lanes]

        def own_1(which, index):
            return own1_ref[which, 128 * index : 128 * index + 128, lanes]

        def own_2(which, index):
            return own2_ref[which, :, lanes]

        def tile(query, own, level, index, count):
            near = [index - 1, index, index + 1]
            return weigh(
                query,
                [piece(own, 0, level, i, count) for i in near],
                [piece(own, 1, level, i, count) for i in near],
                left_bias if index == 0 else None,
                right_bias if index == count - 1 else None,
            )

        at_3 = weigh(
            jnp.concatenate(q3, axis=0),
            [chips_ref[0, 0, :, lanes], chip_ref[0, :, lanes], chips_ref[0, 1, :, lanes]],
            [chips_ref[1, 0, :, lanes], chip_ref[1, :, lanes], chips_ref[1, 1, :, lanes]],
            left_chip,
            right_chip,
        )
        at_2 = merge(tile(jnp.concatenate(q2, axis=0), own_2, 2, 0, 1), at_3)
        for j in range(2):
            half_2 = tuple(x[64 * j : 64 * j + 64] for x in at_2)
            query_1 = jnp.concatenate(q1[2 * j : 2 * j + 2], axis=0)
            at_1 = merge(tile(query_1, own_1, 1, j, 2), half_2)
            for n in (2 * j, 2 * j + 1):
                start = 64 * (n - 2 * j)
                half_1 = tuple(x[start : start + 64] for x in at_1)
                _, sums = merge(tile(q0[n], own_0, 0, n, 4), half_1)
                attended = (sums[:, :128] / sums[:, 128:]).astype(BF16)
                out_ref[128 * n : 128 * n + 128, lanes] = dot(back, attended).astype(BF16)
        return carry

    lax.fori_loop(0, HEADS_HERE, one_head, 0, unroll=2)


def project_kernel(
    own_ref, one_ref, three_ref, upper_ref, lower_ref, mine_ref, other_ref, out_ref
):
    core = lax.axis_index("core")
    twist = lax.axis_index("head") ^ lax.axis_index("x")
    half = ROWS // 2

    def run(first, second):
        def weight(i):
            return jnp.concatenate(
                [ref[twist ^ i, z] for z in range(first.shape[1]) for ref in (first, second)], axis=0
            )

        weights = [weight(i) for i in range(4)]
        for start, across in ((0, upper_ref), (half, lower_ref)):
            rows = slice(start, start + half)
            total = dot(own_ref[rows, :], weights[0], NT)
            total += dot(one_ref[rows, :], weights[1], NT)
            total += dot(three_ref[rows, :], weights[3], NT)
            total += dot(across[...], weights[2], NT)
            out_ref[rows, :] = total.astype(BF16)

    pl.when(core == 0)(functools.partial(run, mine_ref, other_ref))
    pl.when(core != 0)(functools.partial(run, other_ref, mine_ref))


def call(kernel, outs, args, work_us, scratch=(), copies=(), specs=None, out_spec=pltpu.VMEM, limit=VMEM_LIMIT, aliases=None):
    shapes = [jax.ShapeDtypeStruct(s, BF16) for s in outs]
    one = len(shapes) == 1
    out_specs = [pl.BlockSpec(memory_space=out_spec)] * len(outs)
    return pl.pallas_call(
        kernel,
        out_shape=shapes[0] if one else shapes,
        in_specs=[pl.BlockSpec(memory_space=s) for s in specs or [pl.ANY] * len(args)],
        out_specs=out_specs[0] if one else out_specs,
        scratch_shapes=[pltpu.VMEM(s, BF16) for s in scratch]
        + [pltpu.SemaphoreType.DMA((n,)) for n in copies],
        input_output_aliases=aliases or {},
        cost_estimate=pl.CostEstimate(flops=int(work_us * 1.1e9), bytes_accessed=0, transcendentals=0),
        compiler_params=pltpu.CompilerParams(vmem_limit_bytes=limit),
    )(*args)


def to_all(piece, gate, axis):
    peers = lax.axis_size(axis)
    copies = call(
        copies_kernel,
        [(peers,) + piece.shape],
        (piece, gate),
        1,
        specs=(pltpu.VMEM, pl.ANY),
    )
    return lax.all_to_all(copies, axis, 0, 0, tiled=True)


def on_device(q, k, v, w):
    x_size, z_size = lax.axis_size("x"), lax.axis_size("z")
    count = lax.axis_size("head")
    devices = 2 * x_size * z_size
    seq = ("x", "z", "core")
    swap = [(i, i ^ 1) for i in range(devices)]

    near_own, side_own, own3 = call(
        coarsen_kernel,
        [(2, 256, WIDTH), (2, 256, WIDTH), (2, 64, WIDTH)],
        (k, v),
        3,
        [(2, ROWS, WIDTH)],
        (2,),
    )
    side = lax.ppermute(side_own, seq, swap)
    turn = [(a * count + b, b * count + a) for a in range(x_size) for b in range(count)]
    w_turned = lax.ppermute(w.T, ("x", "head"), turn)
    w_turned = call(hold_kernel, [w_turned.shape], (w_turned,), 3, out_spec=pl.ANY, aliases={0: 0})

    near, chip3 = call(
        prepare_kernel,
        [(2, 320, WIDTH), (2, 128, WIDTH)],
        (side, near_own, own3),
        2,
        specs=[pltpu.VMEM] * 3,
    )
    to_near = [(i, i + 1 if i % 2 else i - 1) for i in range(1, devices - 1)]
    to_far = [(i, j) for i in range(devices) for j in [i - 3 if i % 2 else i + 3] if 0 <= j < devices]
    far_in = lax.ppermute(chip3, seq, to_far)
    near_in = lax.ppermute(near, seq, to_near)

    w_z = to_all(w_turned, chip3, "z")

    attended = call(
        attention_kernel,
        [(ROWS, WIDTH)],
        (q, k, v, side, chip3, near_in, far_in),
        11,
        [(2, 256, WIDTH), (2, 128, WIDTH), (2, 2, 384, WIDTH), (2, 2, 128, WIDTH)],
        specs=[pltpu.VMEM] * 7,
    )

    one = [(i, i ^ 1) for i in range(count)]
    three = [(i, i ^ 3) for i in range(count)]
    half = ROWS // 2
    from_one = lax.ppermute(attended, "head", one)
    from_three = lax.ppermute(attended, "head", three)

    w_x = [w_z] + [
        lax.ppermute(w_z, "x", [(i, i ^ j) for i in range(x_size)]) for j in range(1, x_size)
    ]
    w_mine = call(
        stack_kernel, [(x_size,) + w_z.shape], w_x + [from_one, from_three], 1, (), (x_size,), out_spec=pl.ANY
    )
    w_other = lax.ppermute(w_mine, seq, swap)

    upper = lax.ppermute(from_one[:half], "head", three)
    lower = lax.ppermute(from_three[half:], "head", one)
    upper, lower = call(
        gate_kernel, [upper.shape] * 2, (upper, lower), 8, out_spec=pl.ANY, aliases={0: 0, 1: 1}
    )
    return call(
        project_kernel,
        [(ROWS, WIDTH)],
        (attended, from_one, from_three, upper, lower, w_mine, w_other),
        3,
        specs=[pltpu.VMEM] * 7,
    )


def solution(mesh):
    count = mesh.shape["head"]
    rows = ("x", "z", "core")
    grid = Mesh(mesh.devices.reshape(4, mesh.shape["seq"] // 8, 2, count), rows + ("head",))
    return jax.shard_map(
        on_device,
        mesh=grid,
        in_specs=(P(rows, "head"), P(rows, "head"), P(rows, "head"), P("head", rows)),
        out_specs=P(rows, "head"),
        check_vma=False,
    )
```
